32 devices in a mesh: seq: 4 (over z), fsdp: 8 (over y, x, core).
Axes of the slice: x: 2, y: 2, z: 4, core: 2. Of those that a mesh axis runs over, the one named last changes fastest.
Arguments:
- inputs: bfloat16 [16, 1024, 1024], P('fsdp', 'seq'), may hold values from -6 to 6
- qkv_proj: bfloat16 [3, 1024, 1024], P(None, ('seq', 'fsdp')), may hold values from -0.1875 to 0.1875
- out_proj: bfloat16 [1024, 1024], P(('seq', 'fsdp')), may hold values from -1.5 to 1.5
- ffn_in: bfloat16 [1024, 4096], P(('seq', 'fsdp')), may hold values from -0.1875 to 0.1875
- ffn_out: bfloat16 [4096, 1024], P(('seq', 'fsdp')), may hold values from -0.09375 to 0.09375
- norm_gains: bfloat16 [3, 1024], P(None, ('seq', 'fsdp')), may hold values from 0.099609375 to 1.8984375
- norm_biases: bfloat16 [3, 1024], P(None, ('seq', 'fsdp')), may hold values from -1.1953125 to 1.1953125
- centroids: bfloat16 [8, 1024], P('fsdp', 'seq'), may hold values from -0.125 to 0.125
- expert_in: bfloat16 [8, 1024, 4096], P('fsdp', None, 'seq'), may hold values from -0.1875 to 0.1875
- expert_out: bfloat16 [8, 4096, 1024], P('fsdp', 'seq'), may hold values from -0.1875 to 0.1875
- doc_lengths: int32 [16, 8], P('fsdp'), may hold values from 1 to 896, 1024 in all within a row
- routes: int32 [4, 16, 256, 1], P('seq', 'fsdp'), may hold values from 0 to 7; in each aligned block of 512 rows (0 to 511, 512 to 1023, ..., all dimensions but the last counted through in order) at most 96 rows name the same one
- out_grad: bfloat16 [16, 1024, 1024], P('fsdp', 'seq'), may hold values from -6 to 6
Outputs:
- outputs: bfloat16 [16, 1024, 1024], P('fsdp', 'seq')
- input_grad: float32 [16, 1024, 1024], P('fsdp', 'seq')
- qkv_proj_grad: float32 [3, 1024, 1024], P(None, ('seq', 'fsdp'))
- out_proj_grad: float32 [1024, 1024], P(('seq', 'fsdp'))
- ffn_in_grad: float32 [1024, 4096], P(('seq', 'fsdp'))
- ffn_out_grad: float32 [4096, 1024], P(('seq', 'fsdp'))
- gains_grad: float32 [3, 1024], P(None, ('seq', 'fsdp'))
- biases_grad: float32 [3, 1024], P(None, ('seq', 'fsdp'))
- centroids_grad: float32 [8, 1024], P('fsdp', 'seq')
- expert_in_grad: float32 [8, 1024, 4096], P('fsdp', None, 'seq')
- expert_out_grad: float32 [8, 4096, 1024], P('fsdp', 'seq')
The draws below stay inside these ranges and needn't reach their ends.
Inputs may be any that keep to these rules, and one draw needn't show every extreme that they name: `doc_lengths`: each row's lengths sum to 1024; the longest is exactly 896. `routes`: each token names one expert; among the tokens of one device no expert is named more than 96 times, a bound that some block reaches.
All inputs are finite; a program needn't handle non-finite values.
Results may differ from the reference program's by a relative error of at most 0.015.
Values may be sent and summed in bfloat16 or wider, within the bound.
A program may use at most 320 MiB of HBM per device.

```python
import math
import jax
import jax.numpy as jnp
import numpy as np
from jax import lax

D = 1024
HEADS = 16
HEAD_DIM = 64
FF = 4096
L = 1024
DOCS = 8
ROWS = 16
TOKENS = 16384
SPAN = 256
TOK_DEV = 512
EXPERTS = 8
CAP = 96
SLOTS = 3072
N_SEQ = 4


def level_of(stream_key, dims, split, least, high):
    def one(position, shards_of):
        heights = jax.random.uniform(jax.random.fold_in(jax.random.fold_in(stream_key, 6), position), (shards_of,), jnp.float32, least / len(split), high / len(split))
        return jnp.repeat(jnp.exp(heights), dims[position] // shards_of).reshape((-1,) + (1,) * (len(dims) - position - 1))

    factor_of = one(*split[0])
    for cut in split[1:]:
        factor_of = factor_of * one(*cut)
    return factor_of


def split_up(amount, total, bound, slope):
    loads = [(1 << 20) // math.isqrt(grade ** slope) + 1 for grade in range(2, amount + 1)]
    rest, holding = total - bound - (amount - 1), [1] * (amount - 1)
    while rest > 0:
        movable = [i for i in range(amount - 1) if holding[i] < bound]
        whole, budget = sum([loads[i] for i in movable]), rest
        for i in movable:
            more = min(bound - holding[i], max(1, budget * loads[i] // whole), rest)
            holding[i] = holding[i] + more
            rest = rest - more
    return np.array([bound] + holding)


def uneven_parts(own_key, number_of, total, reach, slope):
    if number_of == 2:
        one = jax.random.randint(own_key, (), max(1, total - reach), min(reach, total - 1) + 1)
        return jnp.stack([one, total - one])
    lengths = jnp.asarray(split_up(number_of, total, reach, slope), jnp.int32)
    couples = (number_of - 1) // 2
    source_of, taker = lengths[1:1 + 2 * couples:2], lengths[2:2 + 2 * couples:2]
    room = jnp.minimum(source_of - 1, reach - taker)
    moved = jax.random.randint(jax.random.fold_in(own_key, 1), (couples,), 0, 1 << 20) % (room + 1)
    lengths = lengths.at[1:1 + 2 * couples:2].set(source_of - moved).at[2:2 + 2 * couples:2].set(taker + moved)
    return lengths[jax.random.permutation(jax.random.fold_in(own_key, 2), number_of)]


def shared_out(key, own, number, rows, number_of, top, most, lean):
    ranking = jax.random.permutation(key, number_of)
    packed, common = shares(number_of, rows * top, most, lean, True), shares(number_of, rows * top, most, lean, False)
    places = jnp.arange(number_of)

    def named(tallies, offset_by):
        used = int((tallies > 0).sum())
        fixed = max(1, used // 4)
        moved = fixed + (places - fixed + offset_by * (used - fixed)) % max(1, number_of - fixed)
        return jnp.zeros((number_of,), jnp.int32).at[ranking[jnp.where(places < fixed, places, moved)]].set(jnp.asarray(tallies, jnp.int32))

    tallies = jnp.where(number % 4 == 0, named(packed, number // 4), named(common, number - number // 4 - 1))
    mixed = jax.random.permutation(jax.random.fold_in(own, 3), number_of)
    giver, sink = mixed[0:number_of // 2 * 2:2], mixed[1:number_of // 2 * 2:2]
    margin = jnp.minimum(tallies[giver] - 1, most - tallies[sink]) // 2
    margin = jnp.where((giver == ranking[0]) | (sink == ranking[0]) | (tallies[sink] == 0), 0, jnp.maximum(margin, 0))
    moved = jax.random.randint(jax.random.fold_in(own, 4), (number_of // 2,), 0, 1 << 20) % (margin + 1)
    tallies = tallies.at[giver].add(-moved).at[sink].add(moved)
    items = jnp.searchsorted(jnp.cumsum(tallies), jnp.arange(rows * top), side="right").astype(jnp.int32)
    table = items.reshape(top, rows).T
    table = table[jax.random.permutation(jax.random.fold_in(own, 1), rows)]
    offset_by = jax.random.randint(jax.random.fold_in(own, 2), (rows, 1), 0, top)
    return jnp.take_along_axis(table, (jnp.arange(top)[None, :] + offset_by) % top, axis=1)


def shares(number_of, total, limit, lean, full):
    weights = [(1 << 20) // math.isqrt(rank ** lean) + 1 for rank in range(1, number_of + 1)]
    largest = limit if full else min(limit, max(-(-total // number_of), total * weights[0] // sum(weights)))
    least = 1 if total - largest >= number_of - 1 else 0
    holding, surplus = [largest] + [least] * (number_of - 1), total - largest - least * (number_of - 1)
    while surplus > 0:
        movable = [i for i in range(1, number_of) if holding[i] < largest] or [i for i in range(1, number_of) if holding[i] < limit]
        whole, remaining = sum([weights[i] for i in movable]), surplus
        for i in movable:
            more = min(limit - holding[i], max(1, remaining * weights[i] // whole), surplus)
            holding[i] = holding[i] + more
            surplus = surplus - more
    return np.array(holding)


def scatter_about(own_key, shape, width, bound, split=(), kind=jnp.bfloat16):
    gain = level_of(own_key, shape, split, -0.22, 0.18) if split else 1.0
    drawn = jax.random.normal(own_key, shape, jnp.float32) * width * gain
    return jnp.minimum(jnp.maximum(drawn, -bound), bound).astype(kind)


def setup_inputs(seed: int = 0) -> dict:
    streams_of = jax.random.split(jax.random.key(seed), 14)
    inputs = scatter_about(streams_of[0], (ROWS, L, D), 1.0, 6.0, ((0, 8), (1, 4)))
    qkv_proj = scatter_about(streams_of[1], (3, D, D), D ** -0.5, 0.1875, ((1, 32),))
    out_proj = scatter_about(streams_of[2], (D, D), (D // 64) ** -0.5, 1.5, ((0, 32),))
    ffn_in = scatter_about(streams_of[3], (D, FF), D ** -0.5, 0.1875, ((0, 32),))
    ffn_out = scatter_about(streams_of[4], (FF, D), FF ** -0.5, 0.09375, ((0, 32),))
    norm_gains = jnp.clip(1.0 + 0.18 * jax.random.normal(streams_of[5], (3, D), jnp.float32), 0.099609375, 1.8984375).astype(jnp.bfloat16)
    norm_biases = scatter_about(streams_of[6], (3, D), 0.2, 1.1953125, ((1, 32),))
    centroids = scatter_about(streams_of[7], (EXPERTS, D), (2 * D) ** -0.5, 0.125, ((0, 8), (1, 4)))
    expert_in = scatter_about(streams_of[8], (EXPERTS, D, FF), D ** -0.5, 0.1875, ((0, 8), (2, 4)))
    expert_out = scatter_about(streams_of[9], (EXPERTS, FF, D), (FF // 4) ** -0.5, 0.1875, ((0, 8), (1, 4)))
    doc_lengths = jax.vmap(lambda own: uneven_parts(own, DOCS, L, L - L // (2 * N_SEQ), 1))(jax.random.split(streams_of[10], ROWS)).reshape((ROWS, DOCS)).astype(jnp.int32)
    routes_keys = jax.random.split(jax.random.fold_in(streams_of[11], 1), N_SEQ * ROWS * SPAN // TOK_DEV)
    routes_turns = jax.random.permutation(jax.random.fold_in(streams_of[11], 3), N_SEQ * ROWS * SPAN // TOK_DEV)
    routes = jax.vmap(lambda own, number: shared_out(jax.random.fold_in(streams_of[11], 2), own, number, TOK_DEV, EXPERTS, 1, CAP, 0))(routes_keys, routes_turns).reshape((N_SEQ, ROWS, SPAN, 1))
    out_grad = scatter_about(streams_of[12], (ROWS, L, D), 1.0, 6.0, ((0, 8), (1, 4)))
    return dict(inputs=inputs, qkv_proj=qkv_proj, out_proj=out_proj, ffn_in=ffn_in, ffn_out=ffn_out, norm_gains=norm_gains, norm_biases=norm_biases, centroids=centroids, expert_in=expert_in, expert_out=expert_out, doc_lengths=doc_lengths, routes=routes, out_grad=out_grad)


@jax.custom_vjp
def low(v):
    return lax.optimization_barrier(v.astype(jnp.bfloat16)).astype(jnp.float32)

@jax.custom_vjp
def low_back(v):
    return v

def low_keep(v):
    return (low(v), None)

def low_pass(kept, grad):
    return (grad,)

def back_keep(v):
    return (v, None)

def back_low(kept, grad):
    return (low(grad),)
low.defvjp(low_keep, low_pass)
low_back.defvjp(back_keep, back_low)
norm_eps = 1e-05
highest = lax.Precision.HIGHEST

def layer_norm(values, gain_row, shift_row):
    average = lax.optimization_barrier(jnp.mean(values, axis=-1, keepdims=True))
    centered = values - average
    variance = lax.optimization_barrier(jnp.mean(centered * centered, axis=-1, keepdims=True))
    return centered * lax.rsqrt(variance + norm_eps) * gain_row + shift_row

def matmul(left_side, right_side):
    return jnp.dot(left_side, right_side, precision=highest)

def dense_row(params, row_input, row_ids):
    qkv_proj, out_proj, ffn_in, ffn_out, norm_gains, norm_biases = params
    normed = low(layer_norm(row_input, norm_gains[0], norm_biases[0]))
    queries = low_back(low(matmul(normed, qkv_proj[0]))).reshape(L, HEADS, HEAD_DIM)
    key_rows = low_back(low(matmul(normed, qkv_proj[1]))).reshape(L, HEADS, HEAD_DIM)
    value_rows = low_back(low(matmul(normed, qkv_proj[2]))).reshape(L, HEADS, HEAD_DIM)
    scores = low_back(jnp.einsum('qhd,khd->hqk', queries, key_rows, precision=highest) * HEAD_DIM ** (-0.5))
    positions = jnp.arange(L, dtype=jnp.int32)
    allowed = (row_ids[:, None] == row_ids[None, :]) & (positions[None, :] <= positions[:, None])
    scores = jnp.where(allowed[None], scores, -1e+30)
    weights = low(jax.nn.softmax(scores, axis=-1))
    attended = jnp.einsum('hqk,khd->qhd', weights, value_rows, precision=highest).reshape(L, D)
    attended = low_back(low(attended))
    middle = row_input + low_back(matmul(attended, out_proj))
    hidden_in = low(layer_norm(middle, norm_gains[1], norm_biases[1]))
    hidden = low_back(matmul(hidden_in, ffn_in))
    activated = low(jax.nn.gelu(hidden, approximate=False))
    return middle + low_back(matmul(activated, ffn_out))

def forward(inputs, qkv_proj, out_proj, ffn_in, ffn_out, norm_gains, norm_biases, centroids, expert_in, expert_out, doc_ids, slot_table):
    params = (qkv_proj, out_proj, ffn_in, ffn_out, norm_gains, norm_biases)

    def row_step(carry_state, row_item):
        return (carry_state, dense_row(params, row_item[0], row_item[1]))
    carry_state, block_out = lax.scan(jax.checkpoint(row_step), jnp.zeros((), jnp.float32), (inputs, doc_ids))
    flat_out = block_out.reshape(TOKENS, D)
    normed = low_back(low(layer_norm(flat_out, norm_gains[2], norm_biases[2])))
    padded = jnp.concatenate([normed, jnp.zeros((1, D), jnp.float32)], axis=0)

    def expert_step(expert_item):
        slot_list, centroid, weight_in, weight_out = expert_item
        slot_rows = padded[slot_list]
        gate_value = jax.nn.sigmoid(matmul(slot_rows, centroid))
        hidden = low_back(matmul(slot_rows, weight_in))
        activated = low(jax.nn.gelu(hidden, approximate=False))
        result = low_back(matmul(activated, weight_out))
        return low_back(low(gate_value[:, None] * result))
    gated_out = lax.map(jax.checkpoint(expert_step), (slot_table, centroids, expert_in, expert_out))
    merged = jnp.zeros((TOKENS + 1, D), jnp.float32).at[slot_table.reshape(-1)].add(gated_out.reshape(-1, D))
    return (flat_out + merged[:TOKENS]).reshape(ROWS, L, D)

def reference(inputs, qkv_proj, out_proj, ffn_in, ffn_out, norm_gains, norm_biases, centroids, expert_in, expert_out, doc_lengths, routes, out_grad):
    doc_ends = jnp.cumsum(doc_lengths, axis=1)
    positions = jnp.arange(L, dtype=jnp.int32)
    doc_ids = lax.optimization_barrier(jnp.sum((positions[None, :, None] >= doc_ends[:, None, :-1]).astype(jnp.int32), axis=-1))
    expert_of = routes[..., 0].transpose(1, 0, 2).reshape(TOKENS)
    choose = (expert_of[:, None] == jnp.arange(EXPERTS, dtype=jnp.int32)[None, :]).astype(jnp.int32)
    slot_rank = lax.optimization_barrier(jnp.sum((jnp.cumsum(choose, axis=0) - 1) * choose, axis=1))
    target = expert_of * SLOTS + slot_rank
    slot_table = jnp.full((EXPERTS * SLOTS,), TOKENS, jnp.int32).at[target].set(jnp.arange(TOKENS, dtype=jnp.int32)).reshape(EXPERTS, SLOTS)
    floats = tuple((array.astype(jnp.float32) for array in (inputs, qkv_proj, out_proj, ffn_in, ffn_out, norm_gains, norm_biases, centroids, expert_in, expert_out)))

    def forward_fn(*values):
        return forward(*values, doc_ids, slot_table)
    outputs, pullback = jax.vjp(forward_fn, *floats)
    gradients = pullback(out_grad.astype(jnp.float32))
    return (outputs.astype(jnp.bfloat16), gradients[0], gradients[1], gradients[2], gradients[3], gradients[4], gradients[5], gradients[6], gradients[7], gradients[8], gradients[9])
```

```python
import functools

import jax
import jax.numpy as jnp
from jax import lax
from jax.experimental import pallas as pl
from jax.experimental.pallas import tpu as pltpu
from jax.sharding import PartitionSpec as P

HEAD_DIM = 64
LANES = 128
norm_eps = 1e-05
BF = jnp.bfloat16
F32 = jnp.float32


def layer_norm(values, gain_row, shift_row):
    average = jnp.mean(values, axis=-1, keepdims=True)
    centered = values - average
    variance = jnp.mean(centered * centered, axis=-1, keepdims=True)
    return centered * lax.rsqrt(variance + norm_eps) * gain_row + shift_row


def gelu_pair(values):
    cdf = 0.5 * (1.0 + lax.erf(values * (0.5**0.5)))
    pdf = 0.3989422804014327 * jnp.exp(-0.5 * values * values)
    return values * cdf, cdf + values * pdf


def mm(left, right):
    return jnp.dot(left, right, preferred_element_type=F32)


def mm_nt(left, right):
    return lax.dot_general(left, right, (((1,), (1,)), ((), ())), preferred_element_type=F32)


def mm_tn(left, right):
    return lax.dot_general(left, right, (((0,), (0,)), ((), ())), preferred_element_type=F32)


def norm_parts(values):
    average = jnp.mean(values, axis=-1, keepdims=True)
    centered = values - average
    variance = jnp.mean(centered * centered, axis=-1, keepdims=True)
    return average, lax.rsqrt(variance + norm_eps)


def norm_back(values, parts, gain_row, grads):
    average, scale = parts
    unit = (values - average) * scale
    unit_grad = grads * gain_row
    first = jnp.mean(unit_grad, axis=-1, keepdims=True)
    second = jnp.mean(unit_grad * unit, axis=-1, keepdims=True)
    return scale * (unit_grad - first - unit * second), jnp.sum(grads * unit, axis=0), jnp.sum(grads, axis=0)


def after(values, *earlier):
    return lax.optimization_barrier((values, *earlier))[0]


def seq_shift(values, step):
    size = lax.axis_size("seq")
    return lax.ppermute(values, "seq", [(i, (i + step) % size) for i in range(size)])


def seq_pair(values):
    size = lax.axis_size("seq")
    return lax.ppermute(values, "seq", [(i, i ^ 1) for i in range(size)])


def put(buffer, values, place):
    return lax.dynamic_update_index_in_dim(buffer, values, place, 0)


def pick(values, place):
    return lax.dynamic_index_in_dim(values, place, 0, keepdims=False)


def seq_exchange(values):
    size = lax.axis_size("seq")
    here = lax.axis_index("seq")
    result = put(jnp.zeros_like(values), pick(values, here), here)
    for step in range(1, size):
        arrived = seq_shift(pick(values, (here + step) % size), step)
        result = put(result, arrived, (here - step) % size)
    return result


def seq_sum_scatter(values):
    size = lax.axis_size("seq")
    here = lax.axis_index("seq")
    total = pick(values, here).astype(F32)
    for step in range(1, size):
        arrived = seq_shift(pick(values, (here + step) % size).astype(BF), step)
        total = total + arrived.astype(F32)
    return total


def masked_pair(block):
    lane = lax.broadcasted_iota(jnp.int32, block.shape, 1)
    zero = jnp.zeros_like(block)
    return jnp.where(lane < HEAD_DIM, block, zero), jnp.where(lane < HEAD_DIM, zero, block)


def allowed_block(id_col, id_row, start, size, end):
    key_pos = lax.broadcasted_iota(jnp.int32, (end, size), 0)
    query_pos = start + lax.broadcasted_iota(jnp.int32, (end, size), 1)
    return (id_col[:end, :] == id_row[:, start:end]) & (key_pos <= query_pos)


def attend_kernel(size, q_ref, k_ref, v_ref, id_row_ref, id_col_ref, o_ref, lse_ref, o_all):
    length = id_row_ref.shape[-1]
    queries = q_ref[...].reshape(length, LANES) * jnp.asarray(HEAD_DIM**-0.5, BF)
    keys = k_ref[...].reshape(length, LANES)
    values_t = v_ref[...].reshape(length, LANES).T
    id_row = id_row_ref[0]
    id_col = id_col_ref[0]
    for start in range(0, length, size):
        end = start + size
        mask = allowed_block(id_col, id_row, start, size, end)
        parts = []
        for head, query in enumerate(masked_pair(queries[start:end])):
            scores = jnp.where(mask, mm_nt(keys[:end], query), -1e30)
            top = jnp.max(scores, axis=0, keepdims=True)
            lse = top + jnp.log(jnp.sum(jnp.exp(scores - top), axis=0, keepdims=True))
            weights = jnp.exp(scores - lse).astype(BF)
            lse_ref[0, 0, pl.ds(head, 1), pl.ds(start, size)] = lse
            part = values_t[head * HEAD_DIM : (head + 1) * HEAD_DIM, :end]
            parts.append(mm(part, weights))
        o_all[pl.ds(start, size), :] = jnp.concatenate(parts, axis=0).T
    o_ref[...] = o_all[...].astype(BF).reshape(o_ref.shape)


def attend_back_kernel(
    size, q_ref, k_ref, v_ref, do_ref, lse_ref, id_row_ref, id_col_ref, dq_ref, dk_ref, dv_ref, dq_all, dk_all, dv_all
):
    length = id_row_ref.shape[-1]
    scale = HEAD_DIM**-0.5
    queries = q_ref[...].reshape(length, LANES) * jnp.asarray(scale, BF)
    keys = k_ref[...].reshape(length, LANES)
    keys_t = keys.T
    values = v_ref[...].reshape(length, LANES)
    grads = do_ref[...].reshape(length, LANES)
    id_row = id_row_ref[0]
    id_col = id_col_ref[0]
    dk_all[...] = jnp.zeros_like(dk_all)
    dv_all[...] = jnp.zeros_like(dv_all)
    for start in range(0, length, size):
        end = start + size
        mask = allowed_block(id_col, id_row, start, size, end)
        parts = []
        heads = zip(masked_pair(queries[start:end]), masked_pair(grads[start:end]), strict=True)
        for head, (query, grad) in enumerate(heads):
            scores = jnp.where(mask, mm_nt(keys[:end], query), -1e30)
            probs = jnp.exp(scores - lse_ref[0, 0, pl.ds(head, 1), pl.ds(start, size)])
            prob_grad = mm_nt(values[:end], grad)
            total = jnp.sum(probs * prob_grad, axis=0, keepdims=True)
            score_grad = (probs * (prob_grad - total)).astype(BF)
            dv_all[pl.ds(0, end), :] += mm(probs.astype(BF), grad)
            dk_all[pl.ds(0, end), :] += mm(score_grad, query)
            parts.append(mm(keys_t[head * HEAD_DIM : (head + 1) * HEAD_DIM, :end], score_grad))
        dq_all[pl.ds(start, size), :] = jnp.concatenate(parts, axis=0).T * scale
    dq_ref[...] = dq_all[...].astype(BF).reshape(dq_ref.shape)
    dk_ref[...] = dk_all[...].astype(BF).reshape(dk_ref.shape)
    dv_ref[...] = dv_all[...].astype(BF).reshape(dv_ref.shape)


def attention_specs(projected, length):
    blocks, rows, span, width3 = projected.shape
    columns = width3 // 3 // LANES

    def part(index):
        return pl.BlockSpec((blocks, 1, span, LANES), lambda r, c: (0, r, 0, index * columns + c))

    id_row = pl.BlockSpec((1, 1, length), lambda r, c: (r, 0, 0))
    id_col = pl.BlockSpec((1, length, 1), lambda r, c: (r, 0, 0))
    lse = pl.BlockSpec((1, 1, 2, length), lambda r, c: (r, c, 0, 0))
    return rows, columns, part, id_row, id_col, lse


def attend(projected, id_rows, id_cols):
    length = id_rows.shape[-1]
    blocks, rows, span, width3 = projected.shape
    rows, columns, part, id_row, id_col, lse = attention_specs(projected, length)
    return pl.pallas_call(
        functools.partial(attend_kernel, min(256, length)),
        grid=(rows, columns),
        in_specs=[part(0), part(1), part(2), id_row, id_col],
        out_specs=[part(0), lse],
        out_shape=[
            jax.ShapeDtypeStruct((blocks, rows, span, width3 // 3), BF),
            jax.ShapeDtypeStruct((rows, columns, 2, length), F32),
        ],
        scratch_shapes=[pltpu.VMEM((length, LANES), F32)],
        compiler_params=pltpu.CompilerParams(vmem_limit_bytes=40 * 2**20),
        cost_estimate=pl.CostEstimate(flops=3 * 10**9, bytes_accessed=8 * 2**20, transcendentals=10**7),
    )(projected, projected, projected, id_rows, id_cols)


def attend_back(projected, grads, lse_rows, id_rows, id_cols):
    length = id_rows.shape[-1]
    blocks, rows, span, width3 = projected.shape
    rows, columns, part, id_row, id_col, lse = attention_specs(projected, length)
    shape = jax.ShapeDtypeStruct((blocks, rows, span, width3 // 3), BF)
    return pl.pallas_call(
        functools.partial(attend_back_kernel, min(256, length)),
        grid=(rows, columns),
        in_specs=[part(0), part(1), part(2), part(0), lse, id_row, id_col],
        out_specs=[part(0)] * 3,
        out_shape=[shape] * 3,
        scratch_shapes=[pltpu.VMEM((length, LANES), F32)] * 3,
        compiler_params=pltpu.CompilerParams(vmem_limit_bytes=48 * 2**20),
        cost_estimate=pl.CostEstimate(flops=8 * 10**9, bytes_accessed=12 * 2**20, transcendentals=10**7),
    )(projected, projected, projected, grads, lse_rows, id_rows, id_cols)


def fsdp_flip(values, bit):
    size = lax.axis_size("fsdp")
    return lax.ppermute(values, "fsdp", [(i, i ^ bit) for i in range(size)])


def fsdp_bits(crossed):
    bits = [1 << i for i in range(1, lax.axis_size("fsdp").bit_length() - 1)]
    return (bits[::-1] if crossed else bits) + [1]


def hyper_split(parts):
    count = parts.shape[1].bit_length() - 1
    return parts.reshape(parts.shape[0], *[2] * count, *parts.shape[2:])


def hyper_scatter_step(held, bit):
    count = lax.axis_size("fsdp").bit_length() - 1
    axis = count + 1 - bit.bit_length()
    bit_here = (lax.axis_index("fsdp") // bit) % 2
    sent = lax.dynamic_slice_in_dim(held, 1 - bit_here, 1, axis)
    kept = lax.dynamic_slice_in_dim(held, bit_here, 1, axis)
    arrived = fsdp_flip(sent, bit)
    return (kept.astype(F32) + arrived.astype(F32)).astype(BF)


def hyper_scatter(held, bits):
    for bit in bits:
        held = hyper_scatter_step(held, bit)
    return held


def by_device(term):
    seq_size, fsdp_size = lax.axis_size("seq"), lax.axis_size("fsdp")
    return term.astype(BF).reshape(seq_size, fsdp_size, -1, term.shape[-1])


def gather_kernel(seq_size, bits, proj_ref, in_ref, out_ref, x_ref, proj_all, in_all, out_all, x_all, *sems):
    own_sem, proj_send, proj_recv, line_send, line_recv, cube_send, cube_recv = sems
    z = lax.axis_index("seq")
    f = lax.axis_index("fsdp")
    count = len(bits)
    high_first = sorted(bits, reverse=True)
    bit_of = {bit: (f // bit) % 2 for bit in bits}
    mesh_id = pl.DeviceIdType.MESH

    barrier = pltpu.get_barrier_semaphore()
    for step in range(1, seq_size):
        pl.semaphore_signal(barrier, inc=1, device_id={"seq": lax.rem(z + step, seq_size)}, device_id_type=mesh_id)
    for bit in bits:
        pl.semaphore_signal(barrier, inc=1, device_id={"fsdp": f + bit * (1 - 2 * bit_of[bit])}, device_id_type=mesh_id)
    pl.semaphore_wait(barrier, seq_size - 1 + count)

    def place(buffer, s, done=()):
        if buffer is x_all:
            return buffer.at[s]
        return buffer.at[(s, *(slice(None) if bit in done else bit_of[bit] for bit in high_first))]

    def order_of(index, turn):
        return bits if (index + turn) % 2 == 0 else bits[-2::-1] + bits[-1:]

    cubes = ((proj_all, 0), (in_all, 0), (out_all, 1))

    def cube(index, s, turn, step):
        buffer, crossed = cubes[index]
        order = order_of(crossed, turn if index == 0 else 0)
        view = place(buffer, s, order[:step])
        bit = order[step]
        return pltpu.make_async_remote_copy(
            src_ref=view,
            dst_ref=view,
            send_sem=cube_send.at[index, turn, step],
            recv_sem=cube_recv.at[index, turn, step],
            device_id={"fsdp": f + bit * (1 - 2 * bit_of[bit])},
            device_id_type=mesh_id,
        )

    lines = ((in_all, in_ref), (out_all, out_ref), (x_all, x_ref))

    def line(index, side, hop):
        buffer, own = lines[index]
        ahead = 1 - 2 * side
        s = z - ahead * (hop - 1)
        view = place(buffer, s)
        return pltpu.make_async_remote_copy(
            src_ref=own if hop == 1 else view,
            dst_ref=view,
            send_sem=line_send.at[index, side, hop - 1],
            recv_sem=line_recv.at[index, side, hop - 1],
            device_id={"seq": z + ahead},
            device_id_type=mesh_id,
        )

    def line_wait(index, side, hop):
        view = place(lines[index][0], z - (1 - 2 * side) * hop)
        pltpu.make_async_remote_copy(
            src_ref=view,
            dst_ref=view,
            send_sem=line_send.at[index, side, hop - 1],
            recv_sem=line_recv.at[index, side, hop - 1],
            device_id={"seq": z - (1 - 2 * side)},
            device_id_type=mesh_id,
        ).wait_recv()

    def has_next(side):
        return z < seq_size - 1 if side == 0 else z > 0

    def has_block(side, hop):
        return z - hop >= 0 if side == 0 else z + hop < seq_size

    def proj(step):
        to = lax.rem(z + step, seq_size)
        return pltpu.make_async_remote_copy(
            src_ref=proj_ref.at[to],
            dst_ref=place(proj_all, z),
            send_sem=proj_send.at[step - 1],
            recv_sem=proj_recv.at[step - 1],
            device_id={"seq": to},
            device_id_type=mesh_id,
        )

    def proj_wait(step):
        view = place(proj_all, lax.rem(z + seq_size - step, seq_size))
        pltpu.make_async_remote_copy(
            src_ref=view,
            dst_ref=view,
            send_sem=proj_send.at[step - 1],
            recv_sem=proj_recv.at[step - 1],
            device_id={"seq": lax.rem(z + step, seq_size)},
            device_id_type=mesh_id,
        ).wait_recv()

    def turn_of(side, hop):
        return 0 if hop == 0 else 2 * hop - 1 + side

    def each_block(hop, act):
        act(0, lax.rem(z + seq_size - hop, seq_size), turn_of(0, hop))
        for index in (1, 2):
            if hop == 0:
                act(index, z, 0)
                continue
            for side in (0, 1):

                @pl.when(has_block(side, hop))
                def _(index=index, side=side):
                    act(index, z - (1 - 2 * side) * hop, turn_of(side, hop))

    owns = [
        pltpu.make_async_copy(own, place(buffer, z), own_sem.at[i])
        for i, (own, buffer) in enumerate(((proj_ref.at[z], proj_all), (in_ref, in_all), (out_ref, out_all), (x_ref, x_all)))
    ]
    for copy in owns:
        copy.start()
    for step in range(1, seq_size):
        proj(step).start()
    for index in range(3):
        for side in (0, 1):

            @pl.when(has_next(side))
            def _(index=index, side=side):
                line(index, side, 1).start()

    for copy in owns:
        copy.wait()
    each_block(0, lambda index, s, turn: cube(index, s, turn, 0).start())

    def advance(hop):
        for step in range(1, count):

            def act(index, s, turn, step=step):
                cube(index, s, turn, step - 1).wait()
                cube(index, s, turn, step).start()

            each_block(hop, act)

    for hop in range(1, seq_size):
        advance(hop - 1)
        proj_wait(hop)
        cube(0, lax.rem(z + seq_size - hop, seq_size), turn_of(0, hop), 0).start()
        for index in range(3):
            for side in (0, 1):

                @pl.when(has_block(side, hop))
                def _(index=index, side=side, hop=hop):
                    line_wait(index, side, hop)
                    if hop < seq_size - 1:

                        @pl.when(has_next(side))
                        def _():
                            line(index, side, hop + 1).start()

                    if index < 2:
                        cube(index + 1, z - (1 - 2 * side) * hop, turn_of(side, hop), 0).start()

    advance(seq_size - 1)
    for hop in range(seq_size):
        each_block(hop, lambda index, s, turn: cube(index, s, turn, count - 1).wait())
    for step in range(1, seq_size):
        proj(step).wait_send()
    for index in range(3):
        for side in (0, 1):
            for hop in range(1, seq_size):

                @pl.when(has_next(side) & has_block(side, hop - 1))
                def _(index=index, side=side, hop=hop):
                    line(index, side, hop).wait_send()


def start_gathers(proj, ffn_in, ffn_out, tokens_in):
    seq_size, fsdp_size = lax.axis_size("seq"), lax.axis_size("fsdp")
    bits = fsdp_bits(False)
    count = len(bits)

    def whole(shard):
        return jax.ShapeDtypeStruct((seq_size, *[2] * count, *shard), BF)

    turns = 2 * seq_size - 1
    dma = pltpu.SemaphoreType.DMA
    anywhere = pl.BlockSpec(memory_space=pl.ANY)
    outs = pl.pallas_call(
        functools.partial(gather_kernel, seq_size, bits),
        in_specs=[anywhere] * 4,
        out_specs=[anywhere] * 4,
        out_shape=[
            whole(proj.shape[1:]),
            whole(ffn_in.shape),
            whole(ffn_out.shape),
            jax.ShapeDtypeStruct((seq_size, *tokens_in.shape), BF),
        ],
        scratch_shapes=[
            dma((4,)),
            dma((seq_size - 1,)),
            dma((seq_size - 1,)),
            dma((3, 2, seq_size - 1)),
            dma((3, 2, seq_size - 1)),
            dma((3, turns, count)),
            dma((3, turns, count)),
        ],
        compiler_params=pltpu.CompilerParams(collective_id=0, has_side_effects=True),
        cost_estimate=pl.CostEstimate(flops=0, bytes_accessed=100 * 2**20, transcendentals=0),
    )(proj, ffn_in, ffn_out, tokens_in)
    proj_all, in_all, out_all, inputs_all = outs
    flat = (seq_size, fsdp_size)
    return (
        proj_all.reshape(*flat, *proj.shape[1:]),
        in_all.reshape(*flat, *ffn_in.shape),
        out_all.reshape(*flat, *ffn_out.shape),
        inputs_all,
    )


def whole_tiles(shard, rows=16):
    return shard if shard.shape[0] % rows == 0 else shard.reshape(rows, -1)


def on_device(
    inputs,
    qkv_proj,
    out_proj,
    ffn_in,
    ffn_out,
    norm_gains,
    norm_biases,
    centroids,
    expert_in,
    expert_out,
    doc_lengths,
    routes,
    out_grad,
):
    rows, span, width = inputs.shape
    tokens = rows * span
    seq_size, fsdp_size = lax.axis_size("seq"), lax.axis_size("fsdp")
    here = lax.axis_index("seq")
    length = span * seq_size
    cols = width // seq_size
    capacity = max(2, 3 * tokens // (2 * fsdp_size))
    groups = seq_size // 2

    docs = doc_lengths.shape[1]
    key_pos = jnp.arange(length, dtype=jnp.int32)
    doc_ids = jnp.zeros((rows, length), jnp.int32)
    doc_end = jnp.zeros((rows, 1), jnp.int32)
    for j in range(docs - 1):
        doc_end = doc_end + doc_lengths[:, j : j + 1]
        doc_ids = doc_ids + (key_pos[None, :] >= doc_end).astype(jnp.int32)
    id_rows, id_cols = doc_ids[:, None, :], doc_ids[:, :, None]

    depth = out_proj.shape[0]
    wide = 3 * cols + width
    slices = qkv_proj.reshape(3, depth, seq_size, cols).transpose(2, 1, 0, 3).reshape(seq_size, depth, 3 * cols)
    slices = jnp.concatenate([slices, jnp.broadcast_to(out_proj[None], (seq_size, depth, width))], axis=2)
    small = jnp.concatenate([norm_gains.reshape(-1), norm_biases.reshape(-1), centroids[0]])
    spare = 32 - depth % 16 if depth % 16 else 16
    extra = jnp.pad(small, (0, spare * wide - small.shape[0])).reshape(1, spare, wide)
    extra = jnp.broadcast_to(extra, (seq_size, spare, wide))
    bits = fsdp_bits(False)
    crossed = fsdp_bits(True)
    tokens_in = inputs.reshape(tokens, width)
    proj_all, ffin_all, ffout_all, inputs_all = start_gathers(
        jnp.concatenate([slices, extra], axis=1), whole_tiles(ffn_in), whole_tiles(ffn_out), tokens_in
    )
    inputs_all = inputs_all.reshape(seq_size * tokens, width)
    ffin_all, ffout_all = ffin_all.reshape(width, -1), ffout_all.reshape(-1, width)
    qkv_mine = proj_all[:, :, :depth, : 3 * cols].reshape(width, 3 * cols)
    out_all = proj_all[:, :, :depth, 3 * cols :].reshape(width, width)
    small = proj_all[:, :, depth, :]
    rows_of = small[:, :, : 6 * depth].astype(F32).reshape(-1, 6, depth).transpose(1, 0, 2).reshape(6, width)
    gain_rows, bias_rows = rows_of[:3], rows_of[3:]
    mine = small[:, :, 6 * depth : 6 * depth + cols]
    centroid = lax.dynamic_index_in_dim(mine, lax.axis_index("fsdp"), 1, keepdims=False).reshape(width)
    win_mine, wout_mine, dr_mine = after((expert_in[0], expert_out[0], out_grad.reshape(tokens, width)), inputs_all)
    parts_all = norm_parts(inputs_all.astype(F32))
    normed_flat = ((inputs_all.astype(F32) - parts_all[0]) * parts_all[1] * gain_rows[0] + bias_rows[0]).astype(BF)
    projected = mm(normed_flat, qkv_mine).astype(BF).reshape(seq_size, rows, span, 3 * cols)

    attended_mine, lse_rows = attend(projected, id_rows, id_cols)
    attended = seq_exchange(attended_mine).transpose(1, 2, 0, 3).reshape(tokens, width)

    route = routes.reshape(tokens)
    later = (jnp.arange(tokens)[:, None] > jnp.arange(tokens)[None, :]).astype(BF)
    choose = route[:, None] == jnp.arange(fsdp_size, dtype=jnp.int32)[None, :]
    before = mm(later, choose.astype(BF))
    slot_rank = jnp.sum(jnp.where(choose, before, 0.0), axis=1).astype(jnp.int32)
    target = route * capacity + slot_rank
    grad_tokens = out_grad.reshape(tokens, width)
    placings = []
    for group in range(groups):
        slot_of = target if group == 0 else seq_shift(target, 2 * group)
        placing = (slot_of[:, None] == jnp.arange(fsdp_size * capacity, dtype=jnp.int32)[None, :]).astype(BF)
        placings.append(placing)

    def slots_of(placing, values):
        return mm_tn(placing, values).astype(BF).reshape(fsdp_size, capacity, width)

    def swap_slots(values):
        return lax.all_to_all(values, "fsdp", split_axis=0, concat_axis=0, tiled=True)

    def tokens_of(placing, values):
        return mm(placing, values.reshape(fsdp_size * capacity, width))

    grad_arrived = []
    for group in range(groups):
        values = grad_tokens if group == 0 else seq_shift(dr_mine, 2 * group)
        grad_arrived.append(swap_slots(slots_of(placings[group], values)).reshape(-1, width))

    win = jnp.concatenate([win_mine, seq_pair(win_mine)], axis=1)
    wout = jnp.concatenate([wout_mine, seq_pair(wout_mine)], axis=0)

    resid_in = tokens_in.astype(F32)
    middle = resid_in + mm(attended, out_all)
    parts_two = norm_parts(middle)
    hidden_low = ((middle - parts_two[0]) * parts_two[1] * gain_rows[1] + bias_rows[1]).astype(BF)
    active, active_slope = gelu_pair(mm(hidden_low, ffin_all))
    active_low, active_slope = lax.optimization_barrier((active.astype(BF), active_slope.astype(BF)))
    block_out = middle + mm(active_low, ffout_all)
    parts_three = norm_parts(block_out)
    routed = ((block_out - parts_three[0]) * parts_three[1] * gain_rows[2] + bias_rows[2]).astype(BF)

    arrived_all, dz_all, du_all, act_all, back_terms, gated_all = [], [], [], [], [], []
    centroid_term = jnp.zeros((width,), F32)
    for group in range(groups):
        values = routed if group == 0 else seq_shift(routed, 2 * group)
        arrived = swap_slots(slots_of(placings[group], values)).reshape(-1, width)
        gated = grad_arrived[group].astype(F32)
        gate = jax.nn.sigmoid(mm(arrived, centroid))
        dz = (gate[:, None] * gated).astype(BF)
        act, slope = gelu_pair(mm(arrived, win))
        act, slope = lax.optimization_barrier((act.astype(BF), slope.astype(BF)))
        result = mm(act, wout)
        dl = jnp.sum(gated * result, axis=-1) * gate * (1.0 - gate)
        du = (slope.astype(F32) * mm_nt(dz, wout)).astype(BF)
        rows_grad = mm_nt(du, win) + dl[:, None] * centroid.astype(F32)
        centroid_term = centroid_term + jnp.sum(dl[:, None] * arrived.astype(F32), axis=0)
        back = tokens_of(placings[group], swap_slots(rows_grad.astype(BF).reshape(fsdp_size, capacity, width)))
        if group:
            back = seq_shift(back.astype(BF), -2 * group).astype(F32)
        back_terms.append(back)
        gated_all.append((gate[:, None] * result).astype(BF).reshape(fsdp_size, capacity, width))
        arrived_all.append(arrived)
        dz_all.append(dz)
        du_all.append(du)
        act_all.append(act)

    half = expert_in.shape[2]
    arrived, dz, du, act = (jnp.concatenate(v, axis=0) for v in (arrived_all, dz_all, du_all, act_all))
    in_sent = mm_tn(arrived, du[:, half:]).astype(BF)
    out_sent = mm_tn(act[:, half:], dz).astype(BF)
    in_kept = mm_tn(arrived, du[:, :half])
    out_kept = mm_tn(act[:, :half], dz)
    in_pair, out_pair = seq_pair(in_sent), seq_pair(out_sent)
    back_sum, in_sent, out_sent, in_kept, out_kept = lax.optimization_barrier(
        (sum(back_terms), in_sent, out_sent, in_kept, out_kept)
    )

    block_norm_grad, gain_three, bias_three = norm_back(block_out, parts_three, gain_rows[2], back_sum)
    block_grad = grad_tokens.astype(F32) + block_norm_grad
    block_low = block_grad.astype(BF)
    hidden_grad = (active_slope.astype(F32) * mm_nt(block_low, ffout_all)).astype(BF)
    normed_two_grad = mm_nt(hidden_grad, ffin_all)
    middle_norm_grad, gain_two, bias_two = norm_back(middle, parts_two, gain_rows[1], normed_two_grad)
    middle_grad = block_grad + middle_norm_grad
    branch = middle_grad.astype(BF)
    attended_grad = mm_nt(branch, out_all).astype(BF)
    attended_grad = attended_grad.reshape(rows, span, seq_size, cols).transpose(2, 0, 1, 3)
    attended_grad = seq_exchange(attended_grad)

    gated_back = swap_slots(jnp.concatenate(gated_all, axis=1)).reshape(fsdp_size, groups, capacity, width)
    outputs = block_out
    for group in range(groups):
        out = tokens_of(placings[group], gated_back[:, group])
        if group:
            out = seq_shift(out.astype(BF), -2 * group).astype(F32)
        outputs = outputs + out
    outputs = outputs.astype(BF).reshape(rows, span, width)

    ffout_terms = hyper_split(by_device(mm_tn(active_low, block_low)))
    ffin_terms = hyper_split(by_device(mm_tn(hidden_low, hidden_grad)))
    out_terms = mm_tn(attended, branch)
    ffout_terms = hyper_scatter_step(ffout_terms, crossed[-1])
    ffin_terms = hyper_scatter_step(ffin_terms, bits[-1])
    attended_grad, ffout_terms, ffin_terms = lax.optimization_barrier((attended_grad, ffout_terms, ffin_terms))
    ffout_terms = hyper_scatter(ffout_terms, crossed[-2:0:-1])
    ffin_terms = hyper_scatter(ffin_terms, bits[-2:0:-1])

    dq, dk, dv = attend_back(projected, attended_grad, lse_rows, id_rows, id_cols)
    projected_grad = jnp.concatenate([dq, dk, dv], axis=-1).reshape(seq_size * tokens, 3 * cols)
    projected_grad, ffout_terms, ffin_terms = lax.optimization_barrier((projected_grad, ffout_terms, ffin_terms))
    normed_low_terms = mm_nt(projected_grad, qkv_mine).astype(BF)
    normed_one_grad = seq_sum_scatter(normed_low_terms.reshape(seq_size, tokens, width))
    unit_all = (inputs_all.astype(F32) - parts_all[0]) * parts_all[1]
    terms_wide = normed_low_terms.astype(F32)
    gain_one, bias_one = jnp.sum(terms_wide * unit_all, axis=0), jnp.sum(terms_wide, axis=0)
    small_terms = jnp.stack([gain_one, gain_two, gain_three, bias_one, bias_two, bias_three])

    ffout_terms = hyper_scatter_step(ffout_terms, crossed[0])
    ffin_terms = hyper_scatter_step(ffin_terms, bits[0])
    ffn_out_grad = seq_sum_scatter(ffout_terms.reshape(seq_size, *ffn_out.shape))
    ffn_in_grad = seq_sum_scatter(ffin_terms.reshape(seq_size, *ffn_in.shape))

    proj_terms = jnp.concatenate([mm_tn(normed_flat, projected_grad).astype(BF), out_terms.astype(BF)], axis=1)
    proj_terms = proj_terms.reshape(seq_size, fsdp_size, depth, wide)
    small_rows = small_terms.astype(BF).reshape(6, seq_size, fsdp_size, depth).transpose(1, 2, 0, 3)
    small_rows = small_rows.reshape(seq_size, fsdp_size, 1, 6 * depth)
    small_rows = jnp.pad(small_rows, ((0, 0), (0, 0), (0, 7), (0, wide - 6 * depth)))
    proj_terms = hyper_split(jnp.concatenate([proj_terms, small_rows], axis=2))
    proj_terms = hyper_scatter(proj_terms, bits[::-1]).reshape(seq_size, depth + 8, wide)
    centroid_rows = centroid_term.astype(BF).reshape(seq_size, 1, cols)
    proj_terms = lax.dynamic_update_slice(proj_terms, centroid_rows, (0, depth + 1, 0))
    proj_sums = seq_exchange(proj_terms).astype(F32)
    qkv_grad = proj_sums[:, :depth, : 3 * cols].reshape(seq_size, depth, 3, cols)
    qkv_grad = qkv_grad.transpose(2, 1, 0, 3).reshape(qkv_proj.shape)
    out_proj_grad = jnp.sum(proj_sums[:, :depth, 3 * cols :], axis=0)
    small_grad = jnp.sum(proj_sums[:, depth, : 6 * depth], axis=0).reshape(6, depth)
    centroids_grad = jnp.sum(proj_sums[:, depth + 1, :cols], axis=0)[None]

    in_pair, out_pair = lax.optimization_barrier((in_pair, out_pair, normed_low_terms))[:2]
    expert_in_grad = (in_kept + in_pair.astype(F32))[None]
    expert_out_grad = (out_kept + out_pair.astype(F32))[None]

    input_norm_grad, _, _ = norm_back(resid_in, norm_parts(resid_in), gain_rows[0], normed_one_grad)
    input_grad = (middle_grad + input_norm_grad).reshape(rows, span, width)
    return (
        outputs,
        input_grad,
        qkv_grad,
        out_proj_grad,
        ffn_in_grad,
        ffn_out_grad,
        small_grad[:3],
        small_grad[3:],
        centroids_grad,
        expert_in_grad,
        expert_out_grad,
    )


def solution(mesh):
    dense = P(("seq", "fsdp"), None)
    placed = (
        P("fsdp", "seq", None),
        P(None, ("seq", "fsdp"), None),
        dense,
        dense,
        dense,
        P(None, ("seq", "fsdp")),
        P(None, ("seq", "fsdp")),
        P("fsdp", "seq"),
        P("fsdp", None, "seq"),
        P("fsdp", "seq", None),
        P("fsdp", None),
        P("seq", "fsdp", None, None),
        P("fsdp", "seq", None),
    )
    returned = (
        P("fsdp", "seq", None),
        P("fsdp", "seq", None),
        P(None, ("seq", "fsdp"), None),
        dense,
        dense,
        dense,
        P(None, ("seq", "fsdp")),
        P(None, ("seq", "fsdp")),
        P("fsdp", "seq"),
        P("fsdp", None, "seq"),
        P("fsdp", "seq", None),
    )
    return jax.shard_map(on_device, mesh=mesh, in_specs=placed, out_specs=returned, check_vma=False)
```

```python
import functools

import jax
import jax.numpy as jnp
from jax import lax
from jax.experimental import pallas as pl
from jax.experimental.pallas import tpu as pltpu
from jax.sharding import PartitionSpec as P

HEAD_DIM = 64
LANES = 128
norm_eps = 1e-05
BF = jnp.bfloat16
F32 = jnp.float32


def layer_norm(values, gain_row, shift_row):
    average = jnp.mean(values, axis=-1, keepdims=True)
    centered = values - average
    variance = jnp.mean(centered * centered, axis=-1, keepdims=True)
    return centered * lax.rsqrt(variance + norm_eps) * gain_row + shift_row


def gelu_pair(values):
    cdf = 0.5 * (1.0 + lax.erf(values * (0.5**0.5)))
    pdf = 0.3989422804014327 * jnp.exp(-0.5 * values * values)
    return values * cdf, cdf + values * pdf


def mm(left, right):
    return jnp.dot(left, right, preferred_element_type=F32)


def mm_nt(left, right):
    return lax.dot_general(left, right, (((1,), (1,)), ((), ())), preferred_element_type=F32)


def mm_tn(left, right):
    return lax.dot_general(left, right, (((0,), (0,)), ((), ())), preferred_element_type=F32)


def norm_parts(values):
    average = jnp.mean(values, axis=-1, keepdims=True)
    centered = values - average
    variance = jnp.mean(centered * centered, axis=-1, keepdims=True)
    return average, lax.rsqrt(variance + norm_eps)


def norm_back(values, parts, gain_row, grads):
    average, scale = parts
    unit = (values - average) * scale
    unit_grad = grads * gain_row
    first = jnp.mean(unit_grad, axis=-1, keepdims=True)
    second = jnp.mean(unit_grad * unit, axis=-1, keepdims=True)
    return scale * (unit_grad - first - unit * second), jnp.sum(grads * unit, axis=0), jnp.sum(grads, axis=0)


def after(values, *earlier):
    return lax.optimization_barrier((values, *earlier))[0]


def seq_shift(values, step):
    size = lax.axis_size("seq")
    return lax.ppermute(values, "seq", [(i, (i + step) % size) for i in range(size)])


def seq_pair(values):
    size = lax.axis_size("seq")
    return lax.ppermute(values, "seq", [(i, i ^ 1) for i in range(size)])


def put(buffer, values, place):
    return lax.dynamic_update_index_in_dim(buffer, values, place, 0)


def pick(values, place):
    return lax.dynamic_index_in_dim(values, place, 0, keepdims=False)


def seq_exchange(values):
    size = lax.axis_size("seq")
    here = lax.axis_index("seq")
    result = put(jnp.zeros_like(values), pick(values, here), here)
    for step in range(1, size):
        arrived = seq_shift(pick(values, (here + step) % size), step)
        result = put(result, arrived, (here - step) % size)
    return result


def seq_sum_scatter(values):
    size = lax.axis_size("seq")
    here = lax.axis_index("seq")
    total = pick(values, here).astype(F32)
    for step in range(1, size):
        arrived = seq_shift(pick(values, (here + step) % size).astype(BF), step)
        total = total + arrived.astype(F32)
    return total


def masked_pair(block):
    lane = lax.broadcasted_iota(jnp.int32, block.shape, 1)
    zero = jnp.zeros_like(block)
    return jnp.where(lane < HEAD_DIM, block, zero), jnp.where(lane < HEAD_DIM, zero, block)


def allowed_block(id_col, id_row, start, size, end):
    key_pos = lax.broadcasted_iota(jnp.int32, (end, size), 0)
    query_pos = start + lax.broadcasted_iota(jnp.int32, (end, size), 1)
    return (id_col[:end, :] == id_row[:, start:end]) & (key_pos <= query_pos)


def attend_kernel(size, q_ref, k_ref, v_ref, id_row_ref, id_col_ref, o_ref, lse_ref, o_all):
    length = id_row_ref.shape[-1]
    queries = q_ref[...].reshape(length, LANES) * jnp.asarray(HEAD_DIM**-0.5, BF)
    keys = k_ref[...].reshape(length, LANES)
    values_t = v_ref[...].reshape(length, LANES).T
    id_row = id_row_ref[0]
    id_col = id_col_ref[0]
    for start in range(0, length, size):
        end = start + size
        mask = allowed_block(id_col, id_row, start, size, end)
        parts = []
        for head, query in enumerate(masked_pair(queries[start:end])):
            scores = jnp.where(mask, mm_nt(keys[:end], query), -1e30)
            top = jnp.max(scores, axis=0, keepdims=True)
            lse = top + jnp.log(jnp.sum(jnp.exp(scores - top), axis=0, keepdims=True))
            weights = jnp.exp(scores - lse).astype(BF)
            lse_ref[0, 0, pl.ds(head, 1), pl.ds(start, size)] = lse
            part = values_t[head * HEAD_DIM : (head + 1) * HEAD_DIM, :end]
            parts.append(mm(part, weights))
        o_all[pl.ds(start, size), :] = jnp.concatenate(parts, axis=0).T
    o_ref[...] = o_all[...].astype(BF).reshape(o_ref.shape)


def attend_back_kernel(
    size, q_ref, k_ref, v_ref, do_ref, lse_ref, id_row_ref, id_col_ref, dq_ref, dk_ref, dv_ref, dq_all, dk_all, dv_all
):
    length = id_row_ref.shape[-1]
    scale = HEAD_DIM**-0.5
    queries = q_ref[...].reshape(length, LANES) * jnp.asarray(scale, BF)
    keys = k_ref[...].reshape(length, LANES)
    keys_t = keys.T
    values = v_ref[...].reshape(length, LANES)
    grads = do_ref[...].reshape(length, LANES)
    id_row = id_row_ref[0]
    id_col = id_col_ref[0]
    dk_all[...] = jnp.zeros_like(dk_all)
    dv_all[...] = jnp.zeros_like(dv_all)
    for start in range(0, length, size):
        end = start + size
        mask = allowed_block(id_col, id_row, start, size, end)
        parts = []
        heads = zip(masked_pair(queries[start:end]), masked_pair(grads[start:end]), strict=True)
        for head, (query, grad) in enumerate(heads):
            scores = jnp.where(mask, mm_nt(keys[:end], query), -1e30)
            probs = jnp.exp(scores - lse_ref[0, 0, pl.ds(head, 1), pl.ds(start, size)])
            prob_grad = mm_nt(values[:end], grad)
            total = jnp.sum(probs * prob_grad, axis=0, keepdims=True)
            score_grad = (probs * (prob_grad - total)).astype(BF)
            dv_all[pl.ds(0, end), :] += mm(probs.astype(BF), grad)
            dk_all[pl.ds(0, end), :] += mm(score_grad, query)
            parts.append(mm(keys_t[head * HEAD_DIM : (head + 1) * HEAD_DIM, :end], score_grad))
        dq_all[pl.ds(start, size), :] = jnp.concatenate(parts, axis=0).T * scale
    dq_ref[...] = dq_all[...].astype(BF).reshape(dq_ref.shape)
    dk_ref[...] = dk_all[...].astype(BF).reshape(dk_ref.shape)
    dv_ref[...] = dv_all[...].astype(BF).reshape(dv_ref.shape)


def attention_specs(projected, length):
    blocks, rows, span, width3 = projected.shape
    columns = width3 // 3 // LANES

    def part(index):
        return pl.BlockSpec((blocks, 1, span, LANES), lambda r, c: (0, r, 0, index * columns + c))

    id_row = pl.BlockSpec((1, 1, length), lambda r, c: (r, 0, 0))
    id_col = pl.BlockSpec((1, length, 1), lambda r, c: (r, 0, 0))
    lse = pl.BlockSpec((1, 1, 2, length), lambda r, c: (r, c, 0, 0))
    return rows, columns, part, id_row, id_col, lse


def attend(projected, id_rows, id_cols):
    length = id_rows.shape[-1]
    blocks, rows, span, width3 = projected.shape
    rows, columns, part, id_row, id_col, lse = attention_specs(projected, length)
    return pl.pallas_call(
        functools.partial(attend_kernel, min(256, length)),
        grid=(rows, columns),
        in_specs=[part(0), part(1), part(2), id_row, id_col],
        out_specs=[part(0), lse],
        out_shape=[
            jax.ShapeDtypeStruct((blocks, rows, span, width3 // 3), BF),
            jax.ShapeDtypeStruct((rows, columns, 2, length), F32),
        ],
        scratch_shapes=[pltpu.VMEM((length, LANES), F32)],
        compiler_params=pltpu.CompilerParams(vmem_limit_bytes=40 * 2**20),
        cost_estimate=pl.CostEstimate(flops=10**6, bytes_accessed=2**16, transcendentals=0),
    )(projected, projected, projected, id_rows, id_cols)


def attend_back(projected, grads, lse_rows, id_rows, id_cols):
    length = id_rows.shape[-1]
    blocks, rows, span, width3 = projected.shape
    rows, columns, part, id_row, id_col, lse = attention_specs(projected, length)
    shape = jax.ShapeDtypeStruct((blocks, rows, span, width3 // 3), BF)
    return pl.pallas_call(
        functools.partial(attend_back_kernel, min(256, length)),
        grid=(rows, columns),
        in_specs=[part(0), part(1), part(2), part(0), lse, id_row, id_col],
        out_specs=[part(0)] * 3,
        out_shape=[shape] * 3,
        scratch_shapes=[pltpu.VMEM((length, LANES), F32)] * 3,
        compiler_params=pltpu.CompilerParams(vmem_limit_bytes=48 * 2**20),
        cost_estimate=pl.CostEstimate(flops=10**6, bytes_accessed=2**16, transcendentals=0),
    )(projected, projected, projected, grads, lse_rows, id_rows, id_cols)


def fsdp_flip(values, bit):
    size = lax.axis_size("fsdp")
    return lax.ppermute(values, "fsdp", [(i, i ^ bit) for i in range(size)])


def fsdp_bits(crossed):
    bits = [1 << i for i in range(1, lax.axis_size("fsdp").bit_length() - 1)]
    return (bits[::-1] if crossed else bits) + [1]


def hyper_split(parts):
    count = parts.shape[1].bit_length() - 1
    return parts.reshape(parts.shape[0], *[2] * count, *parts.shape[2:])


def hyper_scatter_step(held, bit):
    count = lax.axis_size("fsdp").bit_length() - 1
    axis = count + 1 - bit.bit_length()
    bit_here = (lax.axis_index("fsdp") // bit) % 2
    sent = lax.dynamic_slice_in_dim(held, 1 - bit_here, 1, axis)
    kept = lax.dynamic_slice_in_dim(held, bit_here, 1, axis)
    arrived = fsdp_flip(sent, bit)
    return (kept.astype(F32) + arrived.astype(F32)).astype(BF)


def hyper_scatter(held, bits):
    for bit in bits:
        held = hyper_scatter_step(held, bit)
    return held


def by_device(term):
    seq_size, fsdp_size = lax.axis_size("seq"), lax.axis_size("fsdp")
    depth = term.shape[0] // (seq_size * fsdp_size)
    tile = (depth, term.shape[1]) if depth % 16 == 0 else (16, depth * term.shape[1] // 16)
    return term.astype(BF).reshape(seq_size, fsdp_size, *tile)


def gather_plan(seq_size, count):
    plan = [("send", 0), ("send", 1), ("own",)]
    for hop in range(1, seq_size):
        plan += [("proj", hop), ("arrive", 0, hop), ("arrive", 1, hop)]
        if hop == 1:
            plan += [("send", 2)]
        if hop < seq_size - 1:
            plan += [("go", hop - 1, 0)]
    last = seq_size - 1
    rest = [("go", 0, 1), ("go", last - 1, 0), ("go", 1, 1), ("go", last, 0)]
    rest += [("go", hop, step) for step in range(1, count - 1) for hop in range(2 if step == 1 else 0, seq_size)]
    plan += [("arrive", 2, 1), *rest[:4]]
    rest = rest[4:]
    share = -(-len(rest) // max(1, seq_size - 2))
    for hop in range(2, seq_size):
        plan += [("arrive", 2, hop), *rest[(hop - 2) * share : (hop - 1) * share]]
    return plan + [("go", hop, count - 1) for hop in range(seq_size)]


def gather_kernel(seq_size, bits, proj_ref, in_ref, out_ref, x_ref, proj_all, in_all, out_all, x_all, *sems):
    own_sem, proj_send, proj_recv, line_send, line_recv, cube_send, cube_recv = sems
    z = lax.axis_index("seq")
    f = lax.axis_index("fsdp")
    count = len(bits)
    high_first = sorted(bits, reverse=True)
    bit_of = {bit: (f // bit) % 2 for bit in bits}
    mesh_id = pl.DeviceIdType.MESH

    barrier = pltpu.get_barrier_semaphore()
    for step in range(1, seq_size):
        pl.semaphore_signal(barrier, inc=1, device_id={"seq": lax.rem(z + step, seq_size)}, device_id_type=mesh_id)
    for bit in bits:
        pl.semaphore_signal(barrier, inc=1, device_id={"fsdp": f + bit * (1 - 2 * bit_of[bit])}, device_id_type=mesh_id)
    pl.semaphore_wait(barrier, seq_size - 1 + count)

    def place(buffer, s, done=()):
        if buffer is x_all:
            return buffer.at[s]
        return buffer.at[(s, *(slice(None) if bit in done else bit_of[bit] for bit in high_first))]

    def order_of(index, turn):
        return bits if (index + turn) % 2 == 0 else bits[-2::-1] + bits[-1:]

    cubes = ((proj_all, 0), (in_all, 0), (out_all, 1))

    def cube(index, s, turn, step):
        buffer, crossed = cubes[index]
        order = order_of(crossed, turn if index == 0 else 0)
        view = place(buffer, s, order[:step])
        bit = order[step]
        return pltpu.make_async_remote_copy(
            src_ref=view,
            dst_ref=view,
            send_sem=cube_send.at[index, turn, step],
            recv_sem=cube_recv.at[index, turn, step],
            device_id={"fsdp": f + bit * (1 - 2 * bit_of[bit])},
            device_id_type=mesh_id,
        )

    lines = ((in_all, in_ref), (out_all, out_ref), (x_all, x_ref))

    def line(index, side, hop):
        buffer, own = lines[index]
        ahead = 1 - 2 * side
        s = z - ahead * (hop - 1)
        view = place(buffer, s)
        return pltpu.make_async_remote_copy(
            src_ref=own if hop == 1 else view,
            dst_ref=view,
            send_sem=line_send.at[index, side, hop - 1],
            recv_sem=line_recv.at[index, side, hop - 1],
            device_id={"seq": z + ahead},
            device_id_type=mesh_id,
        )

    def line_wait(index, side, hop):
        view = place(lines[index][0], z - (1 - 2 * side) * hop)
        pltpu.make_async_remote_copy(
            src_ref=view,
            dst_ref=view,
            send_sem=line_send.at[index, side, hop - 1],
            recv_sem=line_recv.at[index, side, hop - 1],
            device_id={"seq": z - (1 - 2 * side)},
            device_id_type=mesh_id,
        ).wait_recv()

    def has_next(side):
        return z < seq_size - 1 if side == 0 else z > 0

    def has_block(side, hop):
        return z - hop >= 0 if side == 0 else z + hop < seq_size

    def proj(step):
        to = lax.rem(z + step, seq_size)
        return pltpu.make_async_remote_copy(
            src_ref=proj_ref.at[to],
            dst_ref=place(proj_all, z),
            send_sem=proj_send.at[step - 1],
            recv_sem=proj_recv.at[step - 1],
            device_id={"seq": to},
            device_id_type=mesh_id,
        )

    def proj_wait(step):
        view = place(proj_all, lax.rem(z + seq_size - step, seq_size))
        pltpu.make_async_remote_copy(
            src_ref=view,
            dst_ref=view,
            send_sem=proj_send.at[step - 1],
            recv_sem=proj_recv.at[step - 1],
            device_id={"seq": lax.rem(z + step, seq_size)},
            device_id_type=mesh_id,
        ).wait_recv()

    def turn_of(side, hop):
        return 0 if hop == 0 else 2 * hop - 1 + side

    def each_block(hop, act):
        act(0, lax.rem(z + seq_size - hop, seq_size), turn_of(0, hop))
        for index in (1, 2):
            if hop == 0:
                act(index, z, 0)
                continue
            for side in (0, 1):

                @pl.when(has_block(side, hop))
                def _(index=index, side=side):
                    act(index, z - (1 - 2 * side) * hop, turn_of(side, hop))

    owns = [
        pltpu.make_async_copy(own, place(buffer, z), own_sem.at[i])
        for i, (own, buffer) in enumerate(((proj_ref.at[z], proj_all), (in_ref, in_all), (out_ref, out_all), (x_ref, x_all)))
    ]
    for copy in owns:
        copy.start()
    for step in range(1, seq_size):
        proj(step).start()
    def send_own(index):
        for side in (0, 1):

            @pl.when(has_next(side))
            def _(side=side):
                line(index, side, 1).start()

    def arrive(index, hop):
        for side in (0, 1):

            @pl.when(has_block(side, hop))
            def _(side=side):
                line_wait(index, side, hop)
                if hop < seq_size - 1:

                    @pl.when(has_next(side))
                    def _():
                        line(index, side, hop + 1).start()

                if index < 2:
                    cube(index + 1, z - (1 - 2 * side) * hop, turn_of(side, hop), 0).start()

    def go_on(hop, step):
        def act(index, s, turn):
            cube(index, s, turn, step).wait()
            if step + 1 < count:
                cube(index, s, turn, step + 1).start()

        each_block(hop, act)

    def proj_arrive(hop):
        proj_wait(hop)
        cube(0, lax.rem(z + seq_size - hop, seq_size), turn_of(0, hop), 0).start()

    def own_cubes():
        for copy in owns:
            copy.wait()
        each_block(0, lambda index, s, turn: cube(index, s, turn, 0).start())

    acts = {"send": send_own, "own": own_cubes, "proj": proj_arrive, "arrive": arrive, "go": go_on}
    for name, *values in gather_plan(seq_size, count):
        acts[name](*values)
    for step in range(1, seq_size):
        proj(step).wait_send()
    for index in range(3):
        for side in (0, 1):
            for hop in range(1, seq_size):

                @pl.when(has_next(side) & has_block(side, hop - 1))
                def _(index=index, side=side, hop=hop):
                    line(index, side, hop).wait_send()


def start_gathers(proj, ffn_in, ffn_out, tokens_in):
    seq_size, fsdp_size = lax.axis_size("seq"), lax.axis_size("fsdp")
    bits = fsdp_bits(False)
    count = len(bits)

    def whole(shard):
        return jax.ShapeDtypeStruct((seq_size, *[2] * count, *shard), BF)

    turns = 2 * seq_size - 1
    dma = pltpu.SemaphoreType.DMA
    anywhere = pl.BlockSpec(memory_space=pl.ANY)
    outs = pl.pallas_call(
        functools.partial(gather_kernel, seq_size, bits),
        in_specs=[pl.BlockSpec(memory_space=pltpu.VMEM)] * 4,
        out_specs=[anywhere] * 4,
        out_shape=[
            whole(proj.shape[1:]),
            whole(ffn_in.shape),
            whole(ffn_out.shape),
            jax.ShapeDtypeStruct((seq_size, *tokens_in.shape), BF),
        ],
        scratch_shapes=[
            dma((4,)),
            dma((seq_size - 1,)),
            dma((seq_size - 1,)),
            dma((3, 2, seq_size - 1)),
            dma((3, 2, seq_size - 1)),
            dma((3, turns, count)),
            dma((3, turns, count)),
        ],
        compiler_params=pltpu.CompilerParams(collective_id=0, has_side_effects=True),
        cost_estimate=pl.CostEstimate(flops=0, bytes_accessed=100 * 2**20, transcendentals=0),
    )(proj, ffn_in, ffn_out, tokens_in)
    proj_all, in_all, out_all, inputs_all = outs
    flat = (seq_size, fsdp_size)
    return (
        proj_all.reshape(*flat, *proj.shape[1:]),
        in_all.reshape(*flat, *ffn_in.shape),
        out_all.reshape(*flat, *ffn_out.shape),
        inputs_all,
    )


def add_into(target, index, term, rows=64):
    depth = target.shape[-2]
    rows = next(n for n in (rows, 48, 32, 16, depth) if depth % n == 0)
    lead = target.shape[len(index) : -2]
    count = 1
    for size in lead:
        count *= size

    def step(i, carry):
        block, place = i // (depth // rows), pl.multiple_of((i % (depth // rows)) * rows, rows)
        where = []
        for size in reversed(lead):
            where.insert(0, block % size)
            block = block // size
        at = (*where, pl.ds(place, rows), slice(None))
        left = target[(*index, *at)].astype(F32)
        target[(*index, *at)] = (left + term(at).astype(F32)).astype(target.dtype)
        return carry

    lax.fori_loop(0, count * (depth // rows), step, 0)


def finish_kernel(seq_size, bits, da_ref, in_ref, out_ref, proj_ref, *refs):
    count = len(bits)
    da_out, in_out, out_out, proj_out = refs[:4]
    da_line, in_line, out_line, in_half, out_half = refs[4:9]
    proj_parts = refs[9 : 9 + count]
    own_sem, line_send, line_recv, half_send, half_recv, cube_send, cube_recv, proj_send, proj_recv = refs[9 + count :]
    z = lax.axis_index("seq")
    f = lax.axis_index("fsdp")
    bit_of = {bit: (f // bit) % 2 for bit in bits}
    mesh_id = pl.DeviceIdType.MESH
    last = seq_size - 1

    def flipped(bit):
        return {"fsdp": f + bit * (1 - 2 * bit_of[bit])}

    barrier = pltpu.get_barrier_semaphore()
    for step in range(1, seq_size):
        pl.semaphore_signal(barrier, inc=1, device_id={"seq": lax.rem(z + step, seq_size)}, device_id_type=mesh_id)
    for bit in bits:
        pl.semaphore_signal(barrier, inc=1, device_id=flipped(bit), device_id_type=mesh_id)
    pl.semaphore_wait(barrier, seq_size - 1 + count)

    lines = ((da_ref, da_line, da_out), (in_half, in_line, in_out), (out_half, out_line, out_out))

    def line(index, side, hop, own):
        terms, sums, _ = lines[index]
        if own:
            source = terms.at[seq_size - hop if side == 0 else hop - 1]
        else:
            source = sums.at[side, hop - 2]
        return pltpu.make_async_remote_copy(
            src_ref=source,
            dst_ref=sums.at[side, hop - 1],
            send_sem=line_send.at[index, side, hop - 1],
            recv_sem=line_recv.at[index, side, hop - 1],
            device_id={"seq": z + 1 - 2 * side},
            device_id_type=mesh_id,
        )

    def at_end(side):
        return z == 0 if side == 0 else z == last

    def from_end(side):
        return z if side == 0 else last - z

    def send_own(index):
        for side in (0, 1):

            @pl.when(at_end(side))
            def _(side=side):
                for hop in range(1, seq_size):
                    line(index, side, hop, True).start()

    def arrive(index, hop):
        terms, sums, _ = lines[index]
        for side in (0, 1):

            @pl.when((from_end(side) >= 1) & (from_end(side) <= hop))
            def _(side=side):
                pltpu.make_async_remote_copy(
                    src_ref=sums.at[side, hop - 1],
                    dst_ref=sums.at[side, hop - 1],
                    send_sem=line_send.at[index, side, hop - 1],
                    recv_sem=line_recv.at[index, side, hop - 1],
                    device_id={"seq": z - 1 + 2 * side},
                    device_id_type=mesh_id,
                ).wait_recv()
                if hop < last:
                    target = z - 1 + seq_size - hop if side == 0 else hop - last + z
                    add_into(sums, (side, hop - 1), lambda at: terms[(target, *at)])
                    line(index, side, hop + 1, False).start()

    def total(index):
        terms, sums, result = lines[index]
        add_first(result, lambda at: terms[(z, *at)])
        for side in (0, 1):

            @pl.when(from_end(side) >= 1)
            def _(side=side):
                add_into(result, (), lambda at: sums[(side, last - 1, *at)])

    def add_first(result, term):
        depth = result.shape[0]
        rows = next(n for n in (64, 32, 16, depth) if depth % n == 0)

        def step(i, carry):
            at = (pl.ds(pl.multiple_of(i * rows, rows), rows), slice(None))
            result[at] = term(at).astype(F32)
            return carry

        lax.fori_loop(0, depth // rows, step, 0)

    halves = ((in_ref, in_half, bits[0]), (out_ref, out_half, bits[-2] if count > 1 else bits[0]))

    def half(index):
        source, target, bit = halves[index]
        return pltpu.make_async_remote_copy(
            src_ref=source.at[:, 1 - bit_of[bit]],
            dst_ref=target,
            send_sem=half_send.at[index],
            recv_sem=half_recv.at[index],
            device_id=flipped(bit),
            device_id_type=mesh_id,
        )

    def half_add(index):
        source, target, bit = halves[index]
        half(index).wait()
        add_into(target, (), lambda at: source[(at[0], bit_of[bit], *at[1:])])

    order = bits[::-1]

    def cube(step):
        source = proj_ref if step == 0 else proj_parts[step - 1]
        left = sorted(order[step:], reverse=True)
        where = left.index(order[step])
        view = source.at[(slice(None),) * (1 + where) + (1 - bit_of[order[step]],)]
        return pltpu.make_async_remote_copy(
            src_ref=view,
            dst_ref=proj_parts[step],
            send_sem=cube_send.at[step],
            recv_sem=cube_recv.at[step],
            device_id=flipped(order[step]),
            device_id_type=mesh_id,
        )

    def cube_add(step):
        source = proj_ref if step == 0 else proj_parts[step - 1]
        left = sorted(order[step:], reverse=True)
        where = 1 + left.index(order[step])
        cube(step).wait()
        add_into(proj_parts[step], (), lambda at: source[(*at[:where], bit_of[order[step]], *at[where:])])

    def proj(step):
        to = lax.rem(z + step, seq_size)
        return pltpu.make_async_remote_copy(
            src_ref=proj_parts[-1].at[to],
            dst_ref=proj_out.at[z],
            send_sem=proj_send.at[step - 1],
            recv_sem=proj_recv.at[step - 1],
            device_id={"seq": to},
            device_id_type=mesh_id,
        )

    def proj_wait(step):
        view = proj_out.at[lax.rem(z + seq_size - step, seq_size)]
        copy = pltpu.make_async_remote_copy(
            src_ref=view,
            dst_ref=view,
            send_sem=proj_send.at[step - 1],
            recv_sem=proj_recv.at[step - 1],
            device_id={"seq": lax.rem(z + step, seq_size)},
            device_id_type=mesh_id,
        )
        copy.wait_recv()

    send_own(0)
    half(0).start()
    half(1).start()
    cube(0).start()
    cube_add(0)
    cube(1).start() if count > 1 else None
    half_add(0)
    half_add(1)
    send_own(1)
    send_own(2)
    for hop in range(1, seq_size):
        arrive(0, hop)
        if hop < count:
            cube_add(hop)
            if hop + 1 < count:
                cube(hop + 1).start()
        if hop == min(count, last) - 1 or (count == 1 and hop == 1):
            own = pltpu.make_async_copy(proj_parts[-1].at[z], proj_out.at[z], own_sem)
            own.start()
            for step in range(1, seq_size):
                proj(step).start()
    total(0)
    for hop in range(1, seq_size):
        arrive(1, hop)
        arrive(2, hop)
    total(1)
    total(2)
    pltpu.make_async_copy(proj_parts[-1].at[z], proj_out.at[z], own_sem).wait()
    for step in range(1, seq_size):
        proj_wait(step)
        proj(step).wait_send()
    for index in range(3):
        for side in (0, 1):
            for hop in range(1, seq_size):

                @pl.when(at_end(side) | ((from_end(side) >= 1) & (from_end(side) <= hop - 1)))
                def _(index=index, side=side, hop=hop):
                    line(index, side, hop, True).wait_send()


def finish_sums(da, ffin, ffout, proj):
    seq_size = lax.axis_size("seq")
    bits = fsdp_bits(False)
    count = len(bits)
    dma = pltpu.SemaphoreType.DMA
    inside = pl.BlockSpec(memory_space=pltpu.VMEM)

    def line_of(shape):
        return pltpu.VMEM((2, seq_size - 1, *shape), BF)

    order = bits[::-1]
    parts = [pltpu.VMEM((seq_size, *[2] * (count - 1 - step), *proj.shape[-2:]), BF) for step in range(count)]
    shapes = [v.shape[-2:] for v in (da, ffin, ffout)]
    return pl.pallas_call(
        functools.partial(finish_kernel, seq_size, bits),
        in_specs=[inside] * 4,
        out_specs=[inside] * 4,
        out_shape=[jax.ShapeDtypeStruct(shape, F32) for shape in shapes]
        + [jax.ShapeDtypeStruct((seq_size, *proj.shape[-2:]), BF)],
        scratch_shapes=[
            *[line_of(shape) for shape in shapes],
            *[pltpu.VMEM((seq_size, *shape), BF) for shape in shapes[1:]],
            *parts,
            dma,
            dma((3, 2, seq_size - 1)),
            dma((3, 2, seq_size - 1)),
            dma((2,)),
            dma((2,)),
            dma((len(order),)),
            dma((len(order),)),
            dma((seq_size - 1,)),
            dma((seq_size - 1,)),
        ],
        compiler_params=pltpu.CompilerParams(
            collective_id=1, has_side_effects=True, vmem_limit_bytes=56 * 2**20
        ),
        cost_estimate=pl.CostEstimate(flops=0, bytes_accessed=100 * 2**20, transcendentals=0),
    )(da, ffin, ffout, proj)


def whole_tiles(shard, rows=16):
    return shard if shard.shape[0] % rows == 0 else shard.reshape(rows, -1)


def on_device(
    inputs,
    qkv_proj,
    out_proj,
    ffn_in,
    ffn_out,
    norm_gains,
    norm_biases,
    centroids,
    expert_in,
    expert_out,
    doc_lengths,
    routes,
    out_grad,
):
    rows, span, width = inputs.shape
    tokens = rows * span
    seq_size, fsdp_size = lax.axis_size("seq"), lax.axis_size("fsdp")
    here = lax.axis_index("seq")
    length = span * seq_size
    cols = width // seq_size
    capacity = max(2, 3 * tokens // (2 * fsdp_size))
    groups = seq_size // 2

    docs = doc_lengths.shape[1]
    key_pos = jnp.arange(length, dtype=jnp.int32)
    doc_ids = jnp.zeros((rows, length), jnp.int32)
    doc_end = jnp.zeros((rows, 1), jnp.int32)
    for j in range(docs - 1):
        doc_end = doc_end + doc_lengths[:, j : j + 1]
        doc_ids = doc_ids + (key_pos[None, :] >= doc_end).astype(jnp.int32)
    id_rows, id_cols = doc_ids[:, None, :], doc_ids[:, :, None]

    depth = out_proj.shape[0]
    wide = 3 * cols + width
    slices = qkv_proj.reshape(3, depth, seq_size, cols).transpose(2, 1, 0, 3).reshape(seq_size, depth, 3 * cols)
    slices = jnp.concatenate([slices, jnp.broadcast_to(out_proj[None], (seq_size, depth, width))], axis=2)
    small = jnp.concatenate([norm_gains.reshape(-1), norm_biases.reshape(-1), centroids[0]])
    spare = 32 - depth % 16 if depth % 16 else 16
    extra = jnp.stack([jnp.pad(v, (0, wide - v.shape[0])) for v in (small, routes.reshape(tokens).astype(BF))])
    extra = jnp.pad(extra, ((0, spare - 2), (0, 0)))[None]
    extra = jnp.broadcast_to(extra, (seq_size, spare, wide))
    bits = fsdp_bits(False)
    crossed = fsdp_bits(True)
    tokens_in = inputs.reshape(tokens, width)
    proj_all, ffin_all, ffout_all, inputs_all = start_gathers(
        jnp.concatenate([slices, extra], axis=1), whole_tiles(ffn_in), whole_tiles(ffn_out), tokens_in
    )
    inputs_all = inputs_all.reshape(seq_size * tokens, width)
    ffin_all, ffout_all = ffin_all.reshape(width, -1), ffout_all.reshape(-1, width)
    qkv_mine = proj_all[:, :, :depth, : 3 * cols].reshape(width, 3 * cols)
    out_all = proj_all[:, :, :depth, 3 * cols :].reshape(width, width)
    small = proj_all[:, :, depth, :]
    rows_of = small[:, :, : 6 * depth].astype(F32).reshape(-1, 6, depth).transpose(1, 0, 2).reshape(6, width)
    gain_rows, bias_rows = rows_of[:3], rows_of[3:]
    mine = small[:, :, 6 * depth : 6 * depth + cols]
    centroid = lax.dynamic_index_in_dim(mine, lax.axis_index("fsdp"), 1, keepdims=False).reshape(width)
    win_mine, wout_mine, dr_mine = after((expert_in[0], expert_out[0], out_grad.reshape(tokens, width)), inputs_all)
    parts_all = norm_parts(inputs_all.astype(F32))
    normed_flat = ((inputs_all.astype(F32) - parts_all[0]) * parts_all[1] * gain_rows[0] + bias_rows[0]).astype(BF)
    projected = mm(normed_flat, qkv_mine).astype(BF).reshape(seq_size, rows, span, 3 * cols)

    attended_mine, lse_rows = attend(projected, id_rows, id_cols)
    win_half, wout_half = win_mine.shape[0] // 2, wout_mine.shape[0] // 2
    pair_in_low = seq_pair(win_mine[:win_half])
    pair_in_high = seq_pair(win_mine[win_half:])
    attended_mine, pair_in_low, pair_in_high = lax.optimization_barrier((attended_mine, pair_in_low, pair_in_high))
    attended = seq_exchange(attended_mine).transpose(1, 2, 0, 3).reshape(tokens, width)
    pair_out_low = seq_pair(after(wout_mine[:wout_half], attended))

    fsdp_here = lax.axis_index("fsdp")
    routes_all = lax.dynamic_index_in_dim(proj_all[:, :, depth + 1, :tokens], fsdp_here, 1, keepdims=False)
    later = (jnp.arange(tokens)[:, None] > jnp.arange(tokens)[None, :]).astype(BF)
    placings = []
    for group in range(groups):
        route = pick(routes_all, (here + seq_size - 2 * group) % seq_size).astype(jnp.int32)
        choose = route[:, None] == jnp.arange(fsdp_size, dtype=jnp.int32)[None, :]
        before = mm(later, choose.astype(BF))
        slot_rank = jnp.sum(jnp.where(choose, before, 0.0), axis=1).astype(jnp.int32)
        target = route * capacity + slot_rank
        slots = jnp.arange(fsdp_size * capacity, dtype=jnp.int32)
        placings.append((target[:, None] == slots[None, :]).astype(BF))
    grad_tokens = out_grad.reshape(tokens, width)

    def slots_of(placing, values):
        return mm_tn(placing, values).astype(BF).reshape(fsdp_size, capacity, width)

    def swap_slots(values):
        return lax.all_to_all(values, "fsdp", split_axis=0, concat_axis=0, tiled=True)

    def tokens_of(placing, values):
        return mm(placing, values.reshape(fsdp_size * capacity, width))

    grad_own = swap_slots(slots_of(placings[0], grad_tokens)).reshape(-1, width)


    resid_in = tokens_in.astype(F32)
    middle = resid_in + mm(attended, out_all)
    parts_two = norm_parts(middle)
    hidden_low = ((middle - parts_two[0]) * parts_two[1] * gain_rows[1] + bias_rows[1]).astype(BF)
    active, active_slope = gelu_pair(mm(hidden_low, ffin_all))
    active_low, active_slope = lax.optimization_barrier((active.astype(BF), active_slope.astype(BF)))
    block_out = middle + mm(active_low, ffout_all)
    parts_three = norm_parts(block_out)
    routed = ((block_out - parts_three[0]) * parts_three[1] * gain_rows[2] + bias_rows[2]).astype(BF)

    routed, pair_out_low = lax.optimization_barrier((routed, pair_out_low))
    slots_own = slots_of(placings[0], routed)
    pair_out_high = seq_pair(after(wout_mine[wout_half:], slots_own))
    win = jnp.concatenate([win_mine, jnp.concatenate([pair_in_low, pair_in_high], axis=0)], axis=1)

    arrived_all, dz_all, du_all, act_all, back_terms, back_slots, gated_all = [], [], [], [], [], [], []
    centroid_term = jnp.zeros((width,), F32)
    for group in range(groups):
        if group == 0:
            arrived, grad_arrived = swap_slots(slots_own).reshape(-1, width), grad_own
        else:
            slots_here = slots_of(placings[group], after(seq_shift(routed, 2 * group), act))
            arrived = swap_slots(slots_here).reshape(-1, width)
            grads_here = seq_shift(after(dr_mine, slots_own), 2 * group)
            grads_here = slots_of(placings[group], after(grads_here, slots_here))
            grad_arrived = swap_slots(grads_here).reshape(-1, width)
        gate = jax.nn.sigmoid(mm(arrived, centroid))
        act, slope = gelu_pair(mm(arrived, win))
        act, slope = lax.optimization_barrier((act.astype(BF), slope.astype(BF)))
        if group == 0:
            wout = jnp.concatenate([wout_mine, pair_out_low, after(pair_out_high, act)], axis=0)
        result = mm(act, wout)
        gated_low = (gate[:, None] * result).astype(BF).reshape(fsdp_size, capacity, width)
        gated = grad_arrived.astype(F32)
        dz = (gate[:, None] * gated).astype(BF)
        dl = jnp.sum(gated * result, axis=-1) * gate * (1.0 - gate)
        du = (slope.astype(F32) * mm_nt(dz, wout)).astype(BF)
        rows_grad = mm_nt(du, win) + dl[:, None] * centroid.astype(F32)
        centroid_term = centroid_term + jnp.sum(dl[:, None] * arrived.astype(F32), axis=0)
        back = swap_slots(rows_grad.astype(BF).reshape(fsdp_size, capacity, width))
        back_slots.append(back)
        back = tokens_of(placings[group], back)
        if group:
            back = seq_shift(back.astype(BF), -2 * group).astype(F32)
        back_terms.append(back)
        gated_all.append(gated_low)
        arrived_all.append(arrived)
        dz_all.append(dz)
        du_all.append(du)
        act_all.append(act)

    half = expert_in.shape[2]
    arrived, dz, du, act = (jnp.concatenate(v, axis=0) for v in (arrived_all, dz_all, du_all, act_all))
    in_sent = mm_tn(arrived, du[:, half:]).astype(BF)
    out_sent = mm_tn(act[:, half:], dz).astype(BF)
    in_kept = mm_tn(arrived, du[:, :half])
    out_kept = mm_tn(act[:, :half], dz)
    in_pair = seq_pair(after(in_sent, in_kept, out_kept))

    gated_back = swap_slots(after(jnp.concatenate(gated_all, axis=1), *back_slots))
    gated_back = gated_back.reshape(fsdp_size, groups, capacity, width)
    out_terms = [tokens_of(placings[group], gated_back[:, group]) for group in range(groups)]
    back_sum, in_sent, out_sent, in_kept, out_kept, *out_terms = lax.optimization_barrier(
        (sum(back_terms), in_sent, out_sent, in_kept, out_kept, out_terms[0], *(v.astype(BF) for v in out_terms[1:]))
    )

    block_norm_grad, gain_three, bias_three = norm_back(block_out, parts_three, gain_rows[2], back_sum)
    block_grad = grad_tokens.astype(F32) + block_norm_grad
    block_low = block_grad.astype(BF)
    hidden_grad = (active_slope.astype(F32) * mm_nt(block_low, ffout_all)).astype(BF)
    normed_two_grad = mm_nt(hidden_grad, ffin_all)
    middle_norm_grad, gain_two, bias_two = norm_back(middle, parts_two, gain_rows[1], normed_two_grad)
    middle_grad = block_grad + middle_norm_grad
    branch = middle_grad.astype(BF)
    attended_grad = mm_nt(branch, out_all).astype(BF)
    attended_grad = attended_grad.reshape(rows, span, seq_size, cols).transpose(2, 0, 1, 3)
    attended_grad, in_pair = lax.optimization_barrier((attended_grad, in_pair))
    active_low, hidden_low = after((active_low, hidden_low), attended_grad)
    attended_grad = seq_exchange(attended_grad)

    ffout_terms = hyper_split(by_device(mm_tn(active_low, block_low)))
    ffin_terms = hyper_split(by_device(mm_tn(hidden_low, hidden_grad)))
    out_proj_term = mm_tn(attended, branch)
    ffout_terms = hyper_scatter_step(ffout_terms, crossed[-1])
    ffin_terms = hyper_scatter_step(ffin_terms, bits[-1])
    attended_grad, ffout_terms, ffin_terms = lax.optimization_barrier((attended_grad, ffout_terms, ffin_terms))
    out_pair = seq_pair(after(out_sent, attended_grad))
    out_terms = out_terms[:1] + [
        seq_shift(after(out_terms[group], attended_grad), -2 * group) for group in range(1, groups)
    ]
    ffout_terms = hyper_scatter(ffout_terms, crossed[-2:0:-1])
    ffin_terms = hyper_scatter(ffin_terms, bits[-2:0:-1])

    dq, dk, dv = attend_back(projected, attended_grad, lse_rows, id_rows, id_cols)
    projected_grad = jnp.concatenate([dq, dk, dv], axis=-1).reshape(seq_size * tokens, 3 * cols)
    projected_grad, out_pair = lax.optimization_barrier((projected_grad, out_pair))
    normed_low_terms = mm_nt(projected_grad, qkv_mine).astype(BF)
    unit_all = (inputs_all.astype(F32) - parts_all[0]) * parts_all[1]
    terms_wide = normed_low_terms.astype(F32)
    gain_one, bias_one = jnp.sum(terms_wide * unit_all, axis=0), jnp.sum(terms_wide, axis=0)
    small_terms = jnp.stack([gain_one, gain_two, gain_three, bias_one, bias_two, bias_three])

    proj_terms = jnp.concatenate([mm_tn(normed_flat, projected_grad).astype(BF), out_proj_term.astype(BF)], axis=1)
    proj_terms = proj_terms.reshape(seq_size, fsdp_size, depth, wide)
    small_rows = small_terms.astype(BF).reshape(6, seq_size, fsdp_size, depth).transpose(1, 2, 0, 3)
    small_rows = small_rows.reshape(seq_size, fsdp_size, 1, 6 * depth)
    small_rows = jnp.pad(small_rows, ((0, 0), (0, 0), (0, spare - 1), (0, wide - 6 * depth)))
    centroid_rows = jnp.where(
        (jnp.arange(fsdp_size) == fsdp_here)[None, :, None], centroid_term.reshape(seq_size, 1, cols), 0.0
    )
    small_rows = lax.dynamic_update_slice(small_rows, centroid_rows.astype(BF)[:, :, None], (0, 0, 1, 0))
    proj_terms = hyper_split(jnp.concatenate([proj_terms, small_rows], axis=2))
    proj_terms, *out_terms = lax.optimization_barrier((proj_terms, *out_terms))
    outputs = block_out + sum(v.astype(F32) for v in out_terms)
    outputs = outputs.astype(BF).reshape(rows, span, width)
    last_in = ffin_terms.reshape(seq_size, 2, *ffin_terms.shape[-2:])
    last_out = ffout_terms.reshape(seq_size, 2, *ffout_terms.shape[-2:])
    normed_one_grad, ffn_in_grad, ffn_out_grad, proj_sums = finish_sums(
        normed_low_terms.reshape(seq_size, tokens, width), last_in, last_out, proj_terms
    )
    ffn_in_grad, ffn_out_grad = ffn_in_grad.reshape(ffn_in.shape), ffn_out_grad.reshape(ffn_out.shape)
    proj_sums = proj_sums.astype(F32)
    qkv_grad = proj_sums[:, :depth, : 3 * cols].reshape(seq_size, depth, 3, cols)
    qkv_grad = qkv_grad.transpose(2, 1, 0, 3).reshape(qkv_proj.shape)
    out_proj_grad = jnp.sum(proj_sums[:, :depth, 3 * cols :], axis=0)
    small_grad = jnp.sum(proj_sums[:, depth, : 6 * depth], axis=0).reshape(6, depth)
    centroids_grad = jnp.sum(proj_sums[:, depth + 1, :cols], axis=0)[None]

    expert_in_grad = (in_kept + in_pair.astype(F32))[None]
    expert_out_grad = (out_kept + out_pair.astype(F32))[None]

    input_norm_grad, _, _ = norm_back(resid_in, norm_parts(resid_in), gain_rows[0], normed_one_grad)
    input_grad = (middle_grad + input_norm_grad).reshape(rows, span, width)
    return (
        outputs,
        input_grad,
        qkv_grad,
        out_proj_grad,
        ffn_in_grad,
        ffn_out_grad,
        small_grad[:3],
        small_grad[3:],
        centroids_grad,
        expert_in_grad,
        expert_out_grad,
    )


def solution(mesh):
    dense = P(("seq", "fsdp"), None)
    placed = (
        P("fsdp", "seq", None),
        P(None, ("seq", "fsdp"), None),
        dense,
        dense,
        dense,
        P(None, ("seq", "fsdp")),
        P(None, ("seq", "fsdp")),
        P("fsdp", "seq"),
        P("fsdp", None, "seq"),
        P("fsdp", "seq", None),
        P("fsdp", None),
        P("seq", "fsdp", None, None),
        P("fsdp", "seq", None),
    )
    returned = (
        P("fsdp", "seq", None),
        P("fsdp", "seq", None),
        P(None, ("seq", "fsdp"), None),
        dense,
        dense,
        dense,
        P(None, ("seq", "fsdp")),
        P(None, ("seq", "fsdp")),
        P("fsdp", "seq"),
        P("fsdp", None, "seq"),
        P("fsdp", "seq", None),
    )
    return jax.shard_map(on_device, mesh=mesh, in_specs=placed, out_specs=returned, check_vma=False)
```

```python
import functools

import jax
import jax.numpy as jnp
from jax import lax
from jax.experimental import pallas as pl
from jax.experimental.pallas import tpu as pltpu
from jax.sharding import PartitionSpec as P

HEAD_DIM = 64
LANES = 128
norm_eps = 1e-05
BF = jnp.bfloat16
F32 = jnp.float32


def layer_norm(values, gain_row, shift_row):
    average = jnp.mean(values, axis=-1, keepdims=True)
    centered = values - average
    variance = jnp.mean(centered * centered, axis=-1, keepdims=True)
    return centered * lax.rsqrt(variance + norm_eps) * gain_row + shift_row


def gelu_pair(values):
    cdf = 0.5 * (1.0 + lax.erf(values * (0.5**0.5)))
    pdf = 0.3989422804014327 * jnp.exp(-0.5 * values * values)
    return values * cdf, cdf + values * pdf


def mm(left, right):
    return jnp.dot(left, right, preferred_element_type=F32)


def mm_nt(left, right):
    return lax.dot_general(left, right, (((1,), (1,)), ((), ())), preferred_element_type=F32)


def mm_tn(left, right):
    return lax.dot_general(left, right, (((0,), (0,)), ((), ())), preferred_element_type=F32)


def norm_parts(values):
    average = jnp.mean(values, axis=-1, keepdims=True)
    centered = values - average
    variance = jnp.mean(centered * centered, axis=-1, keepdims=True)
    return average, lax.rsqrt(variance + norm_eps)


def norm_back(values, parts, gain_row, grads):
    average, scale = parts
    unit = (values - average) * scale
    unit_grad = grads * gain_row
    first = jnp.mean(unit_grad, axis=-1, keepdims=True)
    second = jnp.mean(unit_grad * unit, axis=-1, keepdims=True)
    return scale * (unit_grad - first - unit * second), jnp.sum(grads * unit, axis=0), jnp.sum(grads, axis=0)


def tie(*values):
    return lax.optimization_barrier(values)


def seq_shift(values, step):
    size = lax.axis_size("seq")
    return lax.ppermute(values, "seq", [(i, (i + step) % size) for i in range(size)])


def seq_pair(values):
    size = lax.axis_size("seq")
    return lax.ppermute(values, "seq", [(i, i ^ 1) for i in range(size)])


def put(buffer, values, place):
    return lax.dynamic_update_index_in_dim(buffer, values, place, 0)


def pick(values, place):
    return lax.dynamic_index_in_dim(values, place, 0, keepdims=False)


def seq_exchange(values, chained=False):
    size = lax.axis_size("seq")
    here = lax.axis_index("seq")
    result = put(jnp.zeros_like(values), pick(values, here), here)
    arrived = None
    for step in range(1, size):
        sent = pick(values, (here + step) % size)
        if chained and arrived is not None:
            sent, arrived = tie(sent, arrived)
        if arrived is not None:
            result = put(result, arrived, (here - step + 1) % size)
        arrived = seq_shift(sent, step)
    return put(result, arrived, (here - size + 1) % size)


def seq_sum_scatter(values):
    size = lax.axis_size("seq")
    here = lax.axis_index("seq")
    total = pick(values, here).astype(F32)
    for step in range(1, size):
        arrived = seq_shift(pick(values, (here + step) % size).astype(BF), step)
        total = total + arrived.astype(F32)
    return total


def masked_pair(block):
    lane = lax.broadcasted_iota(jnp.int32, block.shape, 1)
    zero = jnp.zeros_like(block)
    return jnp.where(lane < HEAD_DIM, block, zero), jnp.where(lane < HEAD_DIM, zero, block)


def allowed_block(id_col, id_row, start, size, end):
    key_pos = lax.broadcasted_iota(jnp.int32, (end, size), 0)
    query_pos = start + lax.broadcasted_iota(jnp.int32, (end, size), 1)
    return (id_col[:end, :] == id_row[:, start:end]) & (key_pos <= query_pos)


def attend_kernel(size, q_ref, k_ref, v_ref, id_row_ref, id_col_ref, o_ref, lse_ref, o_all):
    length = id_row_ref.shape[-1]
    queries = q_ref[...].reshape(length, LANES) * jnp.asarray(HEAD_DIM**-0.5, BF)
    keys = k_ref[...].reshape(length, LANES)
    values_t = v_ref[...].reshape(length, LANES).T
    id_row = id_row_ref[0]
    id_col = id_col_ref[0]
    for start in range(0, length, size):
        end = start + size
        mask = allowed_block(id_col, id_row, start, size, end)
        parts = []
        for head, query in enumerate(masked_pair(queries[start:end])):
            scores = jnp.where(mask, mm_nt(keys[:end], query), -1e30)
            top = jnp.max(scores, axis=0, keepdims=True)
            powers = jnp.exp(scores - top)
            whole = jnp.sum(powers, axis=0, keepdims=True)
            weights = (powers * (1.0 / whole)).astype(BF)
            lse_ref[0, 0, pl.ds(head, 1), pl.ds(start, size)] = top + jnp.log(whole)
            part = values_t[head * HEAD_DIM : (head + 1) * HEAD_DIM, :end]
            parts.append(mm(part, weights))
        o_all[pl.ds(start, size), :] = jnp.concatenate(parts, axis=0).T
    o_ref[...] = o_all[...].astype(BF).reshape(o_ref.shape)


def attend_back_kernel(
    size, q_ref, k_ref, v_ref, do_ref, lse_ref, id_row_ref, id_col_ref, dq_ref, dk_ref, dv_ref, dq_all, dk_all, dv_all
):
    length = id_row_ref.shape[-1]
    scale = HEAD_DIM**-0.5
    queries = q_ref[...].reshape(length, LANES) * jnp.asarray(scale, BF)
    keys = k_ref[...].reshape(length, LANES)
    keys_t = keys.T
    values = v_ref[...].reshape(length, LANES)
    grads = do_ref[...].reshape(length, LANES)
    id_row = id_row_ref[0]
    id_col = id_col_ref[0]
    dk_all[...] = jnp.zeros_like(dk_all)
    dv_all[...] = jnp.zeros_like(dv_all)
    for start in range(0, length, size):
        end = start + size
        mask = allowed_block(id_col, id_row, start, size, end)
        parts = []
        heads = zip(masked_pair(queries[start:end]), masked_pair(grads[start:end]), strict=True)
        for head, (query, grad) in enumerate(heads):
            scores = jnp.where(mask, mm_nt(keys[:end], query), -1e30)
            probs = jnp.exp(scores - lse_ref[0, 0, pl.ds(head, 1), pl.ds(start, size)])
            prob_grad = mm_nt(values[:end], grad)
            total = jnp.sum(probs * prob_grad, axis=0, keepdims=True)
            score_grad = (probs * (prob_grad - total)).astype(BF)
            dv_all[pl.ds(0, end), :] += mm(probs.astype(BF), grad)
            dk_all[pl.ds(0, end), :] += mm(score_grad, query)
            parts.append(mm(keys_t[head * HEAD_DIM : (head + 1) * HEAD_DIM, :end], score_grad))
        dq_all[pl.ds(start, size), :] = jnp.concatenate(parts, axis=0).T * scale
    dq_ref[...] = dq_all[...].astype(BF).reshape(dq_ref.shape)
    dk_ref[...] = dk_all[...].astype(BF).reshape(dk_ref.shape)
    dv_ref[...] = dv_all[...].astype(BF).reshape(dv_ref.shape)


def attention_specs(projected, length):
    blocks, rows, span, width3 = projected.shape
    columns = width3 // 3 // LANES

    def part(index):
        return pl.BlockSpec((blocks, 1, span, LANES), lambda r, c: (0, r, 0, index * columns + c))

    id_row = pl.BlockSpec((1, 1, length), lambda r, c: (r, 0, 0))
    id_col = pl.BlockSpec((1, length, 1), lambda r, c: (r, 0, 0))
    lse = pl.BlockSpec((1, 1, 2, length), lambda r, c: (r, c, 0, 0))
    return rows, columns, part, id_row, id_col, lse


def attend(projected, id_rows, id_cols):
    length = id_rows.shape[-1]
    blocks, rows, span, width3 = projected.shape
    rows, columns, part, id_row, id_col, lse = attention_specs(projected, length)
    return pl.pallas_call(
        functools.partial(attend_kernel, min(256, length)),
        grid=(rows, columns),
        in_specs=[part(0), part(1), part(2), id_row, id_col],
        out_specs=[part(0), lse],
        out_shape=[
            jax.ShapeDtypeStruct((blocks, rows, span, width3 // 3), BF),
            jax.ShapeDtypeStruct((rows, columns, 2, length), F32),
        ],
        scratch_shapes=[pltpu.VMEM((length, LANES), F32)],
        compiler_params=pltpu.CompilerParams(vmem_limit_bytes=40 * 2**20),
        cost_estimate=pl.CostEstimate(flops=10**6, bytes_accessed=2**16, transcendentals=0),
    )(projected, projected, projected, id_rows, id_cols)


def attend_back(projected, grads, lse_rows, id_rows, id_cols):
    length = id_rows.shape[-1]
    blocks, rows, span, width3 = projected.shape
    rows, columns, part, id_row, id_col, lse = attention_specs(projected, length)
    shape = jax.ShapeDtypeStruct((blocks, rows, span, width3 // 3), BF)
    return pl.pallas_call(
        functools.partial(attend_back_kernel, min(256, length)),
        grid=(rows, columns),
        in_specs=[part(0), part(1), part(2), part(0), lse, id_row, id_col],
        out_specs=[part(0)] * 3,
        out_shape=[shape] * 3,
        scratch_shapes=[pltpu.VMEM((length, LANES), F32)] * 3,
        compiler_params=pltpu.CompilerParams(vmem_limit_bytes=48 * 2**20),
        cost_estimate=pl.CostEstimate(flops=10**6, bytes_accessed=2**16, transcendentals=0),
    )(projected, projected, projected, grads, lse_rows, id_rows, id_cols)


def fsdp_flip(values, bit):
    size = lax.axis_size("fsdp")
    return lax.ppermute(values, "fsdp", [(i, i ^ bit) for i in range(size)])


def fsdp_bits(crossed):
    bits = [1 << i for i in range(1, lax.axis_size("fsdp").bit_length() - 1)]
    return (bits[::-1] if crossed else bits) + [1]


def hyper_split(parts):
    count = parts.shape[1].bit_length() - 1
    return parts.reshape(parts.shape[0], *[2] * count, *parts.shape[2:])


def by_device(term):
    seq_size, fsdp_size = lax.axis_size("seq"), lax.axis_size("fsdp")
    depth = term.shape[0] // (seq_size * fsdp_size)
    tile = (depth, term.shape[1]) if depth % 16 == 0 else (16, depth * term.shape[1] // 16)
    return term.astype(BF).reshape(seq_size, fsdp_size, *tile)


def ffn_kernel(middle_ref, gains_ref, biases_ref, win_ref, wout_ref, normed_ref, act_ref, slope_ref, block_ref, routed_ref):
    chunk = pl.program_id(0)

    def norm(values, row):
        average, scale = norm_parts(values)
        return ((values - average) * scale * gains_ref[row : row + 1] + biases_ref[row : row + 1]).astype(BF)

    @pl.when(chunk == 0)
    def _():
        normed_ref[...] = norm(middle_ref[...], 1)
        block_ref[...] = middle_ref[...]

    act, slope = gelu_pair(mm(normed_ref[...], win_ref[...]))
    act = act.astype(BF)
    act_ref[...] = act
    slope_ref[...] = slope.astype(BF)
    block_ref[...] += mm(act, wout_ref[...])

    @pl.when(chunk == pl.num_programs(0) - 1)
    def _():
        routed_ref[...] = norm(block_ref[...], 2)


def ffn_specs(tokens, width, hidden):
    size = min(512, hidden)
    whole = pl.BlockSpec((tokens, width), lambda j: (0, 0))
    piece = pl.BlockSpec((tokens, size), lambda j: (0, j))
    row = pl.BlockSpec((8, width), lambda j: (0, 0))
    return size, whole, piece, row, [
        pl.BlockSpec((width, size), lambda j: (0, j)),
        pl.BlockSpec((size, width), lambda j: (j, 0)),
    ]


def ffn_forward(middle, gains, biases, win, wout):
    tokens, width = middle.shape
    hidden = win.shape[1]
    size, whole, piece, row, weights = ffn_specs(tokens, width, hidden)
    low, wide = jax.ShapeDtypeStruct((tokens, width), BF), jax.ShapeDtypeStruct((tokens, hidden), BF)
    return pl.pallas_call(
        ffn_kernel,
        grid=(hidden // size,),
        in_specs=[whole, row, row, *weights],
        out_specs=[whole, piece, piece, whole, whole],
        out_shape=[low, wide, wide, jax.ShapeDtypeStruct((tokens, width), F32), low],
        compiler_params=pltpu.CompilerParams(vmem_limit_bytes=48 * 2**20),
        cost_estimate=pl.CostEstimate(flops=10**6, bytes_accessed=2**16, transcendentals=0),
    )(middle, gains, biases, win, wout)


def ffn_back_kernel(
    back_ref, block_ref, grad_ref, middle_ref, gains_ref, slope_ref, win_ref, wout_ref,
    low_ref, du_ref, dh_ref, branch_ref, terms_ref, total,
):
    chunk = pl.program_id(0)

    def norm_grad(values, row, grads):
        moved, gain, bias = norm_back(values, norm_parts(values), gains_ref[row : row + 1], grads)
        return moved, gain[None], bias[None]

    @pl.when(chunk == 0)
    def _():
        moved, gain, bias = norm_grad(block_ref[...], 2, back_ref[...])
        grads = grad_ref[...].astype(F32) + moved
        dh_ref[...] = grads
        low_ref[...] = grads.astype(BF)
        terms_ref[0:1] = gain
        terms_ref[1:2] = bias
        total[...] = jnp.zeros_like(total)

    du = (slope_ref[...].astype(F32) * mm_nt(low_ref[...], wout_ref[...])).astype(BF)
    du_ref[...] = du
    total[...] += mm_nt(du, win_ref[...])

    @pl.when(chunk == pl.num_programs(0) - 1)
    def _():
        moved, gain, bias = norm_grad(middle_ref[...], 1, total[...])
        grads = dh_ref[...] + moved
        dh_ref[...] = grads
        branch_ref[...] = grads.astype(BF)
        terms_ref[2:3] = gain
        terms_ref[3:4] = bias


def ffn_backward(back, block_out, grads, middle, gains, slope, win, wout):
    tokens, width = middle.shape
    hidden = win.shape[1]
    size, whole, piece, row, weights = ffn_specs(tokens, width, hidden)
    low, wide = jax.ShapeDtypeStruct((tokens, width), BF), jax.ShapeDtypeStruct((tokens, hidden), BF)
    f32 = jax.ShapeDtypeStruct((tokens, width), F32)
    return pl.pallas_call(
        ffn_back_kernel,
        grid=(hidden // size,),
        in_specs=[whole, whole, whole, whole, row, piece, *weights],
        out_specs=[whole, piece, whole, whole, row],
        out_shape=[low, wide, f32, low, jax.ShapeDtypeStruct((8, width), F32)],
        scratch_shapes=[pltpu.VMEM((tokens, width), F32)],
        compiler_params=pltpu.CompilerParams(vmem_limit_bytes=48 * 2**20),
        cost_estimate=pl.CostEstimate(flops=10**6, bytes_accessed=2**16, transcendentals=0),
    )(back, block_out, grads, middle, gains, slope, win, wout)


def expert_kernel(x_ref, dr_ref, centroid_ref, win_own, wout_own, win_low, win_high, wout_low, wout_high, *refs):
    act_ref, du_ref, dz_ref, all_ref, gated_ref, dx_ref, term_ref, total, back, win_ref, wout_ref = refs[-11:]
    chunk = pl.program_id(0)
    own = pl.num_programs(0) - 2
    for here, win_part, wout_part in (
        (chunk < own, win_own, wout_own),
        (chunk == own, win_low, wout_low),
        (chunk == own + 1, win_high, wout_high),
    ):

        @pl.when(here)
        def _(win_part=win_part, wout_part=wout_part):
            win_ref[...] = win_part[...]
            wout_ref[...] = wout_part[...]

    x = x_ref[...]

    def gate_of():
        logits = mm_nt(x, centroid_ref[...])[:, :1]
        return 1.0 / (1.0 + jnp.exp(-logits))

    @pl.when(chunk == 0)
    def _():
        dz_ref[...] = (gate_of() * dr_ref[...].astype(F32)).astype(BF)
        all_ref[...] = x
        total[...] = jnp.zeros_like(total)
        back[...] = jnp.zeros_like(back)

    act, slope = gelu_pair(mm(x, win_ref[...]))
    act = act.astype(BF)
    act_ref[...] = act
    total[...] += mm(act, wout_ref[...])
    du = (slope * mm_nt(dz_ref[...], wout_ref[...])).astype(BF)
    du_ref[...] = du
    back[...] += mm_nt(du, win_ref[...])

    @pl.when(chunk == pl.num_programs(0) - 1)
    def _():
        gate = gate_of()
        result = total[...]
        gated_ref[...] = (gate * result).astype(BF)
        dl = jnp.sum(dr_ref[...].astype(F32) * result, axis=1, keepdims=True) * gate * (1.0 - gate)
        dx_ref[...] = (back[...] + dl * centroid_ref[:1].astype(F32)).astype(BF)
        term_ref[...] = jnp.broadcast_to(jnp.sum(dl * x.astype(F32), axis=0, keepdims=True), term_ref.shape)


def expert_block(group, groups, arrived, grads, centroid, weights, earlier):
    slots, width = arrived.shape
    size = weights[2].shape[1]
    own = weights[0].shape[1] // size
    hidden = (own + 2) * size
    whole = pl.BlockSpec((slots, width), lambda j: (0, 0))
    shared = pl.BlockSpec((slots, width), lambda j: (group, 0))
    piece = pl.BlockSpec((slots, size), lambda j: (group, j))
    row = pl.BlockSpec((LANES, width), lambda j: (0, 0))
    term = pl.BlockSpec((8, width), lambda j: (0, 0))
    win_piece = pl.BlockSpec((width, size), lambda j: (0, 0))
    wout_piece = pl.BlockSpec((size, width), lambda j: (0, 0))
    return pl.pallas_call(
        expert_kernel,
        grid=(own + 2,),
        in_specs=[
            whole,
            whole,
            row,
            pl.BlockSpec((width, size), lambda j: (0, jnp.minimum(j, own - 1))),
            pl.BlockSpec((size, width), lambda j: (jnp.minimum(j, own - 1), 0)),
            win_piece,
            win_piece,
            wout_piece,
            wout_piece,
            *[pl.BlockSpec(memory_space=pl.ANY)] * len(earlier),
        ],
        out_specs=[piece, piece, shared, shared, whole, whole, term],
        out_shape=[jax.ShapeDtypeStruct((groups * slots, hidden), BF)] * 2
        + [jax.ShapeDtypeStruct((groups * slots, width), BF)] * 2
        + [jax.ShapeDtypeStruct((slots, width), BF)] * 2
        + [jax.ShapeDtypeStruct((8, width), F32)],
        scratch_shapes=[pltpu.VMEM((slots, width), F32)] * 2
        + [pltpu.VMEM((width, size), BF), pltpu.VMEM((size, width), BF)],
        input_output_aliases={9 + i: i for i in range(len(earlier))},
        compiler_params=pltpu.CompilerParams(vmem_limit_bytes=48 * 2**20),
        cost_estimate=pl.CostEstimate(flops=10**6, bytes_accessed=2**16, transcendentals=0),
    )(arrived, grads, jnp.broadcast_to(centroid[None], (LANES, width)), *weights, *earlier)


def gather_plan(seq_size, count):
    plan = [("send", 0), ("send", 1), ("own",)]
    for hop in range(1, seq_size):
        plan += [("proj", hop), ("arrive", 0, hop), ("arrive", 1, hop)]
        if hop == 1:
            plan += [("send", 2)]
        if hop < seq_size - 1:
            plan += [("go", hop - 1, 0)]
    last = seq_size - 1
    rest = [("go", 0, 1), ("go", last - 1, 0), ("go", 1, 1), ("go", last, 0)]
    rest += [("go", hop, step) for step in range(1, count - 1) for hop in range(2 if step == 1 else 0, seq_size)]
    plan += [("arrive", 2, 1), *rest[:4]]
    rest = rest[4:]
    share = -(-len(rest) // max(1, seq_size - 2))
    for hop in range(2, seq_size):
        plan += [("arrive", 2, hop), *rest[(hop - 2) * share : (hop - 1) * share]]
    return plan + [("go", hop, count - 1) for hop in range(seq_size)]


def gather_kernel(seq_size, bits, proj_ref, in_ref, out_ref, x_ref, proj_all, in_all, out_all, x_all, *sems):
    own_sem, proj_send, proj_recv, line_send, line_recv, cube_send, cube_recv = sems
    z = lax.axis_index("seq")
    f = lax.axis_index("fsdp")
    count = len(bits)
    high_first = sorted(bits, reverse=True)
    bit_of = {bit: (f // bit) % 2 for bit in bits}
    mesh_id = pl.DeviceIdType.MESH

    barrier = pltpu.get_barrier_semaphore()
    for step in range(1, seq_size):
        pl.semaphore_signal(barrier, inc=1, device_id={"seq": lax.rem(z + step, seq_size)}, device_id_type=mesh_id)
    for bit in bits:
        pl.semaphore_signal(barrier, inc=1, device_id={"fsdp": f + bit * (1 - 2 * bit_of[bit])}, device_id_type=mesh_id)
    pl.semaphore_wait(barrier, seq_size - 1 + count)

    def place(buffer, s, done=()):
        if buffer is x_all:
            return buffer.at[s]
        return buffer.at[(s, *(slice(None) if bit in done else bit_of[bit] for bit in high_first))]

    def order_of(index, turn):
        return bits if (index + turn) % 2 == 0 else bits[-2::-1] + bits[-1:]

    cubes = ((proj_all, 0), (in_all, 0), (out_all, 1))

    def cube(index, s, turn, step):
        buffer, crossed = cubes[index]
        order = order_of(crossed, turn if index == 0 else 0)
        view = place(buffer, s, order[:step])
        bit = order[step]
        return pltpu.make_async_remote_copy(
            src_ref=view,
            dst_ref=view,
            send_sem=cube_send.at[index, turn, step],
            recv_sem=cube_recv.at[index, turn, step],
            device_id={"fsdp": f + bit * (1 - 2 * bit_of[bit])},
            device_id_type=mesh_id,
        )

    lines = ((in_all, in_ref), (out_all, out_ref), (x_all, x_ref))

    def line(index, side, hop):
        buffer, own = lines[index]
        ahead = 1 - 2 * side
        s = z - ahead * (hop - 1)
        view = place(buffer, s)
        return pltpu.make_async_remote_copy(
            src_ref=own if hop == 1 else view,
            dst_ref=view,
            send_sem=line_send.at[index, side, hop - 1],
            recv_sem=line_recv.at[index, side, hop - 1],
            device_id={"seq": z + ahead},
            device_id_type=mesh_id,
        )

    def line_wait(index, side, hop):
        view = place(lines[index][0], z - (1 - 2 * side) * hop)
        pltpu.make_async_remote_copy(
            src_ref=view,
            dst_ref=view,
            send_sem=line_send.at[index, side, hop - 1],
            recv_sem=line_recv.at[index, side, hop - 1],
            device_id={"seq": z - (1 - 2 * side)},
            device_id_type=mesh_id,
        ).wait_recv()

    def has_next(side):
        return z < seq_size - 1 if side == 0 else z > 0

    def has_block(side, hop):
        return z - hop >= 0 if side == 0 else z + hop < seq_size

    def proj(step):
        to = lax.rem(z + step, seq_size)
        return pltpu.make_async_remote_copy(
            src_ref=proj_ref.at[to],
            dst_ref=place(proj_all, z),
            send_sem=proj_send.at[step - 1],
            recv_sem=proj_recv.at[step - 1],
            device_id={"seq": to},
            device_id_type=mesh_id,
        )

    def proj_wait(step):
        view = place(proj_all, lax.rem(z + seq_size - step, seq_size))
        pltpu.make_async_remote_copy(
            src_ref=view,
            dst_ref=view,
            send_sem=proj_send.at[step - 1],
            recv_sem=proj_recv.at[step - 1],
            device_id={"seq": lax.rem(z + step, seq_size)},
            device_id_type=mesh_id,
        ).wait_recv()

    def turn_of(side, hop):
        return 0 if hop == 0 else 2 * hop - 1 + side

    def each_block(hop, act):
        act(0, lax.rem(z + seq_size - hop, seq_size), turn_of(0, hop))
        for index in (1, 2):
            if hop == 0:
                act(index, z, 0)
                continue
            for side in (0, 1):

                @pl.when(has_block(side, hop))
                def _(index=index, side=side):
                    act(index, z - (1 - 2 * side) * hop, turn_of(side, hop))

    owns = [
        pltpu.make_async_copy(own, place(buffer, z), own_sem.at[i])
        for i, (own, buffer) in enumerate(((proj_ref.at[z], proj_all), (in_ref, in_all), (out_ref, out_all), (x_ref, x_all)))
    ]
    for copy in owns:
        copy.start()
    for step in range(1, seq_size):
        proj(step).start()
    def send_own(index):
        for side in (0, 1):

            @pl.when(has_next(side))
            def _(side=side):
                line(index, side, 1).start()

    def arrive(index, hop):
        for side in (0, 1):

            @pl.when(has_block(side, hop))
            def _(side=side):
                line_wait(index, side, hop)
                if hop < seq_size - 1:

                    @pl.when(has_next(side))
                    def _():
                        line(index, side, hop + 1).start()

                if index < 2:
                    cube(index + 1, z - (1 - 2 * side) * hop, turn_of(side, hop), 0).start()

    def go_on(hop, step):
        def act(index, s, turn):
            cube(index, s, turn, step).wait()
            if step + 1 < count:
                cube(index, s, turn, step + 1).start()

        each_block(hop, act)

    def proj_arrive(hop):
        proj_wait(hop)
        cube(0, lax.rem(z + seq_size - hop, seq_size), turn_of(0, hop), 0).start()

    def own_cubes():
        for copy in owns:
            copy.wait()
        each_block(0, lambda index, s, turn: cube(index, s, turn, 0).start())

    acts = {"send": send_own, "own": own_cubes, "proj": proj_arrive, "arrive": arrive, "go": go_on}
    for name, *values in gather_plan(seq_size, count):
        acts[name](*values)
    for step in range(1, seq_size):
        proj(step).wait_send()
    for index in range(3):
        for side in (0, 1):
            for hop in range(1, seq_size):

                @pl.when(has_next(side) & has_block(side, hop - 1))
                def _(index=index, side=side, hop=hop):
                    line(index, side, hop).wait_send()


def start_gathers(proj, ffn_in, ffn_out, tokens_in):
    seq_size, fsdp_size = lax.axis_size("seq"), lax.axis_size("fsdp")
    bits = fsdp_bits(False)
    count = len(bits)

    def whole(shard):
        return jax.ShapeDtypeStruct((seq_size, *[2] * count, *shard), BF)

    turns = 2 * seq_size - 1
    dma = pltpu.SemaphoreType.DMA
    anywhere = pl.BlockSpec(memory_space=pl.ANY)
    outs = pl.pallas_call(
        functools.partial(gather_kernel, seq_size, bits),
        in_specs=[pl.BlockSpec(memory_space=pltpu.VMEM)] * 4,
        out_specs=[anywhere] * 4,
        out_shape=[
            whole(proj.shape[1:]),
            whole(ffn_in.shape),
            whole(ffn_out.shape),
            jax.ShapeDtypeStruct((seq_size, *tokens_in.shape), BF),
        ],
        scratch_shapes=[
            dma((4,)),
            dma((seq_size - 1,)),
            dma((seq_size - 1,)),
            dma((3, 2, seq_size - 1)),
            dma((3, 2, seq_size - 1)),
            dma((3, turns, count)),
            dma((3, turns, count)),
        ],
        compiler_params=pltpu.CompilerParams(collective_id=0, has_side_effects=True),
        cost_estimate=pl.CostEstimate(flops=0, bytes_accessed=100 * 2**20, transcendentals=0),
    )(proj, ffn_in, ffn_out, tokens_in)
    proj_all, in_all, out_all, inputs_all = outs
    flat = (seq_size, fsdp_size)
    return (
        proj_all.reshape(*flat, *proj.shape[1:]),
        in_all.reshape(*flat, *ffn_in.shape),
        out_all.reshape(*flat, *ffn_out.shape),
        inputs_all,
    )


def copy_into(target, index, term, rows=64, add=False):
    depth = target.shape[-2]
    rows = next(n for n in (rows, 48, 32, 16, depth) if depth % n == 0)
    lead = target.shape[len(index) : -2]
    count = 1
    for size in lead:
        count *= size

    def step(i, carry):
        block, place = i // (depth // rows), pl.multiple_of((i % (depth // rows)) * rows, rows)
        where = []
        for size in reversed(lead):
            where.insert(0, block % size)
            block = block // size
        at = (*where, pl.ds(place, rows), slice(None))
        value = term(at).astype(target.dtype)
        target[(*index, *at)] = target[(*index, *at)] + value if add else value
        return carry

    lax.fori_loop(0, count * (depth // rows), step, 0)


def add_into(target, index, term):
    copy_into(target, index, term, add=True)


def finish_plan(seq_size, count):
    last = count - 1
    plan = [("send", 0), ("open",), ("arrive", 0, 1)]
    ffn = [("add", index, step) for step in range(1, count) for index in (0, 1)]
    for hop in range(2, seq_size):
        plan += [("arrive", 0, hop)]
        share = len(ffn) - 2 if hop == seq_size - 2 else 0
        plan += ffn[:share]
        ffn = ffn[share:]
        if hop == seq_size - 2:
            plan += [("add", 2, 0), ("add", 3, 0)]
    if seq_size == 2:
        plan += [("add", 2, 0), ("add", 3, 0)]
    for item in ffn:
        plan += [item] + ([("send", 1 + item[1])] if item[2] == last else [])
    rest = [("add", index, step) for step in range(1, count) for index in (2, 3)] + [("proj",)]
    for hop in range(1, seq_size):
        share = -(-len(rest) // (seq_size - hop))
        plan += [("arrive", 1, hop), ("arrive", 2, hop), *rest[:share]]
        rest = rest[share:]
    return plan + [("total", 0), ("total", 1), ("total", 2)]


def finish_kernel(seq_size, bits, da_ref, in_ref, in_added, out_ref, out_added, proj_ref, *refs):
    count = len(bits)
    da_out, in_out, out_out, proj_out = refs[:4]
    da_line, in_line, out_line = refs[4:7]
    in_parts, out_parts, proj_parts = (refs[7 + i * count : 7 + (i + 1) * count] for i in range(3))
    own_sem, keep_sem, line_send, line_recv, cube_send, cube_recv, proj_send, proj_recv = refs[7 + 3 * count :]
    z = lax.axis_index("seq")
    f = lax.axis_index("fsdp")
    bit_of = {bit: (f // bit) % 2 for bit in bits}
    mesh_id = pl.DeviceIdType.MESH
    last = seq_size - 1

    def flipped(bit):
        return {"fsdp": f + bit * (1 - 2 * bit_of[bit])}

    barrier = pltpu.get_barrier_semaphore()
    for step in range(1, seq_size):
        pl.semaphore_signal(barrier, inc=1, device_id={"seq": lax.rem(z + step, seq_size)}, device_id_type=mesh_id)
    for bit in bits:
        pl.semaphore_signal(barrier, inc=1, device_id=flipped(bit), device_id_type=mesh_id)
    pl.semaphore_wait(barrier, seq_size - 1 + count)

    lines = ((da_ref, da_line, da_out), (in_parts[-1], in_line, in_out), (out_parts[-1], out_line, out_out))

    def line(index, side, hop, own):
        terms, sums, _ = lines[index]
        if own:
            source = terms.at[seq_size - hop if side == 0 else hop - 1]
        else:
            source = sums.at[side, hop - 2]
        return pltpu.make_async_remote_copy(
            src_ref=source,
            dst_ref=sums.at[side, hop - 1],
            send_sem=line_send.at[index, side, hop - 1],
            recv_sem=line_recv.at[index, side, hop - 1],
            device_id={"seq": z + 1 - 2 * side},
            device_id_type=mesh_id,
        )

    def at_end(side):
        return z == 0 if side == 0 else z == last

    def from_end(side):
        return z if side == 0 else last - z

    def send_own(index):
        for side in (0, 1):

            @pl.when(at_end(side))
            def _(side=side):
                for hop in range(1, seq_size):
                    line(index, side, hop, True).start()

    def arrive(index, hop):
        terms, sums, _ = lines[index]
        for side in (0, 1):

            @pl.when((from_end(side) >= 1) & (from_end(side) <= hop))
            def _(side=side):
                pltpu.make_async_remote_copy(
                    src_ref=sums.at[side, hop - 1],
                    dst_ref=sums.at[side, hop - 1],
                    send_sem=line_send.at[index, side, hop - 1],
                    recv_sem=line_recv.at[index, side, hop - 1],
                    device_id={"seq": z - 1 + 2 * side},
                    device_id_type=mesh_id,
                ).wait_recv()
                if hop < last:
                    target = z - 1 + seq_size - hop if side == 0 else hop - last + z
                    add_into(sums, (side, hop - 1), lambda at: terms[(target, *at)])
                    line(index, side, hop + 1, False).start()

    def total(index):
        terms, sums, result = lines[index]
        add_first(result, lambda at: terms[(z, *at)])
        for side in (0, 1):

            @pl.when(from_end(side) >= 1)
            def _(side=side):
                add_into(result, (), lambda at: sums[(side, last - 1, *at)])

    def add_first(result, term):
        depth = result.shape[0]
        rows = next(n for n in (64, 32, 16, depth) if depth % n == 0)

        def step(i, carry):
            at = (pl.ds(pl.multiple_of(i * rows, rows), rows), slice(None))
            result[at] = term(at).astype(F32)
            return carry

        lax.fori_loop(0, depth // rows, step, 0)

    plain = bits[::-1]
    turned = plain[:1] + plain[:0:-1]
    some = seq_size // 2
    cubes = (
        ([in_ref, *in_parts], plain, None),
        ([out_ref, *out_parts], turned, None),
        ([proj_ref, *proj_parts], plain, 0),
        ([proj_ref, *proj_parts], turned, some),
    )

    def half_of(index, step, kept):
        states, order, _ = cubes[index]
        where = 1 + sorted(order[step:], reverse=True).index(order[step])
        return states[step], where, bit_of[order[step]] if kept else 1 - bit_of[order[step]]

    def rows_of(index):
        offset = cubes[index][2]
        return slice(None) if offset is None else pl.ds(offset, some)

    def cube(index, step):
        source, where, bit = half_of(index, step, False)
        states, order, _ = cubes[index]
        return pltpu.make_async_remote_copy(
            src_ref=source.at[(rows_of(index),) + (slice(None),) * (where - 1) + (bit,)],
            dst_ref=states[step + 1].at[rows_of(index)],
            send_sem=cube_send.at[index, step],
            recv_sem=cube_recv.at[index, step],
            device_id=flipped(order[step]),
            device_id_type=mesh_id,
        )

    def cube_add(index, step):
        source, where, bit = half_of(index, step, True)
        states, _, offset = cubes[index]
        cube(index, step).wait()
        for i in range(seq_size if offset is None else some):
            row = i + (offset or 0)
            add_into(states[step + 1], (row,), lambda at, row=row: source[(row, *at[: where - 1], bit, *at[where - 1 :])])
        if step + 1 < count:
            cube(index, step + 1).start()

    def keep(index):
        source, where, bit = half_of(index, 0, True)
        return pltpu.make_async_copy(
            source.at[(slice(None),) * where + (bit,)], cubes[index][0][1], keep_sem.at[index]
        )

    def open_cubes():
        for index in (2, 3):
            cube(index, 0).start()
        for index in (0, 1):
            keep(index).start()
        for index, added in ((0, in_added), (1, out_added)):
            keep(index).wait()
            for row in range(seq_size):
                add_into(cubes[index][0][1], (row,), lambda at, row=row: added[(row, *at)])
            cube(index, 1).start()

    def proj(step):
        to = lax.rem(z + step, seq_size)
        return pltpu.make_async_remote_copy(
            src_ref=proj_parts[-1].at[to],
            dst_ref=proj_out.at[z],
            send_sem=proj_send.at[step - 1],
            recv_sem=proj_recv.at[step - 1],
            device_id={"seq": to},
            device_id_type=mesh_id,
        )

    def proj_wait(step):
        view = proj_out.at[lax.rem(z + seq_size - step, seq_size)]
        copy = pltpu.make_async_remote_copy(
            src_ref=view,
            dst_ref=view,
            send_sem=proj_send.at[step - 1],
            recv_sem=proj_recv.at[step - 1],
            device_id={"seq": lax.rem(z + step, seq_size)},
            device_id_type=mesh_id,
        )
        copy.wait_recv()

    def proj_start():
        pltpu.make_async_copy(proj_parts[-1].at[z], proj_out.at[z], own_sem).start()
        for step in range(1, seq_size):
            proj(step).start()

    acts = {"send": send_own, "open": open_cubes, "add": cube_add, "arrive": arrive, "proj": proj_start, "total": total}
    for name, *values in finish_plan(seq_size, count):
        acts[name](*values)
    pltpu.make_async_copy(proj_parts[-1].at[z], proj_out.at[z], own_sem).wait()
    for step in range(1, seq_size):
        proj_wait(step)
        proj(step).wait_send()
    for index in range(3):
        for side in (0, 1):
            for hop in range(1, seq_size):

                @pl.when(at_end(side) | ((from_end(side) >= 1) & (from_end(side) <= hop - 1)))
                def _(index=index, side=side, hop=hop):
                    line(index, side, hop, True).wait_send()


def finish_sums(da, ffin, ffout, proj):
    seq_size = lax.axis_size("seq")
    bits = fsdp_bits(False)
    count = len(bits)
    dma = pltpu.SemaphoreType.DMA
    inside, anywhere = pl.BlockSpec(memory_space=pltpu.VMEM), pl.BlockSpec(memory_space=pl.ANY)
    shapes = [v.shape[-2:] for v in (da, ffin[0], ffout[0])]

    def parts_of(shape, first):
        return [pltpu.VMEM((seq_size, *[2] * (count - step), *shape), BF) for step in range(first, count + 1)]

    return pl.pallas_call(
        functools.partial(finish_kernel, seq_size, bits),
        in_specs=[inside, anywhere, inside, anywhere, inside, inside],
        out_specs=[inside] * 4,
        out_shape=[jax.ShapeDtypeStruct(shape, F32) for shape in shapes]
        + [jax.ShapeDtypeStruct((seq_size, *proj.shape[-2:]), BF)],
        scratch_shapes=[
            *[pltpu.VMEM((2, seq_size - 1, *shape), BF) for shape in shapes],
            *parts_of(shapes[1], 1),
            *parts_of(shapes[2], 1),
            *parts_of(proj.shape[-2:], 1),
            dma,
            dma((2,)),
            dma((3, 2, seq_size - 1)),
            dma((3, 2, seq_size - 1)),
            dma((4, count)),
            dma((4, count)),
            dma((seq_size - 1,)),
            dma((seq_size - 1,)),
        ],
        compiler_params=pltpu.CompilerParams(
            collective_id=1, has_side_effects=True, vmem_limit_bytes=56 * 2**20
        ),
        cost_estimate=pl.CostEstimate(flops=0, bytes_accessed=100 * 2**20, transcendentals=0),
    )(da, *ffin, *ffout, proj)


def whole_tiles(shard, rows=16):
    return shard if shard.shape[0] % rows == 0 else shard.reshape(rows, -1)


def on_device(
    inputs,
    qkv_proj,
    out_proj,
    ffn_in,
    ffn_out,
    norm_gains,
    norm_biases,
    centroids,
    expert_in,
    expert_out,
    doc_lengths,
    routes,
    out_grad,
):
    rows, span, width = inputs.shape
    tokens = rows * span
    seq_size, fsdp_size = lax.axis_size("seq"), lax.axis_size("fsdp")
    here = lax.axis_index("seq")
    length = span * seq_size
    cols = width // seq_size
    capacity = max(2, 3 * tokens // (2 * fsdp_size))
    groups = seq_size // 2

    docs = doc_lengths.shape[1]
    key_pos = jnp.arange(length, dtype=jnp.int32)
    doc_ids = jnp.zeros((rows, length), jnp.int32)
    doc_end = jnp.zeros((rows, 1), jnp.int32)
    for j in range(docs - 1):
        doc_end = doc_end + doc_lengths[:, j : j + 1]
        doc_ids = doc_ids + (key_pos[None, :] >= doc_end).astype(jnp.int32)
    id_rows, id_cols = doc_ids[:, None, :], doc_ids[:, :, None]

    depth = out_proj.shape[0]
    wide = 3 * cols + width
    slices = qkv_proj.reshape(3, depth, seq_size, cols).transpose(2, 1, 0, 3).reshape(seq_size, depth, 3 * cols)
    slices = jnp.concatenate([slices, jnp.broadcast_to(out_proj[None], (seq_size, depth, width))], axis=2)
    small = jnp.concatenate([norm_gains.reshape(-1), norm_biases.reshape(-1), centroids[0]])
    spare = 16 - depth % 16
    extra = jnp.stack([jnp.pad(v, (0, wide - v.shape[0])) for v in (small, routes.reshape(tokens).astype(BF))])
    extra = jnp.pad(extra, ((0, spare - 2), (0, 0)))[None]
    extra = jnp.broadcast_to(extra, (seq_size, spare, wide))
    bits = fsdp_bits(False)
    crossed = fsdp_bits(True)
    tokens_in = inputs.reshape(tokens, width)
    proj_all, ffin_all, ffout_all, inputs_all = start_gathers(
        jnp.concatenate([slices, extra], axis=1), whole_tiles(ffn_in), whole_tiles(ffn_out), tokens_in
    )
    inputs_all = inputs_all.reshape(seq_size * tokens, width)
    ffin_all, ffout_all = ffin_all.reshape(width, -1), ffout_all.reshape(-1, width)
    qkv_mine = proj_all[:, :, :depth, : 3 * cols].reshape(width, 3 * cols)
    out_all = proj_all[:, :, :depth, 3 * cols :].reshape(width, width)
    small = proj_all[:, :, depth, :]
    rows_of = small[:, :, : 6 * depth].astype(F32).reshape(-1, 6, depth).transpose(1, 0, 2).reshape(6, width)
    gain_rows, bias_rows = rows_of[:3], rows_of[3:]
    mine = small[:, :, 6 * depth : 6 * depth + cols]
    centroid = lax.dynamic_index_in_dim(mine, lax.axis_index("fsdp"), 1, keepdims=False).reshape(width)
    inputs_all, win_mine, wout_mine, dr_mine = tie(
        inputs_all, expert_in[0], expert_out[0], out_grad.reshape(tokens, width)
    )
    parts_all = norm_parts(inputs_all.astype(F32))
    normed_flat = ((inputs_all.astype(F32) - parts_all[0]) * parts_all[1] * gain_rows[0] + bias_rows[0]).astype(BF)
    projected = mm(normed_flat, qkv_mine).astype(BF).reshape(seq_size, rows, span, 3 * cols)

    attended_mine, lse_rows = attend(projected, id_rows, id_cols)
    win_half, wout_half = win_mine.shape[1] // 2, wout_mine.shape[0] // 2
    pair_in_low = seq_pair(win_mine[:, :win_half])
    grad_moved = [seq_shift(dr_mine, 2 * group) for group in range(1, groups)]
    attended_mine, pair_in_low, *grad_moved = tie(attended_mine, pair_in_low, *grad_moved)
    attended = seq_exchange(attended_mine).transpose(1, 2, 0, 3).reshape(tokens, width)
    attended, pair_in_high, pair_out_low, wout_high = tie(
        attended, win_mine[:, win_half:], wout_mine[:wout_half], wout_mine[wout_half:]
    )
    pair_in_high, pair_out_low = seq_pair(pair_in_high), seq_pair(pair_out_low)

    fsdp_here = lax.axis_index("fsdp")
    routes_all = lax.dynamic_index_in_dim(proj_all[:, :, depth + 1, :tokens], fsdp_here, 1, keepdims=False)
    later = (jnp.arange(tokens)[:, None] > jnp.arange(tokens)[None, :]).astype(BF)
    placings = []
    for group in range(groups):
        route = pick(routes_all, (here + seq_size - 2 * group) % seq_size).astype(jnp.int32)
        choose = route[:, None] == jnp.arange(fsdp_size, dtype=jnp.int32)[None, :]
        before = mm(later, choose.astype(BF))
        slot_rank = jnp.sum(jnp.where(choose, before, 0.0), axis=1).astype(jnp.int32)
        target = route * capacity + slot_rank
        slots = jnp.arange(fsdp_size * capacity, dtype=jnp.int32)
        placings.append((target[:, None] == slots[None, :]).astype(BF))
    grad_tokens = out_grad.reshape(tokens, width)

    def slots_of(placing, values):
        return mm_tn(placing, values).astype(BF).reshape(fsdp_size, capacity, width)

    def swap_slots(values):
        return lax.all_to_all(values, "fsdp", split_axis=0, concat_axis=0, tiled=True)

    def tokens_of(placing, values):
        return mm(placing, values.reshape(fsdp_size * capacity, width))

    grad_slots = [slots_of(placings[group], ([grad_tokens] + grad_moved)[group]) for group in range(groups)]
    grad_slots = swap_slots(jnp.concatenate(grad_slots, axis=1)).reshape(fsdp_size, groups, capacity, width)
    grad_slots = [grad_slots[:, group].reshape(-1, width) for group in range(groups)]


    resid_in = tokens_in.astype(F32)
    middle = resid_in + mm(attended, out_all)
    gains_pad, biases_pad = jnp.pad(gain_rows, ((0, 5), (0, 0))), jnp.pad(bias_rows, ((0, 5), (0, 0)))
    hidden_low, active_low, active_slope, block_out, routed = ffn_forward(
        middle, gains_pad, biases_pad, ffin_all, ffout_all
    )
    routed, wout_high, pair_in_high, pair_out_low, *grad_slots = tie(
        routed, wout_high, pair_in_high, pair_out_low, *grad_slots
    )
    slots_own = slots_of(placings[0], routed)
    pair_out_high = seq_pair(wout_high)

    arrived = [swap_slots(slots_own).reshape(-1, width)]
    for group in range(1, groups):
        routed_here = seq_shift(routed, 2 * group)
        routed_here, pair_out_high = tie(routed_here, pair_out_high)
        slots_here = slots_of(placings[group], routed_here)
        slots_here, pair_out_high, *arrived = tie(slots_here, pair_out_high, *arrived)
        arrived.append(swap_slots(slots_here).reshape(-1, width))
    weights = (win_mine, wout_mine, pair_in_low, pair_in_high, pair_out_low, pair_out_high)
    shared, gateds, rows_grads, terms = (), [], [], []
    for group in range(groups):
        *shared, gated, rows_grad, term = expert_block(
            group, groups, arrived[group], grad_slots[group], centroid, weights, shared
        )
        gateds.append(gated)
        rows_grads.append(rows_grad)
        terms.append(term)
    act, du, dz, arrived = shared

    half = expert_in.shape[2]
    in_sent = mm_tn(arrived, du[:, half:]).astype(BF)
    back_low = [None] * groups
    for group in reversed(range(groups)):
        rows_grad = rows_grads[group].reshape(fsdp_size, capacity, width)
        if group + 1 < groups:
            rows_grad, back_low[group + 1] = tie(rows_grad, back_low[group + 1])
        back_slots = swap_slots(rows_grad)
        if group + 1 == groups:
            back_slots, in_sent = tie(back_slots, in_sent)
        back_low[group] = tokens_of(placings[group], back_slots)
        if group:
            back_low[group] = back_low[group].astype(BF)
    in_pair = seq_pair(in_sent)
    gated_all = jnp.concatenate([gated.reshape(fsdp_size, capacity, width) for gated in gateds], axis=1)
    if groups > 1:
        gated_all, arrived, act, du, back_low[-1] = tie(gated_all, arrived, act, du, back_low[-1])
    back_sum = back_low[0]
    for group in range(1, groups):
        back_sum = back_sum + seq_shift(back_low[group], -2 * group).astype(F32)
    centroid_term = sum(term[0] for term in terms)
    out_sent = mm_tn(act[:, half:], dz).astype(BF)
    in_kept = mm_tn(arrived, du[:, :half])
    out_kept = mm_tn(act[:, :half], dz)

    gated_back = swap_slots(gated_all).reshape(fsdp_size, groups, capacity, width)
    out_terms = [tokens_of(placings[group], gated_back[:, group]) for group in range(groups)]
    back_sum, out_sent, in_kept, out_kept, *out_terms = tie(
        back_sum, out_sent, in_kept, out_kept, out_terms[0], *(v.astype(BF) for v in out_terms[1:])
    )

    block_low, hidden_grad, middle_grad, branch, dense_rows = ffn_backward(
        back_sum, block_out, grad_tokens, middle, gains_pad, active_slope, ffin_all, ffout_all
    )
    gain_three, bias_three, gain_two, bias_two = (dense_rows[i] for i in range(4))
    attended_grad = mm_nt(branch, out_all).astype(BF)
    attended_grad = attended_grad.reshape(rows, span, seq_size, cols).transpose(2, 0, 1, 3)
    attended_grad, in_pair, active_low, hidden_low, attended = tie(
        attended_grad, in_pair, active_low, hidden_low, attended
    )
    attended_grad = seq_exchange(attended_grad, True)

    def halved(term):
        terms = hyper_split(by_device(term))
        sent = lax.dynamic_index_in_dim(terms, 1 - fsdp_here % 2, terms.ndim - 3, keepdims=False)
        return terms, fsdp_flip(sent, 1)

    ffout_terms = halved(mm_tn(active_low, block_low))
    ffin_terms = halved(mm_tn(hidden_low, hidden_grad))
    proj_terms = mm_tn(attended, branch).astype(BF).reshape(seq_size, fsdp_size, depth, width)
    proj_terms = jnp.pad(proj_terms, ((0, 0), (0, 0), (0, spare), (3 * cols, 0)))
    def halves(values):
        return values[: values.shape[0] // 2], values[values.shape[0] // 2 :]

    out_halves = [halves(values) for values in [out_sent, *out_terms[1:]]]
    attended_grad, *out_first = tie(attended_grad, *[first for first, _ in out_halves])
    out_first = [seq_pair(out_first[0])] + [seq_shift(out_first[group], -2 * group) for group in range(1, groups)]

    dq, dk, dv = attend_back(projected, attended_grad, lse_rows, id_rows, id_cols)
    projected_grad = jnp.concatenate([dq, dk, dv], axis=-1).reshape(seq_size * tokens, 3 * cols)
    sizes = len(out_first)
    projected_grad, *moved = tie(projected_grad, *out_first, *[second for _, second in out_halves])
    out_first, out_second = moved[:sizes], moved[sizes:]
    out_second = [seq_pair(out_second[0])] + [seq_shift(out_second[group], -2 * group) for group in range(1, groups)]
    normed_low_terms = mm_nt(projected_grad, qkv_mine).astype(BF)
    unit_all = (inputs_all.astype(F32) - parts_all[0]) * parts_all[1]
    terms_wide = normed_low_terms.astype(F32)
    gain_one, bias_one = jnp.sum(terms_wide * unit_all, axis=0), jnp.sum(terms_wide, axis=0)
    small_terms = jnp.stack([gain_one, gain_two, gain_three, bias_one, bias_two, bias_three])

    qkv_term = mm_tn(normed_flat, projected_grad).astype(BF).reshape(seq_size, fsdp_size, depth, 3 * cols)
    small_rows = small_terms.astype(BF).reshape(6, seq_size, fsdp_size, depth).transpose(1, 2, 0, 3)
    small_rows = small_rows.reshape(seq_size, fsdp_size, 1, 6 * depth)
    small_rows = jnp.pad(small_rows, ((0, 0), (0, 0), (0, spare - 1), (0, wide - 6 * depth)))
    centroid_rows = jnp.where(
        (jnp.arange(fsdp_size) == fsdp_here)[None, :, None], centroid_term.reshape(seq_size, 1, cols), 0.0
    )
    small_rows = lax.dynamic_update_slice(small_rows, centroid_rows.astype(BF)[:, :, None], (0, 0, 1, 0))
    proj_terms = lax.dynamic_update_slice(proj_terms, qkv_term, (0, 0, 0, 0))
    proj_terms = hyper_split(lax.dynamic_update_slice(proj_terms, small_rows, (0, 0, depth, 0)))
    proj_terms, *out_second = tie(proj_terms, *out_second)
    out_pair, *out_moved = [jnp.concatenate(v, axis=0) for v in zip(out_first, out_second, strict=True)]
    outputs = block_out + out_terms[0] + sum(v.astype(F32) for v in out_moved)
    outputs = outputs.astype(BF).reshape(rows, span, width)
    normed_one_grad, ffn_in_grad, ffn_out_grad, proj_sums = finish_sums(
        normed_low_terms.reshape(seq_size, tokens, width), ffin_terms, ffout_terms, proj_terms
    )
    ffn_in_grad, ffn_out_grad = ffn_in_grad.reshape(ffn_in.shape), ffn_out_grad.reshape(ffn_out.shape)
    proj_sums = proj_sums.astype(F32)
    qkv_grad = proj_sums[:, :depth, : 3 * cols].reshape(seq_size, depth, 3, cols)
    qkv_grad = qkv_grad.transpose(2, 1, 0, 3).reshape(qkv_proj.shape)
    out_proj_grad = jnp.sum(proj_sums[:, :depth, 3 * cols :], axis=0)
    small_grad = jnp.sum(proj_sums[:, depth, : 6 * depth], axis=0).reshape(6, depth)
    centroids_grad = jnp.sum(proj_sums[:, depth + 1, :cols], axis=0)[None]

    expert_in_grad = (in_kept + in_pair.astype(F32))[None]
    expert_out_grad = (out_kept + out_pair.astype(F32))[None]

    input_norm_grad, _, _ = norm_back(resid_in, norm_parts(resid_in), gain_rows[0], normed_one_grad)
    input_grad = (middle_grad + input_norm_grad).reshape(rows, span, width)
    return (
        outputs,
        input_grad,
        qkv_grad,
        out_proj_grad,
        ffn_in_grad,
        ffn_out_grad,
        small_grad[:3],
        small_grad[3:],
        centroids_grad,
        expert_in_grad,
        expert_out_grad,
    )


def solution(mesh):
    dense = P(("seq", "fsdp"), None)
    placed = (
        P("fsdp", "seq", None),
        P(None, ("seq", "fsdp"), None),
        dense,
        dense,
        dense,
        P(None, ("seq", "fsdp")),
        P(None, ("seq", "fsdp")),
        P("fsdp", "seq"),
        P("fsdp", None, "seq"),
        P("fsdp", "seq", None),
        P("fsdp", None),
        P("seq", "fsdp", None, None),
        P("fsdp", "seq", None),
    )
    returned = (
        P("fsdp", "seq", None),
        P("fsdp", "seq", None),
        P(None, ("seq", "fsdp"), None),
        dense,
        dense,
        dense,
        P(None, ("seq", "fsdp")),
        P(None, ("seq", "fsdp")),
        P("fsdp", "seq"),
        P("fsdp", None, "seq"),
        P("fsdp", "seq", None),
    )
    return jax.shard_map(on_device, mesh=mesh, in_specs=placed, out_specs=returned, check_vma=False)
```

```python
import functools

import jax
import jax.numpy as jnp
from jax import lax
from jax.experimental import pallas as pl
from jax.experimental.pallas import tpu as pltpu
from jax.sharding import PartitionSpec as P

HEAD_DIM = 64
LANES = 128
norm_eps = 1e-05
BF = jnp.bfloat16
F32 = jnp.float32


def layer_norm(values, gain_row, shift_row):
    average = jnp.mean(values, axis=-1, keepdims=True)
    centered = values - average
    variance = jnp.mean(centered * centered, axis=-1, keepdims=True)
    return centered * lax.rsqrt(variance + norm_eps) * gain_row + shift_row


def gelu_pair(values):
    cdf = 0.5 * (1.0 + lax.erf(values * (0.5**0.5)))
    pdf = 0.3989422804014327 * jnp.exp(-0.5 * values * values)
    return values * cdf, cdf + values * pdf


def mm(left, right):
    return jnp.dot(left, right, preferred_element_type=F32)


def mm_nt(left, right):
    return lax.dot_general(left, right, (((1,), (1,)), ((), ())), preferred_element_type=F32)


def mm_tn(left, right):
    return lax.dot_general(left, right, (((0,), (0,)), ((), ())), preferred_element_type=F32)


def norm_parts(values):
    average = jnp.mean(values, axis=-1, keepdims=True)
    centered = values - average
    variance = jnp.mean(centered * centered, axis=-1, keepdims=True)
    return average, lax.rsqrt(variance + norm_eps)


def norm_back(values, parts, gain_row, grads):
    average, scale = parts
    unit = (values - average) * scale
    unit_grad = grads * gain_row
    first = jnp.mean(unit_grad, axis=-1, keepdims=True)
    second = jnp.mean(unit_grad * unit, axis=-1, keepdims=True)
    return scale * (unit_grad - first - unit * second), jnp.sum(grads * unit, axis=0), jnp.sum(grads, axis=0)


def tie(*values):
    return lax.optimization_barrier(values)


def seq_shift(values, step):
    size = lax.axis_size("seq")
    return lax.ppermute(values, "seq", [(i, (i + step) % size) for i in range(size)])


def seq_pair(values):
    size = lax.axis_size("seq")
    return lax.ppermute(values, "seq", [(i, i ^ 1) for i in range(size)])


def put(buffer, values, place):
    return lax.dynamic_update_index_in_dim(buffer, values, place, 0)


def pick(values, place):
    return lax.dynamic_index_in_dim(values, place, 0, keepdims=False)


def seq_exchange(values, chained=False):
    size = lax.axis_size("seq")
    here = lax.axis_index("seq")
    result = put(jnp.zeros_like(values), pick(values, here), here)
    arrived = None
    for step in range(1, size):
        sent = pick(values, (here + step) % size)
        if chained and arrived is not None:
            sent, arrived = tie(sent, arrived)
        if arrived is not None:
            result = put(result, arrived, (here - step + 1) % size)
        arrived = seq_shift(sent, step)
    return put(result, arrived, (here - size + 1) % size)


def seq_sum_scatter(values):
    size = lax.axis_size("seq")
    here = lax.axis_index("seq")
    total = pick(values, here).astype(F32)
    for step in range(1, size):
        arrived = seq_shift(pick(values, (here + step) % size).astype(BF), step)
        total = total + arrived.astype(F32)
    return total


def masked_pair(block):
    lane = lax.broadcasted_iota(jnp.int32, block.shape, 1)
    zero = jnp.zeros_like(block)
    return jnp.where(lane < HEAD_DIM, block, zero), jnp.where(lane < HEAD_DIM, zero, block)


def allowed_block(id_col, id_row, start, size, end):
    key_pos = lax.broadcasted_iota(jnp.int32, (end, size), 0)
    query_pos = start + lax.broadcasted_iota(jnp.int32, (end, size), 1)
    return (id_col[:end, :] == id_row[:, start:end]) & (key_pos <= query_pos)


def attend_kernel(size, q_ref, k_ref, v_ref, id_row_ref, id_col_ref, o_ref, lse_ref, o_all):
    length = id_row_ref.shape[-1]
    queries = q_ref[...].reshape(length, LANES) * jnp.asarray(HEAD_DIM**-0.5, BF)
    keys = k_ref[...].reshape(length, LANES)
    values_t = v_ref[...].reshape(length, LANES).T
    id_row = id_row_ref[0]
    id_col = id_col_ref[0]
    for start in range(0, length, size):
        end = start + size
        mask = allowed_block(id_col, id_row, start, size, end)
        parts = []
        for head, query in enumerate(masked_pair(queries[start:end])):
            scores = jnp.where(mask, mm_nt(keys[:end], query), -1e30)
            top = jnp.max(scores, axis=0, keepdims=True)
            powers = jnp.exp(scores - top)
            whole = jnp.sum(powers, axis=0, keepdims=True)
            weights = (powers * (1.0 / whole)).astype(BF)
            lse_ref[0, 0, pl.ds(head, 1), pl.ds(start, size)] = top + jnp.log(whole)
            part = values_t[head * HEAD_DIM : (head + 1) * HEAD_DIM, :end]
            parts.append(mm(part, weights))
        o_all[pl.ds(start, size), :] = jnp.concatenate(parts, axis=0).T
    o_ref[...] = o_all[...].astype(BF).reshape(o_ref.shape)


def attend_back_kernel(
    size, q_ref, k_ref, v_ref, do_ref, lse_ref, id_row_ref, id_col_ref, dq_ref, dk_ref, dv_ref, dq_all, dk_all, dv_all
):
    length = id_row_ref.shape[-1]
    scale = HEAD_DIM**-0.5
    queries = q_ref[...].reshape(length, LANES) * jnp.asarray(scale, BF)
    keys = k_ref[...].reshape(length, LANES)
    keys_t = keys.T
    values = v_ref[...].reshape(length, LANES)
    grads = do_ref[...].reshape(length, LANES)
    id_row = id_row_ref[0]
    id_col = id_col_ref[0]
    dk_all[...] = jnp.zeros_like(dk_all)
    dv_all[...] = jnp.zeros_like(dv_all)
    for start in range(0, length, size):
        end = start + size
        mask = allowed_block(id_col, id_row, start, size, end)
        parts = []
        heads = zip(masked_pair(queries[start:end]), masked_pair(grads[start:end]), strict=True)
        for head, (query, grad) in enumerate(heads):
            scores = jnp.where(mask, mm_nt(keys[:end], query), -1e30)
            probs = jnp.exp(scores - lse_ref[0, 0, pl.ds(head, 1), pl.ds(start, size)])
            prob_grad = mm_nt(values[:end], grad)
            total = jnp.sum(probs * prob_grad, axis=0, keepdims=True)
            score_grad = (probs * (prob_grad - total)).astype(BF)
            dv_all[pl.ds(0, end), :] += mm(probs.astype(BF), grad)
            dk_all[pl.ds(0, end), :] += mm(score_grad, query)
            parts.append(mm(keys_t[head * HEAD_DIM : (head + 1) * HEAD_DIM, :end], score_grad))
        dq_all[pl.ds(start, size), :] = jnp.concatenate(parts, axis=0).T * scale
    dq_ref[...] = dq_all[...].astype(BF).reshape(dq_ref.shape)
    dk_ref[...] = dk_all[...].astype(BF).reshape(dk_ref.shape)
    dv_ref[...] = dv_all[...].astype(BF).reshape(dv_ref.shape)


def attention_specs(projected, length):
    blocks, rows, span, width3 = projected.shape
    columns = width3 // 3 // LANES

    def part(index):
        return pl.BlockSpec((blocks, 1, span, LANES), lambda r, c: (0, r, 0, index * columns + c))

    id_row = pl.BlockSpec((1, 1, length), lambda r, c: (r, 0, 0))
    id_col = pl.BlockSpec((1, length, 1), lambda r, c: (r, 0, 0))
    lse = pl.BlockSpec((1, 1, 2, length), lambda r, c: (r, c, 0, 0))
    return rows, columns, part, id_row, id_col, lse


def attend(projected, id_rows, id_cols):
    length = id_rows.shape[-1]
    blocks, rows, span, width3 = projected.shape
    rows, columns, part, id_row, id_col, lse = attention_specs(projected, length)
    return pl.pallas_call(
        functools.partial(attend_kernel, min(256, length)),
        grid=(rows, columns),
        in_specs=[part(0), part(1), part(2), id_row, id_col],
        out_specs=[part(0), lse],
        out_shape=[
            jax.ShapeDtypeStruct((blocks, rows, span, width3 // 3), BF),
            jax.ShapeDtypeStruct((rows, columns, 2, length), F32),
        ],
        scratch_shapes=[pltpu.VMEM((length, LANES), F32)],
        compiler_params=pltpu.CompilerParams(vmem_limit_bytes=40 * 2**20),
        cost_estimate=pl.CostEstimate(flops=10**6, bytes_accessed=2**16, transcendentals=0),
    )(projected, projected, projected, id_rows, id_cols)


def attend_back(projected, grads, lse_rows, id_rows, id_cols):
    length = id_rows.shape[-1]
    blocks, rows, span, width3 = projected.shape
    rows, columns, part, id_row, id_col, lse = attention_specs(projected, length)
    shape = jax.ShapeDtypeStruct((blocks, rows, span, width3 // 3), BF)
    return pl.pallas_call(
        functools.partial(attend_back_kernel, min(256, length)),
        grid=(rows, columns),
        in_specs=[part(0), part(1), part(2), part(0), lse, id_row, id_col],
        out_specs=[part(0)] * 3,
        out_shape=[shape] * 3,
        scratch_shapes=[pltpu.VMEM((length, LANES), F32)] * 3,
        compiler_params=pltpu.CompilerParams(vmem_limit_bytes=48 * 2**20),
        cost_estimate=pl.CostEstimate(flops=10**6, bytes_accessed=2**16, transcendentals=0),
    )(projected, projected, projected, grads, lse_rows, id_rows, id_cols)


def fsdp_flip(values, bit):
    size = lax.axis_size("fsdp")
    return lax.ppermute(values, "fsdp", [(i, i ^ bit) for i in range(size)])


def fsdp_bits(crossed):
    bits = [1 << i for i in range(1, lax.axis_size("fsdp").bit_length() - 1)]
    return (bits[::-1] if crossed else bits) + [1]


def hyper_split(parts):
    count = parts.shape[1].bit_length() - 1
    return parts.reshape(parts.shape[0], *[2] * count, *parts.shape[2:])


def by_device(term):
    seq_size, fsdp_size = lax.axis_size("seq"), lax.axis_size("fsdp")
    depth = term.shape[0] // (seq_size * fsdp_size)
    tile = (depth, term.shape[1]) if depth % 16 == 0 else (16, depth * term.shape[1] // 16)
    return term.astype(BF).reshape(seq_size, fsdp_size, *tile)


def project_kernel(x_ref, gains_ref, biases_ref, w_ref, normed_ref, out_ref):
    x = x_ref[...].astype(F32)
    average, scale = norm_parts(x)
    normed = ((x - average) * scale * gains_ref[0:1] + biases_ref[0:1]).astype(BF)
    normed_ref[...] = normed
    out_ref[...] = mm(normed, w_ref[...].reshape(x.shape[1], w_ref.shape[-1])).astype(BF)


def project(inputs_all, gains, biases, weights, columns, tokens):
    width = inputs_all.shape[1]
    row = pl.BlockSpec((8, width), lambda i: (0, 0))
    return pl.pallas_call(
        project_kernel,
        grid=(inputs_all.shape[0] // tokens,),
        in_specs=[
            pl.BlockSpec((tokens, width), lambda i: (i, 0)),
            row,
            row,
            pl.BlockSpec((*weights.shape[:3], columns), lambda i: (0, 0, 0, 0)),
        ],
        out_specs=[pl.BlockSpec((tokens, width), lambda i: (i, 0)), pl.BlockSpec((tokens, columns), lambda i: (i, 0))],
        out_shape=[
            jax.ShapeDtypeStruct(inputs_all.shape, BF),
            jax.ShapeDtypeStruct((inputs_all.shape[0], columns), BF),
        ],
        compiler_params=pltpu.CompilerParams(vmem_limit_bytes=40 * 2**20),
        cost_estimate=pl.CostEstimate(flops=10**6, bytes_accessed=2**16, transcendentals=0),
    )(inputs_all, gains, biases, weights)


def ffn_kernel(middle_ref, gains_ref, biases_ref, win_ref, wout_ref, normed_ref, act_ref, slope_ref, block_ref, routed_ref):
    chunk = pl.program_id(0)

    def norm(values, row):
        average, scale = norm_parts(values)
        return ((values - average) * scale * gains_ref[row : row + 1] + biases_ref[row : row + 1]).astype(BF)

    @pl.when(chunk == 0)
    def _():
        normed_ref[...] = norm(middle_ref[...], 1)
        block_ref[...] = middle_ref[...]

    act, slope = gelu_pair(mm(normed_ref[...], win_ref[...]))
    act = act.astype(BF)
    act_ref[...] = act
    slope_ref[...] = slope.astype(BF)
    block_ref[...] += mm(act, wout_ref[...])

    @pl.when(chunk == pl.num_programs(0) - 1)
    def _():
        routed_ref[...] = norm(block_ref[...], 2)


def ffn_specs(tokens, width, hidden):
    size = min(512, hidden)
    whole = pl.BlockSpec((tokens, width), lambda j: (0, 0))
    piece = pl.BlockSpec((tokens, size), lambda j: (0, j))
    row = pl.BlockSpec((8, width), lambda j: (0, 0))
    return size, whole, piece, row, [
        pl.BlockSpec((width, size), lambda j: (0, j)),
        pl.BlockSpec((size, width), lambda j: (j, 0)),
    ]


def ffn_forward(middle, gains, biases, win, wout):
    tokens, width = middle.shape
    hidden = win.shape[1]
    size, whole, piece, row, weights = ffn_specs(tokens, width, hidden)
    low, wide = jax.ShapeDtypeStruct((tokens, width), BF), jax.ShapeDtypeStruct((tokens, hidden), BF)
    return pl.pallas_call(
        ffn_kernel,
        grid=(hidden // size,),
        in_specs=[whole, row, row, *weights],
        out_specs=[whole, piece, piece, whole, whole],
        out_shape=[low, wide, wide, jax.ShapeDtypeStruct((tokens, width), F32), low],
        compiler_params=pltpu.CompilerParams(vmem_limit_bytes=48 * 2**20),
        cost_estimate=pl.CostEstimate(flops=10**6, bytes_accessed=2**16, transcendentals=0),
    )(middle, gains, biases, win, wout)


def ffn_back_kernel(
    back_ref, block_ref, grad_ref, middle_ref, gains_ref, slope_ref, win_ref, wout_ref,
    low_ref, du_ref, dh_ref, branch_ref, terms_ref, total,
):
    chunk = pl.program_id(0)

    def norm_grad(values, row, grads):
        moved, gain, bias = norm_back(values, norm_parts(values), gains_ref[row : row + 1], grads)
        return moved, gain[None], bias[None]

    @pl.when(chunk == 0)
    def _():
        moved, gain, bias = norm_grad(block_ref[...], 2, back_ref[...])
        grads = grad_ref[...].astype(F32) + moved
        dh_ref[...] = grads
        low_ref[...] = grads.astype(BF)
        terms_ref[0:1] = gain
        terms_ref[1:2] = bias
        total[...] = jnp.zeros_like(total)

    du = (slope_ref[...].astype(F32) * mm_nt(low_ref[...], wout_ref[...])).astype(BF)
    du_ref[...] = du
    total[...] += mm_nt(du, win_ref[...])

    @pl.when(chunk == pl.num_programs(0) - 1)
    def _():
        moved, gain, bias = norm_grad(middle_ref[...], 1, total[...])
        grads = dh_ref[...] + moved
        dh_ref[...] = grads
        branch_ref[...] = grads.astype(BF)
        terms_ref[2:3] = gain
        terms_ref[3:4] = bias


def ffn_backward(back, block_out, grads, middle, gains, slope, win, wout):
    tokens, width = middle.shape
    hidden = win.shape[1]
    size, whole, piece, row, weights = ffn_specs(tokens, width, hidden)
    low, wide = jax.ShapeDtypeStruct((tokens, width), BF), jax.ShapeDtypeStruct((tokens, hidden), BF)
    f32 = jax.ShapeDtypeStruct((tokens, width), F32)
    return pl.pallas_call(
        ffn_back_kernel,
        grid=(hidden // size,),
        in_specs=[whole, whole, whole, whole, row, piece, *weights],
        out_specs=[whole, piece, whole, whole, row],
        out_shape=[low, wide, f32, low, jax.ShapeDtypeStruct((8, width), F32)],
        scratch_shapes=[pltpu.VMEM((tokens, width), F32)],
        compiler_params=pltpu.CompilerParams(vmem_limit_bytes=48 * 2**20),
        cost_estimate=pl.CostEstimate(flops=10**6, bytes_accessed=2**16, transcendentals=0),
    )(back, block_out, grads, middle, gains, slope, win, wout)


def expert_kernel(x_ref, dr_ref, centroid_ref, win_own, wout_own, win_low, win_high, wout_low, wout_high, *refs):
    act_ref, du_ref, dz_ref, all_ref, gated_ref, dx_ref, term_ref, total, back, win_ref, wout_ref = refs[-11:]
    groups_of = gated_ref.shape
    chunk = pl.program_id(0)
    own = pl.num_programs(0) - 2
    for here, win_part, wout_part in (
        (chunk < own, win_own, wout_own),
        (chunk == own, win_low, wout_low),
        (chunk == own + 1, win_high, wout_high),
    ):

        @pl.when(here)
        def _(win_part=win_part, wout_part=wout_part):
            win_ref[...] = win_part[...]
            wout_ref[...] = wout_part[...]

    x = x_ref[...]

    def gate_of():
        logits = mm_nt(x, centroid_ref[...])[:, :1]
        return 1.0 / (1.0 + jnp.exp(-logits))

    @pl.when(chunk == 0)
    def _():
        dz_ref[...] = (gate_of() * dr_ref[...].astype(F32)).astype(BF)
        all_ref[...] = x
        total[...] = jnp.zeros_like(total)
        back[...] = jnp.zeros_like(back)

    act, slope = gelu_pair(mm(x, win_ref[...]))
    act = act.astype(BF)
    act_ref[...] = act
    total[...] += mm(act, wout_ref[...])
    du = (slope * mm_nt(dz_ref[...], wout_ref[...])).astype(BF)
    du_ref[...] = du
    back[...] += mm_nt(du, win_ref[...])

    @pl.when(chunk == pl.num_programs(0) - 1)
    def _():
        gate = gate_of()
        result = total[...]
        gated_ref[...] = (gate * result).astype(BF).reshape(groups_of)
        dl = jnp.sum(dr_ref[...].astype(F32) * result, axis=1, keepdims=True) * gate * (1.0 - gate)
        dx_ref[...] = (back[...] + dl * centroid_ref[:1].astype(F32)).astype(BF)
        term_ref[...] = jnp.broadcast_to(jnp.sum(dl * x.astype(F32), axis=0, keepdims=True), term_ref.shape)


def expert_block(group, groups, blocks, arrived, grads, centroid, weights, earlier):
    slots, width = arrived.shape
    size = weights[2].shape[1]
    own = weights[0].shape[1] // size
    hidden = (own + 2) * size
    whole = pl.BlockSpec((slots, width), lambda j: (0, 0))
    shared = pl.BlockSpec((slots, width), lambda j: (group, 0))
    piece = pl.BlockSpec((slots, size), lambda j: (group, j))
    row = pl.BlockSpec((LANES, width), lambda j: (0, 0))
    term = pl.BlockSpec((8, width), lambda j: (0, 0))
    win_piece = pl.BlockSpec((width, size), lambda j: (0, 0))
    wout_piece = pl.BlockSpec((size, width), lambda j: (0, 0))
    return pl.pallas_call(
        expert_kernel,
        grid=(own + 2,),
        in_specs=[
            whole,
            whole,
            row,
            pl.BlockSpec((width, size), lambda j: (0, jnp.minimum(j, own - 1))),
            pl.BlockSpec((size, width), lambda j: (jnp.minimum(j, own - 1), 0)),
            win_piece,
            win_piece,
            wout_piece,
            wout_piece,
            *[pl.BlockSpec(memory_space=pl.ANY)] * len(earlier),
        ],
        out_specs=[
            piece,
            piece,
            shared,
            shared,
            pl.BlockSpec((blocks, slots // blocks, width), lambda j: (0, group, 0)),
            whole,
            term,
        ],
        out_shape=[jax.ShapeDtypeStruct((groups * slots, hidden), BF)] * 2
        + [jax.ShapeDtypeStruct((groups * slots, width), BF)] * 2
        + [jax.ShapeDtypeStruct((blocks, groups * slots // blocks, width), BF)]
        + [jax.ShapeDtypeStruct((slots, width), BF)]
        + [jax.ShapeDtypeStruct((8, width), F32)],
        scratch_shapes=[pltpu.VMEM((slots, width), F32)] * 2
        + [pltpu.VMEM((width, size), BF), pltpu.VMEM((size, width), BF)],
        input_output_aliases={9 + i: i for i in range(len(earlier))},
        compiler_params=pltpu.CompilerParams(vmem_limit_bytes=48 * 2**20),
        cost_estimate=pl.CostEstimate(flops=10**6, bytes_accessed=2**16, transcendentals=0),
    )(arrived, grads, jnp.broadcast_to(centroid[None], (LANES, width)), *weights, *earlier)


def gather_plan(seq_size, count):
    plan = [("send", 0), ("send", 1), ("own",)]
    for hop in range(1, seq_size):
        plan += [("proj", hop), ("arrive", 0, hop), ("arrive", 1, hop)]
        if hop == 1:
            plan += [("send", 2)]
        if hop < seq_size - 1:
            plan += [("go", hop - 1, 0)]
    last = seq_size - 1
    rest = [("go", 0, 1), ("go", last - 1, 0), ("go", 1, 1), ("go", last, 0)]
    rest += [("go", hop, step) for step in range(1, count - 1) for hop in range(2 if step == 1 else 0, seq_size)]
    plan += [("arrive", 2, 1), *rest[:4]]
    rest = rest[4:]
    share = -(-len(rest) // max(1, seq_size - 2))
    for hop in range(2, seq_size):
        plan += [("arrive", 2, hop), *rest[(hop - 2) * share : (hop - 1) * share]]
    return plan + [("go", hop, count - 1) for hop in range(seq_size)]


def gather_kernel(seq_size, bits, proj_ref, in_ref, out_ref, x_ref, proj_all, in_all, out_all, x_all, *sems):
    own_sem, proj_send, proj_recv, line_send, line_recv, cube_send, cube_recv = sems
    z = lax.axis_index("seq")
    f = lax.axis_index("fsdp")
    count = len(bits)
    high_first = sorted(bits, reverse=True)
    bit_of = {bit: (f // bit) % 2 for bit in bits}
    mesh_id = pl.DeviceIdType.MESH

    barrier = pltpu.get_barrier_semaphore()
    for step in range(1, seq_size):
        pl.semaphore_signal(barrier, inc=1, device_id={"seq": lax.rem(z + step, seq_size)}, device_id_type=mesh_id)
    for bit in bits:
        pl.semaphore_signal(barrier, inc=1, device_id={"fsdp": f + bit * (1 - 2 * bit_of[bit])}, device_id_type=mesh_id)
    pl.semaphore_wait(barrier, seq_size - 1 + count)

    def place(buffer, s, done=()):
        if buffer is x_all:
            return buffer.at[s]
        return buffer.at[(s, *(slice(None) if bit in done else bit_of[bit] for bit in high_first))]

    def order_of(index, turn):
        return bits if (index + turn) % 2 == 0 else bits[-2::-1] + bits[-1:]

    cubes = ((proj_all, 0), (in_all, 0), (out_all, 1))

    def cube(index, s, turn, step):
        buffer, crossed = cubes[index]
        order = order_of(crossed, turn if index == 0 else 0)
        view = place(buffer, s, order[:step])
        bit = order[step]
        return pltpu.make_async_remote_copy(
            src_ref=view,
            dst_ref=view,
            send_sem=cube_send.at[index, turn, step],
            recv_sem=cube_recv.at[index, turn, step],
            device_id={"fsdp": f + bit * (1 - 2 * bit_of[bit])},
            device_id_type=mesh_id,
        )

    lines = ((in_all, in_ref), (out_all, out_ref), (x_all, x_ref))

    def line(index, side, hop):
        buffer, own = lines[index]
        ahead = 1 - 2 * side
        s = z - ahead * (hop - 1)
        view = place(buffer, s)
        return pltpu.make_async_remote_copy(
            src_ref=own if hop == 1 else view,
            dst_ref=view,
            send_sem=line_send.at[index, side, hop - 1],
            recv_sem=line_recv.at[index, side, hop - 1],
            device_id={"seq": z + ahead},
            device_id_type=mesh_id,
        )

    def line_wait(index, side, hop):
        view = place(lines[index][0], z - (1 - 2 * side) * hop)
        pltpu.make_async_remote_copy(
            src_ref=view,
            dst_ref=view,
            send_sem=line_send.at[index, side, hop - 1],
            recv_sem=line_recv.at[index, side, hop - 1],
            device_id={"seq": z - (1 - 2 * side)},
            device_id_type=mesh_id,
        ).wait_recv()

    def has_next(side):
        return z < seq_size - 1 if side == 0 else z > 0

    def has_block(side, hop):
        return z - hop >= 0 if side == 0 else z + hop < seq_size

    def proj(step):
        to = lax.rem(z + step, seq_size)
        return pltpu.make_async_remote_copy(
            src_ref=proj_ref.at[to],
            dst_ref=place(proj_all, z),
            send_sem=proj_send.at[step - 1],
            recv_sem=proj_recv.at[step - 1],
            device_id={"seq": to},
            device_id_type=mesh_id,
        )

    def proj_wait(step):
        view = place(proj_all, lax.rem(z + seq_size - step, seq_size))
        pltpu.make_async_remote_copy(
            src_ref=view,
            dst_ref=view,
            send_sem=proj_send.at[step - 1],
            recv_sem=proj_recv.at[step - 1],
            device_id={"seq": lax.rem(z + step, seq_size)},
            device_id_type=mesh_id,
        ).wait_recv()

    def turn_of(side, hop):
        return 0 if hop == 0 else 2 * hop - 1 + side

    def each_block(hop, act):
        act(0, lax.rem(z + seq_size - hop, seq_size), turn_of(0, hop))
        for index in (1, 2):
            if hop == 0:
                act(index, z, 0)
                continue
            for side in (0, 1):

                @pl.when(has_block(side, hop))
                def _(index=index, side=side):
                    act(index, z - (1 - 2 * side) * hop, turn_of(side, hop))

    owns = [
        pltpu.make_async_copy(own, place(buffer, z), own_sem.at[i])
        for i, (own, buffer) in enumerate(((proj_ref.at[z], proj_all), (in_ref, in_all), (out_ref, out_all), (x_ref, x_all)))
    ]
    for copy in owns:
        copy.start()
    for step in range(1, seq_size):
        proj(step).start()
    def send_own(index):
        for side in (0, 1):

            @pl.when(has_next(side))
            def _(side=side):
                line(index, side, 1).start()

    def arrive(index, hop):
        for side in (0, 1):

            @pl.when(has_block(side, hop))
            def _(side=side):
                line_wait(index, side, hop)
                if hop < seq_size - 1:

                    @pl.when(has_next(side))
                    def _():
                        line(index, side, hop + 1).start()

                if index < 2:
                    cube(index + 1, z - (1 - 2 * side) * hop, turn_of(side, hop), 0).start()

    def go_on(hop, step):
        def act(index, s, turn):
            cube(index, s, turn, step).wait()
            if step + 1 < count:
                cube(index, s, turn, step + 1).start()

        each_block(hop, act)

    def proj_arrive(hop):
        proj_wait(hop)
        cube(0, lax.rem(z + seq_size - hop, seq_size), turn_of(0, hop), 0).start()

    def own_cubes():
        for copy in owns:
            copy.wait()
        each_block(0, lambda index, s, turn: cube(index, s, turn, 0).start())

    acts = {"send": send_own, "own": own_cubes, "proj": proj_arrive, "arrive": arrive, "go": go_on}
    for name, *values in gather_plan(seq_size, count):
        acts[name](*values)
    for step in range(1, seq_size):
        proj(step).wait_send()
    for index in range(3):
        for side in (0, 1):
            for hop in range(1, seq_size):

                @pl.when(has_next(side) & has_block(side, hop - 1))
                def _(index=index, side=side, hop=hop):
                    line(index, side, hop).wait_send()


def start_gathers(proj, ffn_in, ffn_out, tokens_in):
    seq_size, fsdp_size = lax.axis_size("seq"), lax.axis_size("fsdp")
    bits = fsdp_bits(False)
    count = len(bits)

    def whole(shard):
        return jax.ShapeDtypeStruct((seq_size, *[2] * count, *shard), BF)

    turns = 2 * seq_size - 1
    dma = pltpu.SemaphoreType.DMA
    anywhere = pl.BlockSpec(memory_space=pl.ANY)
    outs = pl.pallas_call(
        functools.partial(gather_kernel, seq_size, bits),
        in_specs=[pl.BlockSpec(memory_space=pltpu.VMEM)] * 4,
        out_specs=[anywhere] * 4,
        out_shape=[
            whole(proj.shape[1:]),
            whole(ffn_in.shape),
            whole(ffn_out.shape),
            jax.ShapeDtypeStruct((seq_size, *tokens_in.shape), BF),
        ],
        scratch_shapes=[
            dma((4,)),
            dma((seq_size - 1,)),
            dma((seq_size - 1,)),
            dma((3, 2, seq_size - 1)),
            dma((3, 2, seq_size - 1)),
            dma((3, turns, count)),
            dma((3, turns, count)),
        ],
        compiler_params=pltpu.CompilerParams(collective_id=0, has_side_effects=True),
        cost_estimate=pl.CostEstimate(flops=0, bytes_accessed=100 * 2**20, transcendentals=0),
    )(proj, ffn_in, ffn_out, tokens_in)
    proj_all, in_all, out_all, inputs_all = outs
    flat = (seq_size, fsdp_size)
    return (
        proj_all.reshape(*flat, *proj.shape[1:]),
        in_all.reshape(*flat, *ffn_in.shape),
        out_all.reshape(*flat, *ffn_out.shape),
        inputs_all,
    )


def copy_into(target, index, term, rows=64, add=False):
    depth = target.shape[-2]
    rows = next(n for n in (rows, 48, 32, 16, depth) if depth % n == 0)
    lead = target.shape[len(index) : -2]
    count = 1
    for size in lead:
        count *= size

    def step(i, carry):
        block, place = i // (depth // rows), pl.multiple_of((i % (depth // rows)) * rows, rows)
        where = []
        for size in reversed(lead):
            where.insert(0, block % size)
            block = block // size
        at = (*where, pl.ds(place, rows), slice(None))
        value = term(at).astype(target.dtype)
        target[(*index, *at)] = target[(*index, *at)] + value if add else value
        return carry

    lax.fori_loop(0, count * (depth // rows), step, 0)


def add_into(target, index, term):
    copy_into(target, index, term, add=True)


def finish_plan(seq_size, count):
    last = count - 1
    steps = [[("add", 2 * row + i, step) for i in (0, 1)] for row in range(seq_size) for step in range(1, count)]
    steps.sort(key=lambda pair: (pair[0][1] // 2 + 1.2 * pair[0][2], pair[0][2]))
    ffn = [item for pair in steps for item in pair]
    halves = [2 * seq_size, 2 * seq_size + 1]
    proj = [("add", k, step) for step in range(count) for k in halves]
    plan = [("send", 0), ("open",)]
    share = -(-len(ffn) // (seq_size - 1))
    for hop in range(1, seq_size):
        chunk, ffn = ffn[:share], ffn[share:]
        if hop == seq_size - 1:
            plan += proj[:2]
            proj = proj[2:]
        plan += chunk[: share // 3] + [("arrive", 0, hop)] + chunk[share // 3 :]
    plan += [("send", 1), ("send", 2)]
    proj += [("proj",)]
    share = -(-len(proj) // (seq_size - 1))
    for hop in range(1, seq_size):
        plan += [*proj[:share], ("arrive", 1, hop), ("arrive", 2, hop)]
        proj = proj[share:]
    return plan + [("total", 0), ("total", 1), ("total", 2)]


def finish_kernel(seq_size, bits, da_ref, in_ref, in_added, out_ref, out_added, proj_ref, *refs):
    count = len(bits)
    da_out, in_out, out_out, proj_out = refs[:4]
    da_line, in_line, out_line = refs[4:7]
    in_parts, out_parts, proj_parts = (refs[7 + i * count : 7 + (i + 1) * count] for i in range(3))
    own_sem, keep_sem, line_send, line_recv, cube_send, cube_recv, proj_send, proj_recv = refs[7 + 3 * count :]
    z = lax.axis_index("seq")
    f = lax.axis_index("fsdp")
    bit_of = {bit: (f // bit) % 2 for bit in bits}
    mesh_id = pl.DeviceIdType.MESH
    last = seq_size - 1

    def flipped(bit):
        return {"fsdp": f + bit * (1 - 2 * bit_of[bit])}

    barrier = pltpu.get_barrier_semaphore()
    for step in range(1, seq_size):
        pl.semaphore_signal(barrier, inc=1, device_id={"seq": lax.rem(z + step, seq_size)}, device_id_type=mesh_id)
    for bit in bits:
        pl.semaphore_signal(barrier, inc=1, device_id=flipped(bit), device_id_type=mesh_id)
    pl.semaphore_wait(barrier, seq_size - 1 + count)

    lines = ((da_ref, da_line, da_out), (in_parts[-1], in_line, in_out), (out_parts[-1], out_line, out_out))

    def line(index, side, hop, own):
        terms, sums, _ = lines[index]
        if own:
            source = terms.at[seq_size - hop if side == 0 else hop - 1]
        else:
            source = sums.at[side, hop - 2]
        return pltpu.make_async_remote_copy(
            src_ref=source,
            dst_ref=sums.at[side, hop - 1],
            send_sem=line_send.at[index, side, hop - 1],
            recv_sem=line_recv.at[index, side, hop - 1],
            device_id={"seq": z + 1 - 2 * side},
            device_id_type=mesh_id,
        )

    def at_end(side):
        return z == 0 if side == 0 else z == last

    def from_end(side):
        return z if side == 0 else last - z

    def send_own(index):
        for side in (0, 1):

            @pl.when(at_end(side))
            def _(side=side):
                for hop in range(1, seq_size):
                    line(index, side, hop, True).start()

    def arrive(index, hop):
        terms, sums, _ = lines[index]
        for side in (0, 1):

            @pl.when((from_end(side) >= 1) & (from_end(side) <= hop))
            def _(side=side):
                pltpu.make_async_remote_copy(
                    src_ref=sums.at[side, hop - 1],
                    dst_ref=sums.at[side, hop - 1],
                    send_sem=line_send.at[index, side, hop - 1],
                    recv_sem=line_recv.at[index, side, hop - 1],
                    device_id={"seq": z - 1 + 2 * side},
                    device_id_type=mesh_id,
                ).wait_recv()
                if hop < last:
                    target = z - 1 + seq_size - hop if side == 0 else hop - last + z
                    add_into(sums, (side, hop - 1), lambda at: terms[(target, *at)])
                    line(index, side, hop + 1, False).start()

    def total(index):
        terms, sums, result = lines[index]
        add_first(result, lambda at: terms[(z, *at)])
        for side in (0, 1):

            @pl.when(from_end(side) >= 1)
            def _(side=side):
                add_into(result, (), lambda at: sums[(side, last - 1, *at)])

    def add_first(result, term):
        depth = result.shape[0]
        rows = next(n for n in (64, 32, 16, depth) if depth % n == 0)

        def step(i, carry):
            at = (pl.ds(pl.multiple_of(i * rows, rows), rows), slice(None))
            result[at] = term(at).astype(F32)
            return carry

        lax.fori_loop(0, depth // rows, step, 0)

    plain = bits[::-1]
    turned = plain[:1] + plain[:0:-1]
    some = seq_size // 2
    cubes = []
    for row in range(seq_size):
        cubes += [([in_ref, *in_parts], plain, row, 1), ([out_ref, *out_parts], turned, row, 1)]
    cubes += [([proj_ref, *proj_parts], plain, 0, some), ([proj_ref, *proj_parts], turned, some, seq_size - some)]

    def half_of(index, step, kept):
        states, order = cubes[index][:2]
        where = 1 + sorted(order[step:], reverse=True).index(order[step])
        return states[step], where, bit_of[order[step]] if kept else 1 - bit_of[order[step]]

    def rows_of(index):
        return pl.ds(cubes[index][2], cubes[index][3])

    def cube(index, step):
        source, where, bit = half_of(index, step, False)
        states, order = cubes[index][:2]
        return pltpu.make_async_remote_copy(
            src_ref=source.at[(rows_of(index),) + (slice(None),) * (where - 1) + (bit,)],
            dst_ref=states[step + 1].at[rows_of(index)],
            send_sem=cube_send.at[index, step],
            recv_sem=cube_recv.at[index, step],
            device_id=flipped(order[step]),
            device_id_type=mesh_id,
        )

    def cube_add(index, step):
        source, where, bit = half_of(index, step, True)
        states, _, offset, length = cubes[index]
        cube(index, step).wait()
        for row in range(offset, offset + length):
            add_into(states[step + 1], (row,), lambda at, row=row: source[(row, *at[: where - 1], bit, *at[where - 1 :])])
        if step + 1 < count:
            cube(index, step + 1).start()

    def keep(index):
        source, where, bit = half_of(index, 0, True)
        view = source.at[(rows_of(index),) + (slice(None),) * (where - 1) + (bit,)]
        return pltpu.make_async_copy(view, cubes[index][0][1].at[rows_of(index)], keep_sem.at[index])

    def open_cubes():
        for index in range(2 * seq_size):
            keep(index).start()
        for index in (2 * seq_size, 2 * seq_size + 1):
            cube(index, 0).start()
        for index in range(2 * seq_size):
            row, added = index // 2, (in_added, out_added)[index % 2]
            keep(index).wait()
            add_into(cubes[index][0][1], (row,), lambda at, row=row, added=added: added[(row, *at)])
            cube(index, 1).start()

    def proj(step):
        to = lax.rem(z + step, seq_size)
        return pltpu.make_async_remote_copy(
            src_ref=proj_parts[-1].at[to],
            dst_ref=proj_out.at[z],
            send_sem=proj_send.at[step - 1],
            recv_sem=proj_recv.at[step - 1],
            device_id={"seq": to},
            device_id_type=mesh_id,
        )

    def proj_wait(step):
        view = proj_out.at[lax.rem(z + seq_size - step, seq_size)]
        copy = pltpu.make_async_remote_copy(
            src_ref=view,
            dst_ref=view,
            send_sem=proj_send.at[step - 1],
            recv_sem=proj_recv.at[step - 1],
            device_id={"seq": lax.rem(z + step, seq_size)},
            device_id_type=mesh_id,
        )
        copy.wait_recv()

    def proj_start():
        pltpu.make_async_copy(proj_parts[-1].at[z], proj_out.at[z], own_sem).start()
        for step in range(1, seq_size):
            proj(step).start()

    acts = {"send": send_own, "open": open_cubes, "add": cube_add, "arrive": arrive, "proj": proj_start, "total": total}
    for name, *values in finish_plan(seq_size, count):
        acts[name](*values)
    pltpu.make_async_copy(proj_parts[-1].at[z], proj_out.at[z], own_sem).wait()
    for step in range(1, seq_size):
        proj_wait(step)
        proj(step).wait_send()
    for index in range(3):
        for side in (0, 1):
            for hop in range(1, seq_size):

                @pl.when(at_end(side) | ((from_end(side) >= 1) & (from_end(side) <= hop - 1)))
                def _(index=index, side=side, hop=hop):
                    line(index, side, hop, True).wait_send()


def finish_sums(da, ffin, ffout, proj):
    seq_size = lax.axis_size("seq")
    bits = fsdp_bits(False)
    count = len(bits)
    dma = pltpu.SemaphoreType.DMA
    inside, anywhere = pl.BlockSpec(memory_space=pltpu.VMEM), pl.BlockSpec(memory_space=pl.ANY)
    shapes = [v.shape[-2:] for v in (da, ffin[0], ffout[0])]

    def parts_of(shape, first):
        return [pltpu.VMEM((seq_size, *[2] * (count - step), *shape), BF) for step in range(first, count + 1)]

    return pl.pallas_call(
        functools.partial(finish_kernel, seq_size, bits),
        in_specs=[inside, anywhere, inside, anywhere, inside, inside],
        out_specs=[inside] * 4,
        out_shape=[jax.ShapeDtypeStruct(shape, F32) for shape in shapes]
        + [jax.ShapeDtypeStruct((seq_size, *proj.shape[-2:]), BF)],
        scratch_shapes=[
            *[pltpu.VMEM((2, seq_size - 1, *shape), BF) for shape in shapes],
            *parts_of(shapes[1], 1),
            *parts_of(shapes[2], 1),
            *parts_of(proj.shape[-2:], 1),
            dma,
            dma((2 * seq_size,)),
            dma((3, 2, seq_size - 1)),
            dma((3, 2, seq_size - 1)),
            dma((2 * seq_size + 2, count)),
            dma((2 * seq_size + 2, count)),
            dma((seq_size - 1,)),
            dma((seq_size - 1,)),
        ],
        compiler_params=pltpu.CompilerParams(
            collective_id=1, has_side_effects=True, vmem_limit_bytes=56 * 2**20
        ),
        cost_estimate=pl.CostEstimate(flops=0, bytes_accessed=100 * 2**20, transcendentals=0),
    )(da, *ffin, *ffout, proj)


def whole_tiles(shard, rows=16):
    return shard if shard.shape[0] % rows == 0 else shard.reshape(rows, -1)


def on_device(
    inputs,
    qkv_proj,
    out_proj,
    ffn_in,
    ffn_out,
    norm_gains,
    norm_biases,
    centroids,
    expert_in,
    expert_out,
    doc_lengths,
    routes,
    out_grad,
):
    rows, span, width = inputs.shape
    tokens = rows * span
    seq_size, fsdp_size = lax.axis_size("seq"), lax.axis_size("fsdp")
    here = lax.axis_index("seq")
    length = span * seq_size
    cols = width // seq_size
    capacity = max(2, 3 * tokens // (2 * fsdp_size))
    groups = seq_size // 2

    docs = doc_lengths.shape[1]
    key_pos = jnp.arange(length, dtype=jnp.int32)
    doc_ids = jnp.zeros((rows, length), jnp.int32)
    doc_end = jnp.zeros((rows, 1), jnp.int32)
    for j in range(docs - 1):
        doc_end = doc_end + doc_lengths[:, j : j + 1]
        doc_ids = doc_ids + (key_pos[None, :] >= doc_end).astype(jnp.int32)
    id_rows, id_cols = doc_ids[:, None, :], doc_ids[:, :, None]

    depth = out_proj.shape[0]
    wide = 3 * cols + width + LANES
    slices = qkv_proj.reshape(3, depth, seq_size, cols).transpose(2, 1, 0, 3).reshape(seq_size, depth, 3 * cols)
    small = jnp.concatenate(
        [norm_gains.reshape(-1), norm_biases.reshape(-1), centroids[0], routes.reshape(tokens).astype(BF)]
    )
    small = jnp.pad(small, (0, depth * LANES - small.shape[0])).reshape(depth, LANES)
    slices = jnp.concatenate(
        [slices, *[jnp.broadcast_to(v[None], (seq_size, *v.shape)) for v in (out_proj, small)]], axis=2
    )
    spare = -depth % 16
    bits = fsdp_bits(False)
    crossed = fsdp_bits(True)
    tokens_in = inputs.reshape(tokens, width)
    proj_all, ffin_all, ffout_all, inputs_all = start_gathers(
        jnp.pad(slices, ((0, 0), (0, spare), (0, 0))), whole_tiles(ffn_in), whole_tiles(ffn_out), tokens_in
    )
    inputs_all = inputs_all.reshape(seq_size * tokens, width)
    ffin_all, ffout_all = ffin_all.reshape(width, -1), ffout_all.reshape(-1, width)
    qkv_mine = proj_all[:, :, :depth, : 3 * cols].reshape(width, 3 * cols)
    out_all = proj_all[:, :, :depth, 3 * cols : 3 * cols + width].reshape(width, width)
    small = proj_all[:, :, :depth, 3 * cols + width :].reshape(seq_size, fsdp_size, -1)
    rows_of = small[:, :, : 6 * depth].astype(F32).reshape(-1, 6, depth).transpose(1, 0, 2).reshape(6, width)
    gain_rows, bias_rows = rows_of[:3], rows_of[3:]
    mine = small[:, :, 6 * depth : 6 * depth + cols]
    centroid = lax.dynamic_index_in_dim(mine, lax.axis_index("fsdp"), 1, keepdims=False).reshape(width)
    inputs_all, win_mine, wout_mine, dr_mine = tie(
        inputs_all, expert_in[0], expert_out[0], out_grad.reshape(tokens, width)
    )
    gains_pad, biases_pad = jnp.pad(gain_rows, ((0, 5), (0, 0))), jnp.pad(bias_rows, ((0, 5), (0, 0)))
    proj_used = proj_all if spare == 0 else proj_all[:, :, :depth, : 3 * cols]
    normed_flat, projected = project(inputs_all, gains_pad, biases_pad, proj_used, 3 * cols, tokens)
    projected = projected.reshape(seq_size, rows, span, 3 * cols)

    attended_mine, lse_rows = attend(projected, id_rows, id_cols)
    fsdp_here = lax.axis_index("fsdp")
    routes_all = small[:, :, 6 * depth + cols : 6 * depth + cols + tokens]
    routes_all = lax.dynamic_index_in_dim(routes_all, fsdp_here, 1, keepdims=False)
    later = (jnp.arange(tokens)[:, None] > jnp.arange(tokens)[None, :]).astype(BF)
    placings = []
    for group in range(groups):
        route = pick(routes_all, (here + seq_size - 2 * group) % seq_size).astype(jnp.int32)
        choose = route[:, None] == jnp.arange(fsdp_size, dtype=jnp.int32)[None, :]
        before = mm(later, choose.astype(BF))
        slot_rank = jnp.sum(jnp.where(choose, before, 0.0), axis=1).astype(jnp.int32)
        target = route * capacity + slot_rank
        slots = jnp.arange(fsdp_size * capacity, dtype=jnp.int32)
        placings.append((target[:, None] == slots[None, :]).astype(BF))
    grad_tokens = out_grad.reshape(tokens, width)

    def slots_of(placing, values):
        return mm_tn(placing, values).astype(BF).reshape(fsdp_size, capacity, width)

    def swap_slots(values):
        return lax.all_to_all(values, "fsdp", split_axis=0, concat_axis=0, tiled=True)

    def tokens_of(placing, values):
        return mm(placing, values.reshape(fsdp_size * capacity, width))

    win_half, wout_half = win_mine.shape[1] // 2, wout_mine.shape[0] // 2
    pair_in_low = seq_pair(win_mine[:, :win_half])
    grad_moved = [seq_shift(dr_mine, 2 * group) for group in range(1, groups)]
    grad_slots = [slots_of(placings[group], ([grad_tokens] + grad_moved)[group]) for group in range(groups)]
    grad_slots = jnp.concatenate(grad_slots, axis=1)
    attended_mine, pair_in_low, grad_slots = tie(attended_mine, pair_in_low, grad_slots)
    grad_slots = swap_slots(grad_slots)
    attended = seq_exchange(attended_mine)
    attended = attended.transpose(1, 2, 0, 3).reshape(tokens, width)
    attended, pair_in_high, pair_out_low, wout_high = tie(
        attended, win_mine[:, win_half:], wout_mine[:wout_half], wout_mine[wout_half:]
    )
    pair_in_high, pair_out_low = seq_pair(pair_in_high), seq_pair(pair_out_low)

    resid_in = tokens_in.astype(F32)
    middle = resid_in + mm(attended, out_all)
    hidden_low, active_low, active_slope, block_out, routed = ffn_forward(
        middle, gains_pad, biases_pad, ffin_all, ffout_all
    )
    routed, wout_high, pair_in_high, pair_out_low, grad_slots = tie(
        routed, wout_high, pair_in_high, pair_out_low, grad_slots
    )
    grad_slots = grad_slots.reshape(fsdp_size, groups, capacity, width)
    grad_slots = [grad_slots[:, group].reshape(-1, width) for group in range(groups)]
    slots_own = slots_of(placings[0], routed)
    pair_out_high = seq_pair(wout_high)

    own_mean, own_scale = norm_parts(resid_in)

    arrived = [swap_slots(slots_own).reshape(-1, width)]
    for group in range(1, groups):
        routed_here = seq_shift(routed, 2 * group)
        routed_here, pair_out_high, qkv_mine, own_mean, own_scale, *grad_slots = tie(
            routed_here, pair_out_high, qkv_mine, own_mean, own_scale, *grad_slots
        )
        slots_here = slots_of(placings[group], routed_here)
        slots_here, pair_out_high, *arrived = tie(slots_here, pair_out_high, *arrived)
        arrived.append(swap_slots(slots_here).reshape(-1, width))
    weights = (win_mine, wout_mine, pair_in_low, pair_in_high, pair_out_low, pair_out_high)
    shared, rows_grads, terms = (), [], []
    for group in range(groups):
        *shared, rows_grad, term = expert_block(
            group, groups, fsdp_size, arrived[group], grad_slots[group], centroid, weights, shared
        )
        rows_grads.append(rows_grad)
        terms.append(term)
    act, du, dz, arrived, gated_all = shared

    half = expert_in.shape[2]
    in_sent = mm_tn(arrived, du[:, half:]).astype(BF)
    back_low = [None] * groups
    for group in reversed(range(groups)):
        rows_grad = rows_grads[group].reshape(fsdp_size, capacity, width)
        if group + 1 < groups:
            rows_grad, back_low[group + 1] = tie(rows_grad, back_low[group + 1])
        back_slots = swap_slots(rows_grad)
        if group + 1 == groups:
            back_slots, in_sent = tie(back_slots, in_sent)
        back_low[group] = tokens_of(placings[group], back_slots)
        if group:
            back_low[group] = back_low[group].astype(BF)
    in_pair = seq_pair(in_sent)
    if groups > 1:
        gated_all, arrived, act, du, back_low[-1] = tie(gated_all, arrived, act, du, back_low[-1])
    back_sum = back_low[0]
    for group in range(1, groups):
        back_sum = back_sum + seq_shift(back_low[group], -2 * group).astype(F32)
    centroid_term = sum(term[0] for term in terms)
    out_sent = mm_tn(act[:, half:], dz).astype(BF)
    in_kept = mm_tn(arrived, du[:, :half])
    out_kept = mm_tn(act[:, :half], dz)

    gated_back = swap_slots(gated_all).reshape(fsdp_size, groups, capacity, width)
    out_terms = [tokens_of(placings[group], gated_back[:, group]) for group in range(groups)]
    out_terms = out_terms[:1] + [v.astype(BF) for v in out_terms[1:]]
    back_sum, out_sent, in_kept, out_kept = tie(back_sum, out_sent, in_kept, out_kept)

    block_low, hidden_grad, middle_grad, branch, dense_rows = ffn_backward(
        back_sum, block_out, grad_tokens, middle, gains_pad, active_slope, ffin_all, ffout_all
    )
    gain_three, bias_three, gain_two, bias_two = (dense_rows[i] for i in range(4))
    attended_grad = mm_nt(branch, out_all).astype(BF)
    attended_grad = attended_grad.reshape(rows, span, seq_size, cols).transpose(2, 0, 1, 3)
    attended_grad, in_pair, active_low, hidden_low, attended = tie(
        attended_grad, in_pair, active_low, hidden_low, attended
    )
    attended_grad = seq_exchange(attended_grad, True)

    def halved(term):
        terms = hyper_split(by_device(term))
        sent = lax.dynamic_index_in_dim(terms, 1 - fsdp_here % 2, terms.ndim - 3, keepdims=False)
        return terms, fsdp_flip(sent, 1)

    ffout_terms = halved(mm_tn(active_low, block_low))
    ffin_terms = mm_tn(hidden_low, hidden_grad).astype(BF)
    proj_terms = mm_tn(attended, branch).astype(BF).reshape(seq_size, fsdp_size, depth, width)
    def split(values):
        size = values.shape[0] // 4
        return values[: 2 * size], values[2 * size : 3 * size], values[3 * size :]

    def send_pieces(pieces):
        return [seq_pair(pieces[0])] + [seq_shift(pieces[group], -2 * group) for group in range(1, groups)]

    out_pieces = [split(values) for values in [out_sent, *out_terms[1:]]]
    sizes = len(out_pieces)
    attended_grad, *out_first = tie(attended_grad, *[pieces[0] for pieces in out_pieces])
    out_first = send_pieces(out_first)

    dq, dk, dv = attend_back(projected, attended_grad, lse_rows, id_rows, id_cols)
    projected_grad = jnp.concatenate([dq, dk, dv], axis=-1).reshape(seq_size * tokens, 3 * cols)
    projected_grad, inputs_all, in_kept, out_kept, proj_terms, ffin_terms, *moved = tie(
        projected_grad,
        inputs_all,
        in_kept,
        out_kept,
        proj_terms,
        ffin_terms,
        *out_first,
        *[pieces[1] for pieces in out_pieces],
    )
    ffin_terms = halved(ffin_terms)
    proj_terms = jnp.pad(proj_terms, ((0, 0), (0, 0), (0, spare), (3 * cols, LANES)))
    out_first, out_second = moved[:sizes], send_pieces(moved[sizes:])
    normed_low_terms = mm_nt(projected_grad, qkv_mine).astype(BF)
    parts_all = norm_parts(inputs_all.astype(F32))
    unit_all = (inputs_all.astype(F32) - parts_all[0]) * parts_all[1]
    terms_wide = normed_low_terms.astype(F32)
    gain_one, bias_one = jnp.sum(terms_wide * unit_all, axis=0), jnp.sum(terms_wide, axis=0)
    small_terms = jnp.stack([gain_one, gain_two, gain_three, bias_one, bias_two, bias_three])

    qkv_term = mm_tn(normed_flat, projected_grad).astype(BF).reshape(seq_size, fsdp_size, depth, 3 * cols)
    qkv_term, *moved = tie(qkv_term, *out_second, *[pieces[2] for pieces in out_pieces])
    out_second, out_third = moved[:sizes], send_pieces(moved[sizes:])
    small_rows = small_terms.astype(BF).reshape(6, seq_size, fsdp_size, depth).transpose(1, 2, 0, 3)
    centroid_rows = jnp.where(
        (jnp.arange(fsdp_size) == fsdp_here)[None, :, None], centroid_term.reshape(seq_size, 1, cols), 0.0
    )
    small_rows = jnp.concatenate([small_rows.reshape(seq_size, fsdp_size, 6 * depth), centroid_rows.astype(BF)], axis=2)
    small_rows = jnp.pad(small_rows, ((0, 0), (0, 0), (0, depth * LANES - small_rows.shape[2])))
    small_rows = small_rows.reshape(seq_size, fsdp_size, depth, LANES)
    proj_terms = lax.dynamic_update_slice(proj_terms, qkv_term, (0, 0, 0, 0))
    proj_terms = hyper_split(lax.dynamic_update_slice(proj_terms, small_rows, (0, 0, 0, 3 * cols + width)))
    proj_terms, *out_third = tie(proj_terms, *out_third)
    out_pair, *out_moved = [jnp.concatenate(v, axis=0) for v in zip(out_first, out_second, out_third, strict=True)]
    outputs = block_out + out_terms[0] + sum(v.astype(F32) for v in out_moved)
    outputs = outputs.astype(BF).reshape(rows, span, width)
    normed_one_grad, ffn_in_grad, ffn_out_grad, proj_sums = finish_sums(
        normed_low_terms.reshape(seq_size, tokens, width), ffin_terms, ffout_terms, proj_terms
    )
    ffn_in_grad, ffn_out_grad = ffn_in_grad.reshape(ffn_in.shape), ffn_out_grad.reshape(ffn_out.shape)
    proj_sums = proj_sums.astype(F32)
    qkv_grad = proj_sums[:, :depth, : 3 * cols].reshape(seq_size, depth, 3, cols)
    qkv_grad = qkv_grad.transpose(2, 1, 0, 3).reshape(qkv_proj.shape)
    out_proj_grad = jnp.sum(proj_sums[:, :depth, 3 * cols : 3 * cols + width], axis=0)
    small = jnp.sum(proj_sums[:, :depth, 3 * cols + width :], axis=0).reshape(-1)
    small_grad = small[: 6 * depth].reshape(6, depth)
    centroids_grad = small[6 * depth : 6 * depth + cols][None]

    expert_in_grad = (in_kept + in_pair.astype(F32))[None]
    expert_out_grad = (out_kept + out_pair.astype(F32))[None]

    input_norm_grad, _, _ = norm_back(resid_in, (own_mean, own_scale), gain_rows[0], normed_one_grad)
    input_grad = (middle_grad + input_norm_grad).reshape(rows, span, width)
    return (
        outputs,
        input_grad,
        qkv_grad,
        out_proj_grad,
        ffn_in_grad,
        ffn_out_grad,
        small_grad[:3],
        small_grad[3:],
        centroids_grad,
        expert_in_grad,
        expert_out_grad,
    )


def solution(mesh):
    dense = P(("seq", "fsdp"), None)
    placed = (
        P("fsdp", "seq", None),
        P(None, ("seq", "fsdp"), None),
        dense,
        dense,
        dense,
        P(None, ("seq", "fsdp")),
        P(None, ("seq", "fsdp")),
        P("fsdp", "seq"),
        P("fsdp", None, "seq"),
        P("fsdp", "seq", None),
        P("fsdp", None),
        P("seq", "fsdp", None, None),
        P("fsdp", "seq", None),
    )
    returned = (
        P("fsdp", "seq", None),
        P("fsdp", "seq", None),
        P(None, ("seq", "fsdp"), None),
        dense,
        dense,
        dense,
        P(None, ("seq", "fsdp")),
        P(None, ("seq", "fsdp")),
        P("fsdp", "seq"),
        P("fsdp", None, "seq"),
        P("fsdp", "seq", None),
    )
    return jax.shard_map(on_device, mesh=mesh, in_specs=placed, out_specs=returned, check_vma=False)
```

```python
import functools

import jax
import jax.numpy as jnp
from jax import lax
from jax.experimental import pallas as pl
from jax.experimental.pallas import tpu as pltpu
from jax.sharding import PartitionSpec as P

HEAD_DIM = 64
LANES = 128
norm_eps = 1e-05
BF = jnp.bfloat16
F32 = jnp.float32


def layer_norm(values, gain_row, shift_row):
    average = jnp.mean(values, axis=-1, keepdims=True)
    centered = values - average
    variance = jnp.mean(centered * centered, axis=-1, keepdims=True)
    return centered * lax.rsqrt(variance + norm_eps) * gain_row + shift_row


def gelu_pair(values):
    cdf = 0.5 * (1.0 + lax.erf(values * (0.5**0.5)))
    pdf = 0.3989422804014327 * jnp.exp(-0.5 * values * values)
    return values * cdf, cdf + values * pdf


def mm(left, right):
    return jnp.dot(left, right, preferred_element_type=F32)


def mm_nt(left, right):
    return lax.dot_general(left, right, (((1,), (1,)), ((), ())), preferred_element_type=F32)


def mm_tn(left, right):
    return lax.dot_general(left, right, (((0,), (0,)), ((), ())), preferred_element_type=F32)


def norm_parts(values):
    average = jnp.mean(values, axis=-1, keepdims=True)
    centered = values - average
    variance = jnp.mean(centered * centered, axis=-1, keepdims=True)
    return average, lax.rsqrt(variance + norm_eps)


def norm_back(values, parts, gain_row, grads):
    average, scale = parts
    unit = (values - average) * scale
    unit_grad = grads * gain_row
    first = jnp.mean(unit_grad, axis=-1, keepdims=True)
    second = jnp.mean(unit_grad * unit, axis=-1, keepdims=True)
    return scale * (unit_grad - first - unit * second), jnp.sum(grads * unit, axis=0), jnp.sum(grads, axis=0)


def tie(*values):
    return lax.optimization_barrier(values)


def seq_shift(values, step):
    size = lax.axis_size("seq")
    return lax.ppermute(values, "seq", [(i, (i + step) % size) for i in range(size)])


def seq_pair(values):
    size = lax.axis_size("seq")
    return lax.ppermute(values, "seq", [(i, i ^ 1) for i in range(size)])


def put(buffer, values, place):
    return lax.dynamic_update_index_in_dim(buffer, values, place, 0)


def pick(values, place):
    return lax.dynamic_index_in_dim(values, place, 0, keepdims=False)


def seq_exchange(values, chained=False):
    size = lax.axis_size("seq")
    here = lax.axis_index("seq")
    result = put(jnp.zeros_like(values), pick(values, here), here)
    arrived = None
    for step in range(1, size):
        sent = pick(values, (here + step) % size)
        if chained and arrived is not None:
            sent, arrived = tie(sent, arrived)
        if arrived is not None:
            result = put(result, arrived, (here - step + 1) % size)
        arrived = seq_shift(sent, step)
    return put(result, arrived, (here - size + 1) % size)


def seq_sum_scatter(values):
    size = lax.axis_size("seq")
    here = lax.axis_index("seq")
    total = pick(values, here).astype(F32)
    for step in range(1, size):
        arrived = seq_shift(pick(values, (here + step) % size).astype(BF), step)
        total = total + arrived.astype(F32)
    return total


def masked_pair(block):
    lane = lax.broadcasted_iota(jnp.int32, block.shape, 1)
    zero = jnp.zeros_like(block)
    return jnp.where(lane < HEAD_DIM, block, zero), jnp.where(lane < HEAD_DIM, zero, block)


def allowed_block(id_col, id_row, start, size, end):
    key_pos = lax.broadcasted_iota(jnp.int32, (end, size), 0)
    query_pos = start + lax.broadcasted_iota(jnp.int32, (end, size), 1)
    return (id_col[:end, :] == id_row[:, start:end]) & (key_pos <= query_pos)


def attend_kernel(size, q_ref, k_ref, v_ref, id_row_ref, id_col_ref, o_ref, lse_ref, o_all):
    length = id_row_ref.shape[-1]
    queries = q_ref[...].reshape(length, LANES) * jnp.asarray(HEAD_DIM**-0.5, BF)
    keys = k_ref[...].reshape(length, LANES)
    values_t = v_ref[...].reshape(length, LANES).T
    id_row = id_row_ref[0]
    id_col = id_col_ref[0]
    for start in range(0, length, size):
        end = start + size
        mask = allowed_block(id_col, id_row, start, size, end)
        parts = []
        for head, query in enumerate(masked_pair(queries[start:end])):
            scores = jnp.where(mask, mm_nt(keys[:end], query), -1e30)
            top = jnp.max(scores, axis=0, keepdims=True)
            powers = jnp.exp(scores - top)
            whole = jnp.sum(powers, axis=0, keepdims=True)
            weights = (powers * (1.0 / whole)).astype(BF)
            lse_ref[0, 0, pl.ds(head, 1), pl.ds(start, size)] = top + jnp.log(whole)
            part = values_t[head * HEAD_DIM : (head + 1) * HEAD_DIM, :end]
            parts.append(mm(part, weights))
        o_all[pl.ds(start, size), :] = jnp.concatenate(parts, axis=0).T
    o_ref[...] = o_all[...].astype(BF).reshape(o_ref.shape)


def attend_back_kernel(
    size, q_ref, k_ref, v_ref, do_ref, lse_ref, id_row_ref, id_col_ref, dq_ref, dk_ref, dv_ref, dq_all, dk_all, dv_all
):
    length = id_row_ref.shape[-1]
    scale = HEAD_DIM**-0.5
    queries = q_ref[...].reshape(length, LANES) * jnp.asarray(scale, BF)
    keys = k_ref[...].reshape(length, LANES)
    keys_t = keys.T
    values = v_ref[...].reshape(length, LANES)
    grads = do_ref[...].reshape(length, LANES)
    id_row = id_row_ref[0]
    id_col = id_col_ref[0]
    dk_all[...] = jnp.zeros_like(dk_all)
    dv_all[...] = jnp.zeros_like(dv_all)
    for start in range(0, length, size):
        end = start + size
        mask = allowed_block(id_col, id_row, start, size, end)
        parts = []
        heads = zip(masked_pair(queries[start:end]), masked_pair(grads[start:end]), strict=True)
        for head, (query, grad) in enumerate(heads):
            scores = jnp.where(mask, mm_nt(keys[:end], query), -1e30)
            probs = jnp.exp(scores - lse_ref[0, 0, pl.ds(head, 1), pl.ds(start, size)])
            prob_grad = mm_nt(values[:end], grad)
            total = jnp.sum(probs * prob_grad, axis=0, keepdims=True)
            score_grad = (probs * (prob_grad - total)).astype(BF)
            dv_all[pl.ds(0, end), :] += mm(probs.astype(BF), grad)
            dk_all[pl.ds(0, end), :] += mm(score_grad, query)
            parts.append(mm(keys_t[head * HEAD_DIM : (head + 1) * HEAD_DIM, :end], score_grad))
        dq_all[pl.ds(start, size), :] = jnp.concatenate(parts, axis=0).T * scale
    dq_ref[...] = dq_all[...].astype(BF).reshape(dq_ref.shape)
    dk_ref[...] = dk_all[...].astype(BF).reshape(dk_ref.shape)
    dv_ref[...] = dv_all[...].astype(BF).reshape(dv_ref.shape)


def attention_specs(projected, length):
    blocks, rows, span, width3 = projected.shape
    columns = width3 // 3 // LANES

    def part(index):
        return pl.BlockSpec((blocks, 1, span, LANES), lambda r, c: (0, r, 0, index * columns + c))

    id_row = pl.BlockSpec((1, 1, length), lambda r, c: (r, 0, 0))
    id_col = pl.BlockSpec((1, length, 1), lambda r, c: (r, 0, 0))
    lse = pl.BlockSpec((1, 1, 2, length), lambda r, c: (r, c, 0, 0))
    return rows, columns, part, id_row, id_col, lse


def attend(projected, id_rows, id_cols):
    length = id_rows.shape[-1]
    blocks, rows, span, width3 = projected.shape
    rows, columns, part, id_row, id_col, lse = attention_specs(projected, length)
    return pl.pallas_call(
        functools.partial(attend_kernel, min(256, length)),
        grid=(rows, columns),
        in_specs=[part(0), part(1), part(2), id_row, id_col],
        out_specs=[part(0), lse],
        out_shape=[
            jax.ShapeDtypeStruct((blocks, rows, span, width3 // 3), BF),
            jax.ShapeDtypeStruct((rows, columns, 2, length), F32),
        ],
        scratch_shapes=[pltpu.VMEM((length, LANES), F32)],
        compiler_params=pltpu.CompilerParams(vmem_limit_bytes=40 * 2**20),
        cost_estimate=pl.CostEstimate(flops=10**6, bytes_accessed=2**16, transcendentals=0),
    )(projected, projected, projected, id_rows, id_cols)


def attend_back(projected, grads, lse_rows, id_rows, id_cols):
    length = id_rows.shape[-1]
    blocks, rows, span, width3 = projected.shape
    rows, columns, part, id_row, id_col, lse = attention_specs(projected, length)
    shape = jax.ShapeDtypeStruct((blocks, rows, span, width3 // 3), BF)
    return pl.pallas_call(
        functools.partial(attend_back_kernel, min(256, length)),
        grid=(rows, columns),
        in_specs=[part(0), part(1), part(2), part(0), lse, id_row, id_col],
        out_specs=[part(0)] * 3,
        out_shape=[shape] * 3,
        scratch_shapes=[pltpu.VMEM((length, LANES), F32)] * 3,
        compiler_params=pltpu.CompilerParams(vmem_limit_bytes=48 * 2**20),
        cost_estimate=pl.CostEstimate(flops=10**6, bytes_accessed=2**16, transcendentals=0),
    )(projected, projected, projected, grads, lse_rows, id_rows, id_cols)


def fsdp_flip(values, bit):
    size = lax.axis_size("fsdp")
    return lax.ppermute(values, "fsdp", [(i, i ^ bit) for i in range(size)])


def fsdp_bits(crossed):
    bits = [1 << i for i in range(1, lax.axis_size("fsdp").bit_length() - 1)]
    return (bits[::-1] if crossed else bits) + [1]


def hyper_split(parts):
    count = parts.shape[1].bit_length() - 1
    return parts.reshape(parts.shape[0], *[2] * count, *parts.shape[2:])


def by_device(term):
    seq_size, fsdp_size = lax.axis_size("seq"), lax.axis_size("fsdp")
    depth = term.shape[0] // (seq_size * fsdp_size)
    tile = (depth, term.shape[1]) if depth % 16 == 0 else (16, depth * term.shape[1] // 16)
    return term.astype(BF).reshape(seq_size, fsdp_size, *tile)


def project_kernel(x_ref, gains_ref, biases_ref, w_ref, normed_ref, out_ref):
    x = x_ref[...].astype(F32)
    average, scale = norm_parts(x)
    normed = ((x - average) * scale * gains_ref[0:1] + biases_ref[0:1]).astype(BF)
    normed_ref[...] = normed
    out_ref[...] = mm(normed, w_ref[...].reshape(x.shape[1], w_ref.shape[-1])).astype(BF)


def project(inputs_all, gains, biases, weights, columns, tokens):
    width = inputs_all.shape[1]
    row = pl.BlockSpec((8, width), lambda i: (0, 0))
    return pl.pallas_call(
        project_kernel,
        grid=(inputs_all.shape[0] // tokens,),
        in_specs=[
            pl.BlockSpec((tokens, width), lambda i: (i, 0)),
            row,
            row,
            pl.BlockSpec((*weights.shape[:3], columns), lambda i: (0, 0, 0, 0)),
        ],
        out_specs=[pl.BlockSpec((tokens, width), lambda i: (i, 0)), pl.BlockSpec((tokens, columns), lambda i: (i, 0))],
        out_shape=[
            jax.ShapeDtypeStruct(inputs_all.shape, BF),
            jax.ShapeDtypeStruct((inputs_all.shape[0], columns), BF),
        ],
        compiler_params=pltpu.CompilerParams(vmem_limit_bytes=40 * 2**20),
        cost_estimate=pl.CostEstimate(flops=10**6, bytes_accessed=2**16, transcendentals=0),
    )(inputs_all, gains, biases, weights)


def ffn_kernel(middle_ref, gains_ref, biases_ref, win_ref, wout_ref, normed_ref, act_ref, slope_ref, block_ref, routed_ref):
    chunk = pl.program_id(0)

    def norm(values, row):
        average, scale = norm_parts(values)
        return ((values - average) * scale * gains_ref[row : row + 1] + biases_ref[row : row + 1]).astype(BF)

    @pl.when(chunk == 0)
    def _():
        normed_ref[...] = norm(middle_ref[...], 1)
        block_ref[...] = middle_ref[...]

    act, slope = gelu_pair(mm(normed_ref[...], win_ref[...]))
    act = act.astype(BF)
    act_ref[...] = act
    slope_ref[...] = slope.astype(BF)
    block_ref[...] += mm(act, wout_ref[...])

    @pl.when(chunk == pl.num_programs(0) - 1)
    def _():
        routed_ref[...] = norm(block_ref[...], 2)


def ffn_specs(tokens, width, hidden):
    size = min(512, hidden)
    whole = pl.BlockSpec((tokens, width), lambda j: (0, 0))
    piece = pl.BlockSpec((tokens, size), lambda j: (0, j))
    row = pl.BlockSpec((8, width), lambda j: (0, 0))
    return size, whole, piece, row, [
        pl.BlockSpec((width, size), lambda j: (0, j)),
        pl.BlockSpec((size, width), lambda j: (j, 0)),
    ]


def ffn_forward(middle, gains, biases, win, wout):
    tokens, width = middle.shape
    hidden = win.shape[1]
    size, whole, piece, row, weights = ffn_specs(tokens, width, hidden)
    low, wide = jax.ShapeDtypeStruct((tokens, width), BF), jax.ShapeDtypeStruct((tokens, hidden), BF)
    return pl.pallas_call(
        ffn_kernel,
        grid=(hidden // size,),
        in_specs=[whole, row, row, *weights],
        out_specs=[whole, piece, piece, whole, whole],
        out_shape=[low, wide, wide, jax.ShapeDtypeStruct((tokens, width), F32), low],
        compiler_params=pltpu.CompilerParams(vmem_limit_bytes=48 * 2**20),
        cost_estimate=pl.CostEstimate(flops=10**6, bytes_accessed=2**16, transcendentals=0),
    )(middle, gains, biases, win, wout)


def ffn_back_kernel(
    back_ref, block_ref, grad_ref, middle_ref, gains_ref, slope_ref, win_ref, wout_ref,
    low_ref, du_ref, dh_ref, branch_ref, terms_ref, total,
):
    chunk = pl.program_id(0)

    def norm_grad(values, row, grads):
        moved, gain, bias = norm_back(values, norm_parts(values), gains_ref[row : row + 1], grads)
        return moved, gain[None], bias[None]

    @pl.when(chunk == 0)
    def _():
        moved, gain, bias = norm_grad(block_ref[...], 2, back_ref[...])
        grads = grad_ref[...].astype(F32) + moved
        dh_ref[...] = grads
        low_ref[...] = grads.astype(BF)
        terms_ref[0:1] = gain
        terms_ref[1:2] = bias
        total[...] = jnp.zeros_like(total)

    du = (slope_ref[...].astype(F32) * mm_nt(low_ref[...], wout_ref[...])).astype(BF)
    du_ref[...] = du
    total[...] += mm_nt(du, win_ref[...])

    @pl.when(chunk == pl.num_programs(0) - 1)
    def _():
        moved, gain, bias = norm_grad(middle_ref[...], 1, total[...])
        grads = dh_ref[...] + moved
        dh_ref[...] = grads
        branch_ref[...] = grads.astype(BF)
        terms_ref[2:3] = gain
        terms_ref[3:4] = bias


def ffn_backward(back, block_out, grads, middle, gains, slope, win, wout):
    tokens, width = middle.shape
    hidden = win.shape[1]
    size, whole, piece, row, weights = ffn_specs(tokens, width, hidden)
    low, wide = jax.ShapeDtypeStruct((tokens, width), BF), jax.ShapeDtypeStruct((tokens, hidden), BF)
    f32 = jax.ShapeDtypeStruct((tokens, width), F32)
    return pl.pallas_call(
        ffn_back_kernel,
        grid=(hidden // size,),
        in_specs=[whole, whole, whole, whole, row, piece, *weights],
        out_specs=[whole, piece, whole, whole, row],
        out_shape=[low, wide, f32, low, jax.ShapeDtypeStruct((8, width), F32)],
        scratch_shapes=[pltpu.VMEM((tokens, width), F32)],
        compiler_params=pltpu.CompilerParams(vmem_limit_bytes=48 * 2**20),
        cost_estimate=pl.CostEstimate(flops=10**6, bytes_accessed=2**16, transcendentals=0),
    )(back, block_out, grads, middle, gains, slope, win, wout)


def expert_kernel(x_ref, dr_ref, centroid_ref, win_own, wout_own, win_low, win_high, wout_low, wout_high, *refs):
    act_ref, du_ref, dz_ref, all_ref, gated_ref, dx_ref, term_ref, total, back, win_ref, wout_ref = refs[-11:]
    groups_of = gated_ref.shape
    chunk = pl.program_id(0)
    own = pl.num_programs(0) - 2
    for here, win_part, wout_part in (
        (chunk < own, win_own, wout_own),
        (chunk == own, win_low, wout_low),
        (chunk == own + 1, win_high, wout_high),
    ):

        @pl.when(here)
        def _(win_part=win_part, wout_part=wout_part):
            win_ref[...] = win_part[...]
            wout_ref[...] = wout_part[...]

    x = x_ref[...]

    def gate_of():
        logits = mm_nt(x, centroid_ref[...])[:, :1]
        return 1.0 / (1.0 + jnp.exp(-logits))

    @pl.when(chunk == 0)
    def _():
        dz_ref[...] = (gate_of() * dr_ref[...].astype(F32)).astype(BF)
        all_ref[...] = x
        total[...] = jnp.zeros_like(total)
        back[...] = jnp.zeros_like(back)

    act, slope = gelu_pair(mm(x, win_ref[...]))
    act = act.astype(BF)
    act_ref[...] = act
    total[...] += mm(act, wout_ref[...])
    du = (slope * mm_nt(dz_ref[...], wout_ref[...])).astype(BF)
    du_ref[...] = du
    back[...] += mm_nt(du, win_ref[...])

    @pl.when(chunk == pl.num_programs(0) - 1)
    def _():
        gate = gate_of()
        result = total[...]
        gated_ref[...] = (gate * result).astype(BF).reshape(groups_of)
        dl = jnp.sum(dr_ref[...].astype(F32) * result, axis=1, keepdims=True) * gate * (1.0 - gate)
        dx_ref[...] = (back[...] + dl * centroid_ref[:1].astype(F32)).astype(BF)
        term_ref[...] = jnp.broadcast_to(jnp.sum(dl * x.astype(F32), axis=0, keepdims=True), term_ref.shape)


def expert_block(group, groups, blocks, arrived, grads, centroid, weights, earlier):
    slots, width = arrived.shape
    size = weights[2].shape[1]
    own = weights[0].shape[1] // size
    hidden = (own + 2) * size
    whole = pl.BlockSpec((slots, width), lambda j: (0, 0))
    shared = pl.BlockSpec((slots, width), lambda j: (group, 0))
    piece = pl.BlockSpec((slots, size), lambda j: (group, j))
    row = pl.BlockSpec((LANES, width), lambda j: (0, 0))
    term = pl.BlockSpec((8, width), lambda j: (0, 0))
    win_piece = pl.BlockSpec((width, size), lambda j: (0, 0))
    wout_piece = pl.BlockSpec((size, width), lambda j: (0, 0))
    return pl.pallas_call(
        expert_kernel,
        grid=(own + 2,),
        in_specs=[
            whole,
            whole,
            row,
            pl.BlockSpec((width, size), lambda j: (0, jnp.minimum(j, own - 1))),
            pl.BlockSpec((size, width), lambda j: (jnp.minimum(j, own - 1), 0)),
            win_piece,
            win_piece,
            wout_piece,
            wout_piece,
            *[pl.BlockSpec(memory_space=pl.ANY)] * len(earlier),
        ],
        out_specs=[
            piece,
            piece,
            shared,
            shared,
            pl.BlockSpec((blocks, slots // blocks, width), lambda j: (0, group, 0)),
            whole,
            term,
        ],
        out_shape=[jax.ShapeDtypeStruct((groups * slots, hidden), BF)] * 2
        + [jax.ShapeDtypeStruct((groups * slots, width), BF)] * 2
        + [jax.ShapeDtypeStruct((blocks, groups * slots // blocks, width), BF)]
        + [jax.ShapeDtypeStruct((slots, width), BF)]
        + [jax.ShapeDtypeStruct((8, width), F32)],
        scratch_shapes=[pltpu.VMEM((slots, width), F32)] * 2
        + [pltpu.VMEM((width, size), BF), pltpu.VMEM((size, width), BF)],
        input_output_aliases={9 + i: i for i in range(len(earlier))},
        compiler_params=pltpu.CompilerParams(vmem_limit_bytes=48 * 2**20),
        cost_estimate=pl.CostEstimate(flops=10**6, bytes_accessed=2**16, transcendentals=0),
    )(arrived, grads, jnp.broadcast_to(centroid[None], (LANES, width)), *weights, *earlier)


def gather_plan(seq_size, count):
    plan = [("send", 0), ("send", 1), ("own",)]
    for hop in range(1, seq_size):
        plan += [("proj", hop), ("arrive", 0, hop), ("arrive", 1, hop)]
        if hop == 1:
            plan += [("send", 2)]
        if hop < seq_size - 1:
            plan += [("go", hop - 1, 0)]
    last = seq_size - 1
    rest = [("go", 0, 1), ("go", last - 1, 0), ("go", 1, 1), ("go", last, 0)]
    rest += [("go", hop, step) for step in range(1, count - 1) for hop in range(2 if step == 1 else 0, seq_size)]
    plan += [("arrive", 2, 1), *rest[:4]]
    rest = rest[4:]
    share = -(-len(rest) // max(1, seq_size - 2))
    for hop in range(2, seq_size):
        plan += [("arrive", 2, hop), *rest[(hop - 2) * share : (hop - 1) * share]]
    return plan + [("go", hop, count - 1) for hop in range(seq_size)]


def gather_kernel(seq_size, bits, proj_ref, in_ref, out_ref, x_ref, proj_all, in_all, out_all, x_all, *sems):
    own_sem, proj_send, proj_recv, line_send, line_recv, cube_send, cube_recv = sems
    z = lax.axis_index("seq")
    f = lax.axis_index("fsdp")
    count = len(bits)
    high_first = sorted(bits, reverse=True)
    bit_of = {bit: (f // bit) % 2 for bit in bits}
    mesh_id = pl.DeviceIdType.MESH

    barrier = pltpu.get_barrier_semaphore()
    for step in range(1, seq_size):
        pl.semaphore_signal(barrier, inc=1, device_id={"seq": lax.rem(z + step, seq_size)}, device_id_type=mesh_id)
    for bit in bits:
        pl.semaphore_signal(barrier, inc=1, device_id={"fsdp": f + bit * (1 - 2 * bit_of[bit])}, device_id_type=mesh_id)
    pl.semaphore_wait(barrier, seq_size - 1 + count)

    def place(buffer, s, done=()):
        if buffer is x_all:
            return buffer.at[s]
        return buffer.at[(s, *(slice(None) if bit in done else bit_of[bit] for bit in high_first))]

    def order_of(index, turn):
        return bits if (index + turn) % 2 == 0 else bits[-2::-1] + bits[-1:]

    cubes = ((proj_all, 0), (in_all, 0), (out_all, 1))

    def cube(index, s, turn, step):
        buffer, crossed = cubes[index]
        order = order_of(crossed, turn if index == 0 else 0)
        view = place(buffer, s, order[:step])
        bit = order[step]
        return pltpu.make_async_remote_copy(
            src_ref=view,
            dst_ref=view,
            send_sem=cube_send.at[index, turn, step],
            recv_sem=cube_recv.at[index, turn, step],
            device_id={"fsdp": f + bit * (1 - 2 * bit_of[bit])},
            device_id_type=mesh_id,
        )

    lines = ((in_all, in_ref), (out_all, out_ref), (x_all, x_ref))

    def line(index, side, hop):
        buffer, own = lines[index]
        ahead = 1 - 2 * side
        s = z - ahead * (hop - 1)
        view = place(buffer, s)
        return pltpu.make_async_remote_copy(
            src_ref=own if hop == 1 else view,
            dst_ref=view,
            send_sem=line_send.at[index, side, hop - 1],
            recv_sem=line_recv.at[index, side, hop - 1],
            device_id={"seq": z + ahead},
            device_id_type=mesh_id,
        )

    def line_wait(index, side, hop):
        view = place(lines[index][0], z - (1 - 2 * side) * hop)
        pltpu.make_async_remote_copy(
            src_ref=view,
            dst_ref=view,
            send_sem=line_send.at[index, side, hop - 1],
            recv_sem=line_recv.at[index, side, hop - 1],
            device_id={"seq": z - (1 - 2 * side)},
            device_id_type=mesh_id,
        ).wait_recv()

    def has_next(side):
        return z < seq_size - 1 if side == 0 else z > 0

    def has_block(side, hop):
        return z - hop >= 0 if side == 0 else z + hop < seq_size

    def proj(step):
        to = lax.rem(z + step, seq_size)
        return pltpu.make_async_remote_copy(
            src_ref=proj_ref.at[to],
            dst_ref=place(proj_all, z),
            send_sem=proj_send.at[step - 1],
            recv_sem=proj_recv.at[step - 1],
            device_id={"seq": to},
            device_id_type=mesh_id,
        )

    def proj_wait(step):
        view = place(proj_all, lax.rem(z + seq_size - step, seq_size))
        pltpu.make_async_remote_copy(
            src_ref=view,
            dst_ref=view,
            send_sem=proj_send.at[step - 1],
            recv_sem=proj_recv.at[step - 1],
            device_id={"seq": lax.rem(z + step, seq_size)},
            device_id_type=mesh_id,
        ).wait_recv()

    def turn_of(side, hop):
        return 0 if hop == 0 else 2 * hop - 1 + side

    def each_block(hop, act):
        act(0, lax.rem(z + seq_size - hop, seq_size), turn_of(0, hop))
        for index in (1, 2):
            if hop == 0:
                act(index, z, 0)
                continue
            for side in (0, 1):

                @pl.when(has_block(side, hop))
                def _(index=index, side=side):
                    act(index, z - (1 - 2 * side) * hop, turn_of(side, hop))

    owns = [
        pltpu.make_async_copy(own, place(buffer, z), own_sem.at[i])
        for i, (own, buffer) in enumerate(((proj_ref.at[z], proj_all), (in_ref, in_all), (out_ref, out_all), (x_ref, x_all)))
    ]
    for copy in owns:
        copy.start()
    for step in range(1, seq_size):
        proj(step).start()
    def send_own(index):
        for side in (0, 1):

            @pl.when(has_next(side))
            def _(side=side):
                line(index, side, 1).start()

    def arrive(index, hop):
        for side in (0, 1):

            @pl.when(has_block(side, hop))
            def _(side=side):
                line_wait(index, side, hop)
                if hop < seq_size - 1:

                    @pl.when(has_next(side))
                    def _():
                        line(index, side, hop + 1).start()

                if index < 2:
                    cube(index + 1, z - (1 - 2 * side) * hop, turn_of(side, hop), 0).start()

    def go_on(hop, step):
        def act(index, s, turn):
            cube(index, s, turn, step).wait()
            if step + 1 < count:
                cube(index, s, turn, step + 1).start()

        each_block(hop, act)

    def proj_arrive(hop):
        proj_wait(hop)
        cube(0, lax.rem(z + seq_size - hop, seq_size), turn_of(0, hop), 0).start()

    def own_cubes():
        for copy in owns:
            copy.wait()
        each_block(0, lambda index, s, turn: cube(index, s, turn, 0).start())

    acts = {"send": send_own, "own": own_cubes, "proj": proj_arrive, "arrive": arrive, "go": go_on}
    for name, *values in gather_plan(seq_size, count):
        acts[name](*values)
    for step in range(1, seq_size):
        proj(step).wait_send()
    for index in range(3):
        for side in (0, 1):
            for hop in range(1, seq_size):

                @pl.when(has_next(side) & has_block(side, hop - 1))
                def _(index=index, side=side, hop=hop):
                    line(index, side, hop).wait_send()


def start_gathers(proj, ffn_in, ffn_out, tokens_in):
    seq_size, fsdp_size = lax.axis_size("seq"), lax.axis_size("fsdp")
    bits = fsdp_bits(False)
    count = len(bits)

    def whole(shard):
        return jax.ShapeDtypeStruct((seq_size, *[2] * count, *shard), BF)

    turns = 2 * seq_size - 1
    dma = pltpu.SemaphoreType.DMA
    anywhere = pl.BlockSpec(memory_space=pl.ANY)
    outs = pl.pallas_call(
        functools.partial(gather_kernel, seq_size, bits),
        in_specs=[pl.BlockSpec(memory_space=pltpu.VMEM)] * 4,
        out_specs=[anywhere] * 4,
        out_shape=[
            whole(proj.shape[1:]),
            whole(ffn_in.shape),
            whole(ffn_out.shape),
            jax.ShapeDtypeStruct((seq_size, *tokens_in.shape), BF),
        ],
        scratch_shapes=[
            dma((4,)),
            dma((seq_size - 1,)),
            dma((seq_size - 1,)),
            dma((3, 2, seq_size - 1)),
            dma((3, 2, seq_size - 1)),
            dma((3, turns, count)),
            dma((3, turns, count)),
        ],
        compiler_params=pltpu.CompilerParams(collective_id=0, has_side_effects=True),
        cost_estimate=pl.CostEstimate(flops=0, bytes_accessed=100 * 2**20, transcendentals=0),
    )(proj, ffn_in, ffn_out, tokens_in)
    proj_all, in_all, out_all, inputs_all = outs
    flat = (seq_size, fsdp_size)
    return (
        proj_all.reshape(*flat, *proj.shape[1:]),
        in_all.reshape(*flat, *ffn_in.shape),
        out_all.reshape(*flat, *ffn_out.shape),
        inputs_all,
    )


def copy_into(target, index, term, rows=64, add=False):
    depth = target.shape[-2]
    rows = next(n for n in (rows, 48, 32, 16, depth) if depth % n == 0)
    lead = target.shape[len(index) : -2]
    count = 1
    for size in lead:
        count *= size

    def step(i, carry):
        block, place = i // (depth // rows), pl.multiple_of((i % (depth // rows)) * rows, rows)
        where = []
        for size in reversed(lead):
            where.insert(0, block % size)
            block = block // size
        at = (*where, pl.ds(place, rows), slice(None))
        value = term(at).astype(target.dtype)
        target[(*index, *at)] = target[(*index, *at)] + value if add else value
        return carry

    lax.fori_loop(0, count * (depth // rows), step, 0)


def add_into(target, index, term):
    copy_into(target, index, term, add=True)


def finish_plan(seq_size, count):
    last = count - 1
    steps = [[("add", 2 * row + i, step) for i in (0, 1)] for row in range(seq_size) for step in range(1, count)]
    steps.sort(key=lambda pair: (pair[0][1] // 2 + 1.2 * pair[0][2], pair[0][2]))
    ffn = [item for pair in steps for item in pair]
    halves = [2 * seq_size, 2 * seq_size + 1]
    proj = [("add", k, step) for step in range(count) for k in halves]
    plan = [("send", 0), ("open",)]
    share = -(-len(ffn) // (seq_size - 1))
    for hop in range(1, seq_size):
        chunk, ffn = ffn[:share], ffn[share:]
        if hop == seq_size - 1:
            plan += proj[:2]
            proj = proj[2:]
        plan += chunk[: share // 3] + [("arrive", 0, hop)] + chunk[share // 3 :]
    plan += [("send", 1), ("send", 2)]
    proj += [("proj",)]
    share = -(-len(proj) // (seq_size - 1))
    for hop in range(1, seq_size):
        plan += [*proj[:share], ("arrive", 1, hop), ("arrive", 2, hop)]
        proj = proj[share:]
    return plan + [("total", 0), ("total", 1), ("total", 2)]


def finish_kernel(seq_size, bits, da_ref, in_ref, in_added, out_ref, out_added, proj_ref, *refs):
    count = len(bits)
    da_out, in_out, out_out, proj_out = refs[:4]
    da_line, in_line, out_line = refs[4:7]
    in_parts, out_parts, proj_parts = (refs[7 + i * count : 7 + (i + 1) * count] for i in range(3))
    own_sem, keep_sem, line_send, line_recv, cube_send, cube_recv, proj_send, proj_recv = refs[7 + 3 * count :]
    z = lax.axis_index("seq")
    f = lax.axis_index("fsdp")
    bit_of = {bit: (f // bit) % 2 for bit in bits}
    mesh_id = pl.DeviceIdType.MESH
    last = seq_size - 1

    def flipped(bit):
        return {"fsdp": f + bit * (1 - 2 * bit_of[bit])}

    barrier = pltpu.get_barrier_semaphore()
    for step in range(1, seq_size):
        pl.semaphore_signal(barrier, inc=1, device_id={"seq": lax.rem(z + step, seq_size)}, device_id_type=mesh_id)
    for bit in bits:
        pl.semaphore_signal(barrier, inc=1, device_id=flipped(bit), device_id_type=mesh_id)
    pl.semaphore_wait(barrier, seq_size - 1 + count)

    lines = ((da_ref, da_line, da_out), (in_parts[-1], in_line, in_out), (out_parts[-1], out_line, out_out))

    def line(index, side, hop, own):
        terms, sums, _ = lines[index]
        if own:
            source = terms.at[seq_size - hop if side == 0 else hop - 1]
        else:
            source = sums.at[side, hop - 2]
        return pltpu.make_async_remote_copy(
            src_ref=source,
            dst_ref=sums.at[side, hop - 1],
            send_sem=line_send.at[index, side, hop - 1],
            recv_sem=line_recv.at[index, side, hop - 1],
            device_id={"seq": z + 1 - 2 * side},
            device_id_type=mesh_id,
        )

    def at_end(side):
        return z == 0 if side == 0 else z == last

    def from_end(side):
        return z if side == 0 else last - z

    def send_own(index):
        for side in (0, 1):

            @pl.when(at_end(side))
            def _(side=side):
                for hop in range(1, seq_size):
                    line(index, side, hop, True).start()

    def arrive(index, hop):
        terms, sums, _ = lines[index]
        for side in (0, 1):

            @pl.when((from_end(side) >= 1) & (from_end(side) <= hop))
            def _(side=side):
                pltpu.make_async_remote_copy(
                    src_ref=sums.at[side, hop - 1],
                    dst_ref=sums.at[side, hop - 1],
                    send_sem=line_send.at[index, side, hop - 1],
                    recv_sem=line_recv.at[index, side, hop - 1],
                    device_id={"seq": z - 1 + 2 * side},
                    device_id_type=mesh_id,
                ).wait_recv()
                if hop < last:
                    target = z - 1 + seq_size - hop if side == 0 else hop - last + z
                    add_into(sums, (side, hop - 1), lambda at: terms[(target, *at)])
                    line(index, side, hop + 1, False).start()

    def total(index):
        terms, sums, result = lines[index]
        add_first(result, lambda at: terms[(z, *at)])
        for side in (0, 1):

            @pl.when(from_end(side) >= 1)
            def _(side=side):
                add_into(result, (), lambda at: sums[(side, last - 1, *at)])

    def add_first(result, term):
        depth = result.shape[0]
        rows = next(n for n in (64, 32, 16, depth) if depth % n == 0)

        def step(i, carry):
            at = (pl.ds(pl.multiple_of(i * rows, rows), rows), slice(None))
            result[at] = term(at).astype(F32)
            return carry

        lax.fori_loop(0, depth // rows, step, 0)

    plain = bits[::-1]
    turned = plain[:1] + plain[:0:-1]
    some = seq_size // 2
    cubes = []
    for row in range(seq_size):
        cubes += [([in_ref, *in_parts], plain, row, 1), ([out_ref, *out_parts], turned, row, 1)]
    cubes += [([proj_ref, *proj_parts], plain, 0, some), ([proj_ref, *proj_parts], turned, some, seq_size - some)]

    def half_of(index, step, kept):
        states, order = cubes[index][:2]
        where = 1 + sorted(order[step:], reverse=True).index(order[step])
        return states[step], where, bit_of[order[step]] if kept else 1 - bit_of[order[step]]

    def rows_of(index):
        return pl.ds(cubes[index][2], cubes[index][3])

    def cube(index, step):
        source, where, bit = half_of(index, step, False)
        states, order = cubes[index][:2]
        return pltpu.make_async_remote_copy(
            src_ref=source.at[(rows_of(index),) + (slice(None),) * (where - 1) + (bit,)],
            dst_ref=states[step + 1].at[rows_of(index)],
            send_sem=cube_send.at[index, step],
            recv_sem=cube_recv.at[index, step],
            device_id=flipped(order[step]),
            device_id_type=mesh_id,
        )

    def cube_add(index, step):
        source, where, bit = half_of(index, step, True)
        states, _, offset, length = cubes[index]
        cube(index, step).wait()
        for row in range(offset, offset + length):
            add_into(states[step + 1], (row,), lambda at, row=row: source[(row, *at[: where - 1], bit, *at[where - 1 :])])
        if step + 1 < count:
            cube(index, step + 1).start()

    def keep(index):
        source, where, bit = half_of(index, 0, True)
        view = source.at[(rows_of(index),) + (slice(None),) * (where - 1) + (bit,)]
        return pltpu.make_async_copy(view, cubes[index][0][1].at[rows_of(index)], keep_sem.at[index])

    def open_cubes():
        for index in range(2 * seq_size):
            keep(index).start()
        for index in (2 * seq_size, 2 * seq_size + 1):
            cube(index, 0).start()
        for index in range(2 * seq_size):
            row, added = index // 2, (in_added, out_added)[index % 2]
            keep(index).wait()
            add_into(cubes[index][0][1], (row,), lambda at, row=row, added=added: added[(row, *at)])
            cube(index, 1).start()

    def proj(step):
        to = lax.rem(z + step, seq_size)
        return pltpu.make_async_remote_copy(
            src_ref=proj_parts[-1].at[to],
            dst_ref=proj_out.at[z],
            send_sem=proj_send.at[step - 1],
            recv_sem=proj_recv.at[step - 1],
            device_id={"seq": to},
            device_id_type=mesh_id,
        )

    def proj_wait(step):
        view = proj_out.at[lax.rem(z + seq_size - step, seq_size)]
        copy = pltpu.make_async_remote_copy(
            src_ref=view,
            dst_ref=view,
            send_sem=proj_send.at[step - 1],
            recv_sem=proj_recv.at[step - 1],
            device_id={"seq": lax.rem(z + step, seq_size)},
            device_id_type=mesh_id,
        )
        copy.wait_recv()

    def proj_start():
        pltpu.make_async_copy(proj_parts[-1].at[z], proj_out.at[z], own_sem).start()
        for step in range(1, seq_size):
            proj(step).start()

    acts = {"send": send_own, "open": open_cubes, "add": cube_add, "arrive": arrive, "proj": proj_start, "total": total}
    for name, *values in finish_plan(seq_size, count):
        acts[name](*values)
    pltpu.make_async_copy(proj_parts[-1].at[z], proj_out.at[z], own_sem).wait()
    for step in range(1, seq_size):
        proj_wait(step)
        proj(step).wait_send()
    for index in range(3):
        for side in (0, 1):
            for hop in range(1, seq_size):

                @pl.when(at_end(side) | ((from_end(side) >= 1) & (from_end(side) <= hop - 1)))
                def _(index=index, side=side, hop=hop):
                    line(index, side, hop, True).wait_send()


def finish_sums(da, ffin, ffout, proj):
    seq_size = lax.axis_size("seq")
    bits = fsdp_bits(False)
    count = len(bits)
    dma = pltpu.SemaphoreType.DMA
    inside, anywhere = pl.BlockSpec(memory_space=pltpu.VMEM), pl.BlockSpec(memory_space=pl.ANY)
    shapes = [v.shape[-2:] for v in (da, ffin[0], ffout[0])]

    def parts_of(shape, first):
        return [pltpu.VMEM((seq_size, *[2] * (count - step), *shape), BF) for step in range(first, count + 1)]

    return pl.pallas_call(
        functools.partial(finish_kernel, seq_size, bits),
        in_specs=[inside, anywhere, inside, anywhere, inside, inside],
        out_specs=[inside] * 4,
        out_shape=[jax.ShapeDtypeStruct(shape, F32) for shape in shapes]
        + [jax.ShapeDtypeStruct((seq_size, *proj.shape[-2:]), BF)],
        scratch_shapes=[
            *[pltpu.VMEM((2, seq_size - 1, *shape), BF) for shape in shapes],
            *parts_of(shapes[1], 1),
            *parts_of(shapes[2], 1),
            *parts_of(proj.shape[-2:], 1),
            dma,
            dma((2 * seq_size,)),
            dma((3, 2, seq_size - 1)),
            dma((3, 2, seq_size - 1)),
            dma((2 * seq_size + 2, count)),
            dma((2 * seq_size + 2, count)),
            dma((seq_size - 1,)),
            dma((seq_size - 1,)),
        ],
        compiler_params=pltpu.CompilerParams(
            collective_id=1, has_side_effects=True, vmem_limit_bytes=56 * 2**20
        ),
        cost_estimate=pl.CostEstimate(flops=0, bytes_accessed=100 * 2**20, transcendentals=0),
    )(da, *ffin, *ffout, proj)


def whole_tiles(shard, rows=16):
    return shard if shard.shape[0] % rows == 0 else shard.reshape(rows, -1)


def on_device(
    inputs,
    qkv_proj,
    out_proj,
    ffn_in,
    ffn_out,
    norm_gains,
    norm_biases,
    centroids,
    expert_in,
    expert_out,
    doc_lengths,
    routes,
    out_grad,
):
    rows, span, width = inputs.shape
    tokens = rows * span
    seq_size, fsdp_size = lax.axis_size("seq"), lax.axis_size("fsdp")
    here = lax.axis_index("seq")
    length = span * seq_size
    cols = width // seq_size
    capacity = max(2, 3 * tokens // (2 * fsdp_size))
    groups = seq_size // 2

    docs = doc_lengths.shape[1]
    key_pos = jnp.arange(length, dtype=jnp.int32)
    doc_ids = jnp.zeros((rows, length), jnp.int32)
    doc_end = jnp.zeros((rows, 1), jnp.int32)
    for j in range(docs - 1):
        doc_end = doc_end + doc_lengths[:, j : j + 1]
        doc_ids = doc_ids + (key_pos[None, :] >= doc_end).astype(jnp.int32)
    id_rows, id_cols = doc_ids[:, None, :], doc_ids[:, :, None]

    depth = out_proj.shape[0]
    wide = 3 * cols + width + LANES
    small = jnp.concatenate(
        [norm_gains.reshape(-1), norm_biases.reshape(-1), centroids[0], routes.reshape(tokens).astype(BF)]
    )
    small = jnp.pad(small, (0, depth * LANES - small.shape[0])).reshape(depth, LANES)
    slices = jnp.stack(
        [
            jnp.concatenate([*[qkv_proj[j, :, i * cols : (i + 1) * cols] for j in range(3)], out_proj, small], axis=1)
            for i in range(seq_size)
        ]
    )
    spare = -depth % 16
    bits = fsdp_bits(False)
    crossed = fsdp_bits(True)
    tokens_in = inputs.reshape(tokens, width)
    proj_all, ffin_all, ffout_all, inputs_all = start_gathers(
        jnp.pad(slices, ((0, 0), (0, spare), (0, 0))), whole_tiles(ffn_in), whole_tiles(ffn_out), tokens_in
    )
    inputs_all = inputs_all.reshape(seq_size * tokens, width)
    ffin_all, ffout_all = ffin_all.reshape(width, -1), ffout_all.reshape(-1, width)
    qkv_mine = proj_all[:, :, :depth, : 3 * cols].reshape(width, 3 * cols)
    out_all = proj_all[:, :, :depth, 3 * cols : 3 * cols + width].reshape(width, width)
    small = proj_all[:, :, :depth, 3 * cols + width :].reshape(seq_size, fsdp_size, -1)
    rows_of = small[:, :, : 6 * depth].astype(F32).reshape(-1, 6, depth).transpose(1, 0, 2).reshape(6, width)
    gain_rows, bias_rows = rows_of[:3], rows_of[3:]
    mine = small[:, :, 6 * depth : 6 * depth + cols]
    centroid = lax.dynamic_index_in_dim(mine, lax.axis_index("fsdp"), 1, keepdims=False).reshape(width)
    inputs_all, win_mine, wout_mine, dr_mine = tie(
        inputs_all, expert_in[0], expert_out[0], out_grad.reshape(tokens, width)
    )
    gains_pad, biases_pad = jnp.pad(gain_rows, ((0, 5), (0, 0))), jnp.pad(bias_rows, ((0, 5), (0, 0)))
    proj_used = proj_all if spare == 0 else proj_all[:, :, :depth, : 3 * cols]
    normed_flat, projected = project(inputs_all, gains_pad, biases_pad, proj_used, 3 * cols, tokens)
    projected = projected.reshape(seq_size, rows, span, 3 * cols)

    attended_mine, lse_rows = attend(projected, id_rows, id_cols)
    fsdp_here = lax.axis_index("fsdp")
    routes_all = small[:, :, 6 * depth + cols : 6 * depth + cols + tokens]
    routes_all = lax.dynamic_index_in_dim(routes_all, fsdp_here, 1, keepdims=False)
    later = (jnp.arange(tokens)[:, None] > jnp.arange(tokens)[None, :]).astype(BF)
    placings = []
    for group in range(groups):
        route = pick(routes_all, (here + seq_size - 2 * group) % seq_size).astype(jnp.int32)
        choose = route[:, None] == jnp.arange(fsdp_size, dtype=jnp.int32)[None, :]
        before = mm(later, choose.astype(BF))
        slot_rank = jnp.sum(jnp.where(choose, before, 0.0), axis=1).astype(jnp.int32)
        target = route * capacity + slot_rank
        slots = jnp.arange(fsdp_size * capacity, dtype=jnp.int32)
        placings.append((target[:, None] == slots[None, :]).astype(BF))
    grad_tokens = out_grad.reshape(tokens, width)

    def slots_of(placing, values):
        return mm_tn(placing, values).astype(BF).reshape(fsdp_size, capacity, width)

    def swap_slots(values):
        return lax.all_to_all(values, "fsdp", split_axis=0, concat_axis=0, tiled=True)

    def tokens_of(placing, values):
        return mm(placing, values.reshape(fsdp_size * capacity, width))

    win_half, wout_half = win_mine.shape[1] // 2, wout_mine.shape[0] // 2
    pair_in_low = seq_pair(win_mine[:, :win_half])
    grad_moved = [seq_shift(dr_mine, 2 * group) for group in range(1, groups)]
    grad_slots = [slots_of(placings[group], ([grad_tokens] + grad_moved)[group]) for group in range(groups)]
    grad_slots = jnp.concatenate(grad_slots, axis=1)
    attended_mine, pair_in_low, grad_slots = tie(attended_mine, pair_in_low, grad_slots)
    grad_slots = swap_slots(grad_slots)
    attended = seq_exchange(attended_mine)
    attended = attended.transpose(1, 2, 0, 3).reshape(tokens, width)
    attended, pair_in_high, pair_out_low, wout_high = tie(
        attended, win_mine[:, win_half:], wout_mine[:wout_half], wout_mine[wout_half:]
    )
    pair_in_high, pair_out_low = seq_pair(pair_in_high), seq_pair(pair_out_low)

    resid_in = tokens_in.astype(F32)
    middle = resid_in + mm(attended, out_all)
    hidden_low, active_low, active_slope, block_out, routed = ffn_forward(
        middle, gains_pad, biases_pad, ffin_all, ffout_all
    )
    routed, wout_high, pair_in_high, pair_out_low, grad_slots = tie(
        routed, wout_high, pair_in_high, pair_out_low, grad_slots
    )
    grad_slots = grad_slots.reshape(fsdp_size, groups, capacity, width)
    grad_slots = [grad_slots[:, group].reshape(-1, width) for group in range(groups)]
    slots_own = slots_of(placings[0], routed)
    pair_out_high = seq_pair(wout_high)

    own_mean, own_scale = norm_parts(resid_in)

    arrived = [swap_slots(slots_own).reshape(-1, width)]
    for group in range(1, groups):
        routed_here = seq_shift(routed, 2 * group)
        routed_here, pair_out_high, qkv_mine, own_mean, own_scale, *grad_slots = tie(
            routed_here, pair_out_high, qkv_mine, own_mean, own_scale, *grad_slots
        )
        slots_here = slots_of(placings[group], routed_here)
        slots_here, pair_out_high, *arrived = tie(slots_here, pair_out_high, *arrived)
        arrived.append(swap_slots(slots_here).reshape(-1, width))
    weights = (win_mine, wout_mine, pair_in_low, pair_in_high, pair_out_low, pair_out_high)
    shared, rows_grads, terms = (), [], []
    for group in range(groups):
        *shared, rows_grad, term = expert_block(
            group, groups, fsdp_size, arrived[group], grad_slots[group], centroid, weights, shared
        )
        rows_grads.append(rows_grad)
        terms.append(term)
    act, du, dz, arrived, gated_all = shared

    half = expert_in.shape[2]
    in_sent = mm_tn(arrived, du[:, half:]).astype(BF)
    back_low = [None] * groups
    for group in reversed(range(groups)):
        rows_grad = rows_grads[group].reshape(fsdp_size, capacity, width)
        if group + 1 < groups:
            rows_grad, back_low[group + 1] = tie(rows_grad, back_low[group + 1])
        back_slots = swap_slots(rows_grad)
        if group + 1 == groups:
            back_slots, in_sent = tie(back_slots, in_sent)
        back_low[group] = tokens_of(placings[group], back_slots)
        if group:
            back_low[group] = back_low[group].astype(BF)
    in_pair = seq_pair(in_sent)
    if groups > 1:
        gated_all, arrived, act, du, back_low[-1] = tie(gated_all, arrived, act, du, back_low[-1])
    back_sum = back_low[0]
    for group in range(1, groups):
        back_sum = back_sum + seq_shift(back_low[group], -2 * group).astype(F32)
    centroid_term = sum(term[0] for term in terms)
    out_sent = mm_tn(act[:, half:], dz).astype(BF)
    in_kept = mm_tn(arrived, du[:, :half])
    out_kept = mm_tn(act[:, :half], dz)

    gated_back = swap_slots(gated_all).reshape(fsdp_size, groups, capacity, width)
    out_terms = [tokens_of(placings[group], gated_back[:, group]) for group in range(groups)]
    out_terms = out_terms[:1] + [v.astype(BF) for v in out_terms[1:]]
    back_sum, out_sent, in_kept, out_kept = tie(back_sum, out_sent, in_kept, out_kept)

    block_low, hidden_grad, middle_grad, branch, dense_rows = ffn_backward(
        back_sum, block_out, grad_tokens, middle, gains_pad, active_slope, ffin_all, ffout_all
    )
    gain_three, bias_three, gain_two, bias_two = (dense_rows[i] for i in range(4))
    attended_grad = mm_nt(branch, out_all).astype(BF)
    attended_grad = attended_grad.reshape(rows, span, seq_size, cols).transpose(2, 0, 1, 3)
    attended_grad, in_pair, active_low, hidden_low, attended = tie(
        attended_grad, in_pair, active_low, hidden_low, attended
    )
    attended_grad = seq_exchange(attended_grad, True)

    def halved(term):
        terms = hyper_split(by_device(term))
        sent = lax.dynamic_index_in_dim(terms, 1 - fsdp_here % 2, terms.ndim - 3, keepdims=False)
        return terms, fsdp_flip(sent, 1)

    ffout_terms = halved(mm_tn(active_low, block_low))
    ffin_terms = mm_tn(hidden_low, hidden_grad).astype(BF)
    proj_terms = mm_tn(attended, branch).astype(BF).reshape(seq_size, fsdp_size, depth, width)
    def split(values):
        size = values.shape[0] // 8
        return values[: 4 * size], values[4 * size : 7 * size], values[7 * size :]

    def send_pieces(pieces):
        return [seq_pair(pieces[0])] + [seq_shift(pieces[group], -2 * group) for group in range(1, groups)]

    out_pieces = [split(values) for values in [out_sent, *out_terms[1:]]]
    sizes = len(out_pieces)
    attended_grad, *out_first = tie(attended_grad, *[pieces[0] for pieces in out_pieces])
    out_first = send_pieces(out_first)

    dq, dk, dv = attend_back(projected, attended_grad, lse_rows, id_rows, id_cols)
    projected_grad = jnp.concatenate([dq, dk, dv], axis=-1).reshape(seq_size * tokens, 3 * cols)
    projected_grad, inputs_all, in_kept, out_kept, proj_terms, ffin_terms, *moved = tie(
        projected_grad,
        inputs_all,
        in_kept,
        out_kept,
        proj_terms,
        ffin_terms,
        *out_first,
        *[pieces[1] for pieces in out_pieces],
    )
    ffin_terms = halved(ffin_terms)
    proj_terms = jnp.pad(proj_terms, ((0, 0), (0, 0), (0, spare), (3 * cols, LANES)))
    out_first, out_second = moved[:sizes], send_pieces(moved[sizes:])
    normed_low_terms = mm_nt(projected_grad, qkv_mine).astype(BF)
    normed_low_terms, *moved = tie(normed_low_terms, *out_second, *[pieces[2] for pieces in out_pieces])
    out_second, out_third = moved[:sizes], send_pieces(moved[sizes:])
    parts_all = norm_parts(inputs_all.astype(F32))
    unit_all = (inputs_all.astype(F32) - parts_all[0]) * parts_all[1]
    terms_wide = normed_low_terms.astype(F32)
    gain_one, bias_one = jnp.sum(terms_wide * unit_all, axis=0), jnp.sum(terms_wide, axis=0)
    small_terms = jnp.stack([gain_one, gain_two, gain_three, bias_one, bias_two, bias_three])

    qkv_term = mm_tn(normed_flat, projected_grad).astype(BF).reshape(seq_size, fsdp_size, depth, 3 * cols)
    small_rows = small_terms.astype(BF).reshape(6, seq_size, fsdp_size, depth).transpose(1, 2, 0, 3)
    centroid_rows = jnp.where(
        (jnp.arange(fsdp_size) == fsdp_here)[None, :, None], centroid_term.reshape(seq_size, 1, cols), 0.0
    )
    small_rows = jnp.concatenate([small_rows.reshape(seq_size, fsdp_size, 6 * depth), centroid_rows.astype(BF)], axis=2)
    small_rows = jnp.pad(small_rows, ((0, 0), (0, 0), (0, depth * LANES - small_rows.shape[2])))
    small_rows = small_rows.reshape(seq_size, fsdp_size, depth, LANES)
    proj_terms = lax.dynamic_update_slice(proj_terms, qkv_term, (0, 0, 0, 0))
    proj_terms = hyper_split(lax.dynamic_update_slice(proj_terms, small_rows, (0, 0, 0, 3 * cols + width)))
    proj_terms, *out_third = tie(proj_terms, *out_third)
    out_pair, *out_moved = [jnp.concatenate(v, axis=0) for v in zip(out_first, out_second, out_third, strict=True)]
    outputs = block_out + out_terms[0] + sum(v.astype(F32) for v in out_moved)
    outputs = outputs.astype(BF).reshape(rows, span, width)
    normed_one_grad, ffn_in_grad, ffn_out_grad, proj_sums = finish_sums(
        normed_low_terms.reshape(seq_size, tokens, width), ffin_terms, ffout_terms, proj_terms
    )
    ffn_in_grad, ffn_out_grad = ffn_in_grad.reshape(ffn_in.shape), ffn_out_grad.reshape(ffn_out.shape)
    proj_sums = proj_sums.astype(F32)
    qkv_grad = jnp.stack(
        [
            jnp.concatenate([proj_sums[i, :depth, j * cols : (j + 1) * cols] for i in range(seq_size)], axis=1)
            for j in range(3)
        ]
    )
    out_proj_grad = jnp.sum(proj_sums[:, :depth, 3 * cols : 3 * cols + width], axis=0)
    small = jnp.sum(proj_sums[:, :depth, 3 * cols + width :], axis=0).reshape(-1)
    small_grad = small[: 6 * depth].reshape(6, depth)
    centroids_grad = small[6 * depth : 6 * depth + cols][None]

    expert_in_grad = (in_kept + in_pair.astype(F32))[None]
    expert_out_grad = (out_kept + out_pair.astype(F32))[None]

    input_norm_grad, _, _ = norm_back(resid_in, (own_mean, own_scale), gain_rows[0], normed_one_grad)
    input_grad = (middle_grad + input_norm_grad).reshape(rows, span, width)
    return (
        outputs,
        input_grad,
        qkv_grad,
        out_proj_grad,
        ffn_in_grad,
        ffn_out_grad,
        small_grad[:3],
        small_grad[3:],
        centroids_grad,
        expert_in_grad,
        expert_out_grad,
    )


def solution(mesh):
    dense = P(("seq", "fsdp"), None)
    placed = (
        P("fsdp", "seq", None),
        P(None, ("seq", "fsdp"), None),
        dense,
        dense,
        dense,
        P(None, ("seq", "fsdp")),
        P(None, ("seq", "fsdp")),
        P("fsdp", "seq"),
        P("fsdp", None, "seq"),
        P("fsdp", "seq", None),
        P("fsdp", None),
        P("seq", "fsdp", None, None),
        P("fsdp", "seq", None),
    )
    returned = (
        P("fsdp", "seq", None),
        P("fsdp", "seq", None),
        P(None, ("seq", "fsdp"), None),
        dense,
        dense,
        dense,
        P(None, ("seq", "fsdp")),
        P(None, ("seq", "fsdp")),
        P("fsdp", "seq"),
        P("fsdp", None, "seq"),
        P("fsdp", "seq", None),
    )
    return jax.shard_map(on_device, mesh=mesh, in_specs=placed, out_specs=returned, check_vma=False)
```

```python
import functools

import jax
import jax.numpy as jnp
from jax import lax
from jax.experimental import pallas as pl
from jax.experimental.pallas import tpu as pltpu
from jax.sharding import PartitionSpec as P

HEAD_DIM = 64
LANES = 128
norm_eps = 1e-05
BF = jnp.bfloat16
F32 = jnp.float32


def layer_norm(values, gain_row, shift_row):
    average = jnp.mean(values, axis=-1, keepdims=True)
    centered = values - average
    variance = jnp.mean(centered * centered, axis=-1, keepdims=True)
    return centered * lax.rsqrt(variance + norm_eps) * gain_row + shift_row


def gelu_pair(values):
    cdf = 0.5 * (1.0 + lax.erf(values * (0.5**0.5)))
    pdf = 0.3989422804014327 * jnp.exp(-0.5 * values * values)
    return values * cdf, cdf + values * pdf


def mm(left, right):
    return jnp.dot(left, right, preferred_element_type=F32)


def mm_nt(left, right):
    return lax.dot_general(left, right, (((1,), (1,)), ((), ())), preferred_element_type=F32)


def mm_tn(left, right):
    return lax.dot_general(left, right, (((0,), (0,)), ((), ())), preferred_element_type=F32)


def norm_parts(values):
    average = jnp.mean(values, axis=-1, keepdims=True)
    centered = values - average
    variance = jnp.mean(centered * centered, axis=-1, keepdims=True)
    return average, lax.rsqrt(variance + norm_eps)


def norm_back(values, parts, gain_row, grads):
    average, scale = parts
    unit = (values - average) * scale
    unit_grad = grads * gain_row
    first = jnp.mean(unit_grad, axis=-1, keepdims=True)
    second = jnp.mean(unit_grad * unit, axis=-1, keepdims=True)
    return scale * (unit_grad - first - unit * second), jnp.sum(grads * unit, axis=0), jnp.sum(grads, axis=0)


def tie(*values):
    return lax.optimization_barrier(values)


def seq_shift(values, step):
    size = lax.axis_size("seq")
    return lax.ppermute(values, "seq", [(i, (i + step) % size) for i in range(size)])


def seq_pair(values):
    size = lax.axis_size("seq")
    return lax.ppermute(values, "seq", [(i, i ^ 1) for i in range(size)])


def put(buffer, values, place):
    return lax.dynamic_update_index_in_dim(buffer, values, place, 0)


def pick(values, place):
    return lax.dynamic_index_in_dim(values, place, 0, keepdims=False)


def seq_exchange(values, chained=False):
    size = lax.axis_size("seq")
    here = lax.axis_index("seq")
    result = put(jnp.zeros_like(values), pick(values, here), here)
    arrived = None
    for step in range(1, size):
        sent = pick(values, (here + step) % size)
        if chained and arrived is not None:
            sent, arrived = tie(sent, arrived)
        if arrived is not None:
            result = put(result, arrived, (here - step + 1) % size)
        arrived = seq_shift(sent, step)
    return put(result, arrived, (here - size + 1) % size)


def seq_sum_scatter(values):
    size = lax.axis_size("seq")
    here = lax.axis_index("seq")
    total = pick(values, here).astype(F32)
    for step in range(1, size):
        arrived = seq_shift(pick(values, (here + step) % size).astype(BF), step)
        total = total + arrived.astype(F32)
    return total


def masked_pair(block):
    lane = lax.broadcasted_iota(jnp.int32, block.shape, 1)
    zero = jnp.zeros_like(block)
    return jnp.where(lane < HEAD_DIM, block, zero), jnp.where(lane < HEAD_DIM, zero, block)


def allowed_block(id_col, id_row, start, size, end):
    key_pos = lax.broadcasted_iota(jnp.int32, (end, size), 0)
    query_pos = start + lax.broadcasted_iota(jnp.int32, (end, size), 1)
    return (id_col[:end, :] == id_row[:, start:end]) & (key_pos <= query_pos)


def attend_kernel(size, q_ref, k_ref, v_ref, id_row_ref, id_col_ref, o_ref, lse_ref, o_all):
    length = id_row_ref.shape[-1]
    queries = q_ref[...].reshape(length, LANES) * jnp.asarray(HEAD_DIM**-0.5, BF)
    keys = k_ref[...].reshape(length, LANES)
    values_t = v_ref[...].reshape(length, LANES).T
    id_row = id_row_ref[0]
    id_col = id_col_ref[0]
    for start in range(0, length, size):
        end = start + size
        mask = allowed_block(id_col, id_row, start, size, end)
        parts = []
        for head, query in enumerate(masked_pair(queries[start:end])):
            scores = jnp.where(mask, mm_nt(keys[:end], query), -1e30)
            top = jnp.max(scores, axis=0, keepdims=True)
            powers = jnp.exp(scores - top)
            whole = jnp.sum(powers, axis=0, keepdims=True)
            weights = (powers * (1.0 / whole)).astype(BF)
            lse_ref[0, 0, pl.ds(head, 1), pl.ds(start, size)] = top + jnp.log(whole)
            part = values_t[head * HEAD_DIM : (head + 1) * HEAD_DIM, :end]
            parts.append(mm(part, weights))
        o_all[pl.ds(start, size), :] = jnp.concatenate(parts, axis=0).T
    o_ref[...] = o_all[...].astype(BF).reshape(o_ref.shape)


def attend_back_kernel(
    size, q_ref, k_ref, v_ref, do_ref, lse_ref, id_row_ref, id_col_ref, dq_ref, dk_ref, dv_ref, dq_all, dk_all, dv_all
):
    length = id_row_ref.shape[-1]
    scale = HEAD_DIM**-0.5
    queries = q_ref[...].reshape(length, LANES) * jnp.asarray(scale, BF)
    keys = k_ref[...].reshape(length, LANES)
    keys_t = keys.T
    values = v_ref[...].reshape(length, LANES)
    grads = do_ref[...].reshape(length, LANES)
    id_row = id_row_ref[0]
    id_col = id_col_ref[0]
    dk_all[...] = jnp.zeros_like(dk_all)
    dv_all[...] = jnp.zeros_like(dv_all)
    for start in range(0, length, size):
        end = start + size
        mask = allowed_block(id_col, id_row, start, size, end)
        parts = []
        heads = zip(masked_pair(queries[start:end]), masked_pair(grads[start:end]), strict=True)
        for head, (query, grad) in enumerate(heads):
            scores = jnp.where(mask, mm_nt(keys[:end], query), -1e30)
            probs = jnp.exp(scores - lse_ref[0, 0, pl.ds(head, 1), pl.ds(start, size)])
            prob_grad = mm_nt(values[:end], grad)
            total = jnp.sum(probs * prob_grad, axis=0, keepdims=True)
            score_grad = (probs * (prob_grad - total)).astype(BF)
            dv_all[pl.ds(0, end), :] += mm(probs.astype(BF), grad)
            dk_all[pl.ds(0, end), :] += mm(score_grad, query)
            parts.append(mm(keys_t[head * HEAD_DIM : (head + 1) * HEAD_DIM, :end], score_grad))
        dq_all[pl.ds(start, size), :] = jnp.concatenate(parts, axis=0).T * scale
    dq_ref[...] = dq_all[...].astype(BF).reshape(dq_ref.shape)
    dk_ref[...] = dk_all[...].astype(BF).reshape(dk_ref.shape)
    dv_ref[...] = dv_all[...].astype(BF).reshape(dv_ref.shape)


def attention_specs(projected, length):
    blocks, rows, span, width3 = projected.shape
    columns = width3 // 3 // LANES

    def part(index):
        return pl.BlockSpec((blocks, 1, span, LANES), lambda r, c: (0, r, 0, index * columns + c))

    id_row = pl.BlockSpec((1, 1, length), lambda r, c: (r, 0, 0))
    id_col = pl.BlockSpec((1, length, 1), lambda r, c: (r, 0, 0))
    lse = pl.BlockSpec((1, 1, 2, length), lambda r, c: (r, c, 0, 0))
    return rows, columns, part, id_row, id_col, lse


def attend(projected, id_rows, id_cols):
    length = id_rows.shape[-1]
    blocks, rows, span, width3 = projected.shape
    rows, columns, part, id_row, id_col, lse = attention_specs(projected, length)
    return pl.pallas_call(
        functools.partial(attend_kernel, min(256, length)),
        grid=(rows, columns),
        in_specs=[part(0), part(1), part(2), id_row, id_col],
        out_specs=[part(0), lse],
        out_shape=[
            jax.ShapeDtypeStruct((blocks, rows, span, width3 // 3), BF),
            jax.ShapeDtypeStruct((rows, columns, 2, length), F32),
        ],
        scratch_shapes=[pltpu.VMEM((length, LANES), F32)],
        compiler_params=pltpu.CompilerParams(vmem_limit_bytes=40 * 2**20),
        cost_estimate=pl.CostEstimate(flops=10**6, bytes_accessed=2**16, transcendentals=0),
    )(projected, projected, projected, id_rows, id_cols)


def attend_back(projected, grads, lse_rows, id_rows, id_cols):
    length = id_rows.shape[-1]
    blocks, rows, span, width3 = projected.shape
    rows, columns, part, id_row, id_col, lse = attention_specs(projected, length)
    shape = jax.ShapeDtypeStruct((blocks, rows, span, width3 // 3), BF)
    return pl.pallas_call(
        functools.partial(attend_back_kernel, min(256, length)),
        grid=(rows, columns),
        in_specs=[part(0), part(1), part(2), part(0), lse, id_row, id_col],
        out_specs=[part(0)] * 3,
        out_shape=[shape] * 3,
        scratch_shapes=[pltpu.VMEM((length, LANES), F32)] * 3,
        compiler_params=pltpu.CompilerParams(vmem_limit_bytes=48 * 2**20),
        cost_estimate=pl.CostEstimate(flops=10**6, bytes_accessed=2**16, transcendentals=0),
    )(projected, projected, projected, grads, lse_rows, id_rows, id_cols)


def fsdp_flip(values, bit):
    size = lax.axis_size("fsdp")
    return lax.ppermute(values, "fsdp", [(i, i ^ bit) for i in range(size)])


def fsdp_bits(crossed):
    bits = [1 << i for i in range(1, lax.axis_size("fsdp").bit_length() - 1)]
    return (bits[::-1] if crossed else bits) + [1]


def hyper_split(parts):
    count = parts.shape[1].bit_length() - 1
    return parts.reshape(parts.shape[0], *[2] * count, *parts.shape[2:])


def by_device(term):
    seq_size, fsdp_size = lax.axis_size("seq"), lax.axis_size("fsdp")
    depth = term.shape[0] // (seq_size * fsdp_size)
    tile = (depth, term.shape[1]) if depth % 16 == 0 else (16, depth * term.shape[1] // 16)
    return term.astype(BF).reshape(seq_size, fsdp_size, *tile)


def project_kernel(x_ref, gains_ref, biases_ref, w_ref, normed_ref, out_ref):
    x = x_ref[...].astype(F32)
    average, scale = norm_parts(x)
    normed = ((x - average) * scale * gains_ref[0:1] + biases_ref[0:1]).astype(BF)
    normed_ref[...] = normed
    out_ref[...] = mm(normed, w_ref[...].reshape(x.shape[1], w_ref.shape[-1])).astype(BF)


def project(inputs_all, gains, biases, weights, columns, tokens):
    width = inputs_all.shape[1]
    row = pl.BlockSpec((8, width), lambda i: (0, 0))
    return pl.pallas_call(
        project_kernel,
        grid=(inputs_all.shape[0] // tokens,),
        in_specs=[
            pl.BlockSpec((tokens, width), lambda i: (i, 0)),
            row,
            row,
            pl.BlockSpec((*weights.shape[:3], columns), lambda i: (0, 0, 0, 0)),
        ],
        out_specs=[pl.BlockSpec((tokens, width), lambda i: (i, 0)), pl.BlockSpec((tokens, columns), lambda i: (i, 0))],
        out_shape=[
            jax.ShapeDtypeStruct(inputs_all.shape, BF),
            jax.ShapeDtypeStruct((inputs_all.shape[0], columns), BF),
        ],
        compiler_params=pltpu.CompilerParams(vmem_limit_bytes=40 * 2**20),
        cost_estimate=pl.CostEstimate(flops=10**6, bytes_accessed=2**16, transcendentals=0),
    )(inputs_all, gains, biases, weights)


def ffn_kernel(middle_ref, gains_ref, biases_ref, win_ref, wout_ref, normed_ref, act_ref, slope_ref, block_ref, routed_ref):
    chunk = pl.program_id(0)

    def norm(values, row):
        average, scale = norm_parts(values)
        return ((values - average) * scale * gains_ref[row : row + 1] + biases_ref[row : row + 1]).astype(BF)

    @pl.when(chunk == 0)
    def _():
        normed_ref[...] = norm(middle_ref[...], 1)
        block_ref[...] = middle_ref[...]

    act, slope = gelu_pair(mm(normed_ref[...], win_ref[...]))
    act = act.astype(BF)
    act_ref[...] = act
    slope_ref[...] = slope.astype(BF)
    block_ref[...] += mm(act, wout_ref[...])

    @pl.when(chunk == pl.num_programs(0) - 1)
    def _():
        routed_ref[...] = norm(block_ref[...], 2)


def ffn_specs(tokens, width, hidden):
    size = min(512, hidden)
    whole = pl.BlockSpec((tokens, width), lambda j: (0, 0))
    piece = pl.BlockSpec((tokens, size), lambda j: (0, j))
    row = pl.BlockSpec((8, width), lambda j: (0, 0))
    return size, whole, piece, row, [
        pl.BlockSpec((width, size), lambda j: (0, j)),
        pl.BlockSpec((size, width), lambda j: (j, 0)),
    ]


def ffn_forward(middle, gains, biases, win, wout):
    tokens, width = middle.shape
    hidden = win.shape[1]
    size, whole, piece, row, weights = ffn_specs(tokens, width, hidden)
    low, wide = jax.ShapeDtypeStruct((tokens, width), BF), jax.ShapeDtypeStruct((tokens, hidden), BF)
    return pl.pallas_call(
        ffn_kernel,
        grid=(hidden // size,),
        in_specs=[whole, row, row, *weights],
        out_specs=[whole, piece, piece, whole, whole],
        out_shape=[low, wide, wide, jax.ShapeDtypeStruct((tokens, width), F32), low],
        compiler_params=pltpu.CompilerParams(vmem_limit_bytes=48 * 2**20),
        cost_estimate=pl.CostEstimate(flops=10**6, bytes_accessed=2**16, transcendentals=0),
    )(middle, gains, biases, win, wout)


def ffn_back_kernel(
    back_ref, block_ref, grad_ref, middle_ref, gains_ref, slope_ref, win_ref, wout_ref,
    low_ref, du_ref, dh_ref, branch_ref, terms_ref, total,
):
    chunk = pl.program_id(0)

    def norm_grad(values, row, grads):
        moved, gain, bias = norm_back(values, norm_parts(values), gains_ref[row : row + 1], grads)
        return moved, gain[None], bias[None]

    @pl.when(chunk == 0)
    def _():
        moved, gain, bias = norm_grad(block_ref[...], 2, back_ref[...])
        grads = grad_ref[...].astype(F32) + moved
        dh_ref[...] = grads
        low_ref[...] = grads.astype(BF)
        terms_ref[0:1] = gain
        terms_ref[1:2] = bias
        total[...] = jnp.zeros_like(total)

    du = (slope_ref[...].astype(F32) * mm_nt(low_ref[...], wout_ref[...])).astype(BF)
    du_ref[...] = du
    total[...] += mm_nt(du, win_ref[...])

    @pl.when(chunk == pl.num_programs(0) - 1)
    def _():
        moved, gain, bias = norm_grad(middle_ref[...], 1, total[...])
        grads = dh_ref[...] + moved
        dh_ref[...] = grads
        branch_ref[...] = grads.astype(BF)
        terms_ref[2:3] = gain
        terms_ref[3:4] = bias


def ffn_backward(back, block_out, grads, middle, gains, slope, win, wout):
    tokens, width = middle.shape
    hidden = win.shape[1]
    size, whole, piece, row, weights = ffn_specs(tokens, width, hidden)
    low, wide = jax.ShapeDtypeStruct((tokens, width), BF), jax.ShapeDtypeStruct((tokens, hidden), BF)
    f32 = jax.ShapeDtypeStruct((tokens, width), F32)
    return pl.pallas_call(
        ffn_back_kernel,
        grid=(hidden // size,),
        in_specs=[whole, whole, whole, whole, row, piece, *weights],
        out_specs=[whole, piece, whole, whole, row],
        out_shape=[low, wide, f32, low, jax.ShapeDtypeStruct((8, width), F32)],
        scratch_shapes=[pltpu.VMEM((tokens, width), F32)],
        compiler_params=pltpu.CompilerParams(vmem_limit_bytes=48 * 2**20),
        cost_estimate=pl.CostEstimate(flops=10**6, bytes_accessed=2**16, transcendentals=0),
    )(back, block_out, grads, middle, gains, slope, win, wout)


def expert_kernel(x_ref, dr_ref, centroid_ref, win_own, wout_own, win_low, win_high, wout_low, wout_high, *refs):
    act_ref, du_ref, dz_ref, all_ref, gated_ref, dx_ref, term_ref, total, back, win_ref, wout_ref = refs[-11:]
    groups_of = gated_ref.shape
    chunk = pl.program_id(0)
    own = pl.num_programs(0) - 2
    for here, win_part, wout_part in (
        (chunk < own, win_own, wout_own),
        (chunk == own, win_low, wout_low),
        (chunk == own + 1, win_high, wout_high),
    ):

        @pl.when(here)
        def _(win_part=win_part, wout_part=wout_part):
            win_ref[...] = win_part[...]
            wout_ref[...] = wout_part[...]

    x = x_ref[...]

    def gate_of():
        logits = mm_nt(x, centroid_ref[...])[:, :1]
        return 1.0 / (1.0 + jnp.exp(-logits))

    @pl.when(chunk == 0)
    def _():
        dz_ref[...] = (gate_of() * dr_ref[...].astype(F32)).astype(BF)
        all_ref[...] = x
        total[...] = jnp.zeros_like(total)
        back[...] = jnp.zeros_like(back)

    act, slope = gelu_pair(mm(x, win_ref[...]))
    act = act.astype(BF)
    act_ref[...] = act
    total[...] += mm(act, wout_ref[...])
    du = (slope * mm_nt(dz_ref[...], wout_ref[...])).astype(BF)
    du_ref[...] = du
    back[...] += mm_nt(du, win_ref[...])

    @pl.when(chunk == pl.num_programs(0) - 1)
    def _():
        gate = gate_of()
        result = total[...]
        gated_ref[...] = (gate * result).astype(BF).reshape(groups_of)
        dl = jnp.sum(dr_ref[...].astype(F32) * result, axis=1, keepdims=True) * gate * (1.0 - gate)
        dx_ref[...] = (back[...] + dl * centroid_ref[:16].astype(F32)[:1]).astype(BF)
        term_ref[...] = jnp.broadcast_to(jnp.sum(dl * x.astype(F32), axis=0, keepdims=True), term_ref.shape)


def expert_block(group, groups, blocks, arrived, grads, centroid, weights, earlier):
    slots, width = arrived.shape
    size = weights[2].shape[1]
    own = weights[0].shape[1] // size
    hidden = (own + 2) * size
    whole = pl.BlockSpec((slots, width), lambda j: (0, 0))
    shared = pl.BlockSpec((slots, width), lambda j: (group, 0))
    piece = pl.BlockSpec((slots, size), lambda j: (group, j))
    row = pl.BlockSpec((LANES, width), lambda j: (0, 0))
    term = pl.BlockSpec((8, width), lambda j: (0, 0))
    win_piece = pl.BlockSpec((width, size), lambda j: (0, 0))
    wout_piece = pl.BlockSpec((size, width), lambda j: (0, 0))
    return pl.pallas_call(
        expert_kernel,
        grid=(own + 2,),
        in_specs=[
            whole,
            whole,
            row,
            pl.BlockSpec((width, size), lambda j: (0, jnp.minimum(j, own - 1))),
            pl.BlockSpec((size, width), lambda j: (jnp.minimum(j, own - 1), 0)),
            win_piece,
            win_piece,
            wout_piece,
            wout_piece,
            *[pl.BlockSpec(memory_space=pl.ANY)] * len(earlier),
        ],
        out_specs=[
            piece,
            piece,
            shared,
            shared,
            pl.BlockSpec((blocks, slots // blocks, width), lambda j: (0, group, 0)),
            whole,
            term,
        ],
        out_shape=[jax.ShapeDtypeStruct((groups * slots, hidden), BF)] * 2
        + [jax.ShapeDtypeStruct((groups * slots, width), BF)] * 2
        + [jax.ShapeDtypeStruct((blocks, groups * slots // blocks, width), BF)]
        + [jax.ShapeDtypeStruct((slots, width), BF)]
        + [jax.ShapeDtypeStruct((8, width), F32)],
        scratch_shapes=[pltpu.VMEM((slots, width), F32)] * 2
        + [pltpu.VMEM((width, size), BF), pltpu.VMEM((size, width), BF)],
        input_output_aliases={9 + i: i for i in range(len(earlier))},
        compiler_params=pltpu.CompilerParams(vmem_limit_bytes=48 * 2**20),
        cost_estimate=pl.CostEstimate(flops=10**6, bytes_accessed=2**16, transcendentals=0),
    )(arrived, grads, jnp.broadcast_to(centroid[None], (LANES, width)), *weights, *earlier)


def gather_plan(seq_size, count):
    plan = [("send", 0), ("send", 1), ("own",)]
    for hop in range(1, seq_size):
        plan += [("proj", hop), ("arrive", 0, hop), ("arrive", 1, hop)]
        if hop == 1:
            plan += [("send", 2)]
        if hop < seq_size - 1:
            plan += [("go", hop - 1, 0)]
    last = seq_size - 1
    rest = [("go", 0, 1), ("go", last - 1, 0), ("go", 1, 1), ("go", last, 0)]
    rest += [("go", hop, step) for step in range(1, count - 1) for hop in range(2 if step == 1 else 0, seq_size)]
    plan += [("arrive", 2, 1), *rest[:4]]
    rest = rest[4:]
    share = -(-len(rest) // max(1, seq_size - 2))
    for hop in range(2, seq_size):
        plan += [("arrive", 2, hop), *rest[(hop - 2) * share : (hop - 1) * share]]
    return plan + [("go", hop, count - 1) for hop in range(seq_size)]


def gather_kernel(seq_size, bits, proj_ref, in_ref, out_ref, x_ref, proj_all, in_all, out_all, x_all, *sems):
    own_sem, proj_send, proj_recv, line_send, line_recv, cube_send, cube_recv = sems
    z = lax.axis_index("seq")
    f = lax.axis_index("fsdp")
    count = len(bits)
    high_first = sorted(bits, reverse=True)
    bit_of = {bit: (f // bit) % 2 for bit in bits}
    mesh_id = pl.DeviceIdType.MESH

    barrier = pltpu.get_barrier_semaphore()
    for step in range(1, seq_size):
        pl.semaphore_signal(barrier, inc=1, device_id={"seq": lax.rem(z + step, seq_size)}, device_id_type=mesh_id)
    for bit in bits:
        pl.semaphore_signal(barrier, inc=1, device_id={"fsdp": f + bit * (1 - 2 * bit_of[bit])}, device_id_type=mesh_id)
    pl.semaphore_wait(barrier, seq_size - 1 + count)

    def place(buffer, s, done=()):
        if buffer is x_all:
            return buffer.at[s]
        return buffer.at[(s, *(slice(None) if bit in done else bit_of[bit] for bit in high_first))]

    def order_of(index, turn):
        return bits if (index + turn) % 2 == 0 else bits[-2::-1] + bits[-1:]

    cubes = ((proj_all, 0), (in_all, 0), (out_all, 1))

    def cube(index, s, turn, step):
        buffer, crossed = cubes[index]
        order = order_of(crossed, turn if index == 0 else 0)
        view = place(buffer, s, order[:step])
        bit = order[step]
        return pltpu.make_async_remote_copy(
            src_ref=view,
            dst_ref=view,
            send_sem=cube_send.at[index, turn, step],
            recv_sem=cube_recv.at[index, turn, step],
            device_id={"fsdp": f + bit * (1 - 2 * bit_of[bit])},
            device_id_type=mesh_id,
        )

    lines = ((in_all, in_ref), (out_all, out_ref), (x_all, x_ref))

    def line(index, side, hop):
        buffer, own = lines[index]
        ahead = 1 - 2 * side
        s = z - ahead * (hop - 1)
        view = place(buffer, s)
        return pltpu.make_async_remote_copy(
            src_ref=own if hop == 1 else view,
            dst_ref=view,
            send_sem=line_send.at[index, side, hop - 1],
            recv_sem=line_recv.at[index, side, hop - 1],
            device_id={"seq": z + ahead},
            device_id_type=mesh_id,
        )

    def line_wait(index, side, hop):
        view = place(lines[index][0], z - (1 - 2 * side) * hop)
        pltpu.make_async_remote_copy(
            src_ref=view,
            dst_ref=view,
            send_sem=line_send.at[index, side, hop - 1],
            recv_sem=line_recv.at[index, side, hop - 1],
            device_id={"seq": z - (1 - 2 * side)},
            device_id_type=mesh_id,
        ).wait_recv()

    def has_next(side):
        return z < seq_size - 1 if side == 0 else z > 0

    def has_block(side, hop):
        return z - hop >= 0 if side == 0 else z + hop < seq_size

    def proj(step):
        to = lax.rem(z + step, seq_size)
        return pltpu.make_async_remote_copy(
            src_ref=proj_ref.at[to],
            dst_ref=place(proj_all, z),
            send_sem=proj_send.at[step - 1],
            recv_sem=proj_recv.at[step - 1],
            device_id={"seq": to},
            device_id_type=mesh_id,
        )

    def proj_wait(step):
        view = place(proj_all, lax.rem(z + seq_size - step, seq_size))
        pltpu.make_async_remote_copy(
            src_ref=view,
            dst_ref=view,
            send_sem=proj_send.at[step - 1],
            recv_sem=proj_recv.at[step - 1],
            device_id={"seq": lax.rem(z + step, seq_size)},
            device_id_type=mesh_id,
        ).wait_recv()

    def turn_of(side, hop):
        return 0 if hop == 0 else 2 * hop - 1 + side

    def each_block(hop, act):
        act(0, lax.rem(z + seq_size - hop, seq_size), turn_of(0, hop))
        for index in (1, 2):
            if hop == 0:
                act(index, z, 0)
                continue
            for side in (0, 1):

                @pl.when(has_block(side, hop))
                def _(index=index, side=side):
                    act(index, z - (1 - 2 * side) * hop, turn_of(side, hop))

    owns = [
        pltpu.make_async_copy(own, place(buffer, z), own_sem.at[i])
        for i, (own, buffer) in enumerate(((proj_ref.at[z], proj_all), (in_ref, in_all), (out_ref, out_all), (x_ref, x_all)))
    ]
    for copy in owns:
        copy.start()
    for step in range(1, seq_size):
        proj(step).start()
    def send_own(index):
        for side in (0, 1):

            @pl.when(has_next(side))
            def _(side=side):
                line(index, side, 1).start()

    def arrive(index, hop):
        for side in (0, 1):

            @pl.when(has_block(side, hop))
            def _(side=side):
                line_wait(index, side, hop)
                if hop < seq_size - 1:

                    @pl.when(has_next(side))
                    def _():
                        line(index, side, hop + 1).start()

                if index < 2:
                    cube(index + 1, z - (1 - 2 * side) * hop, turn_of(side, hop), 0).start()

    def go_on(hop, step):
        def act(index, s, turn):
            cube(index, s, turn, step).wait()
            if step + 1 < count:
                cube(index, s, turn, step + 1).start()

        each_block(hop, act)

    def proj_arrive(hop):
        proj_wait(hop)
        cube(0, lax.rem(z + seq_size - hop, seq_size), turn_of(0, hop), 0).start()

    def own_cubes():
        for copy in owns:
            copy.wait()
        each_block(0, lambda index, s, turn: cube(index, s, turn, 0).start())

    acts = {"send": send_own, "own": own_cubes, "proj": proj_arrive, "arrive": arrive, "go": go_on}
    for name, *values in gather_plan(seq_size, count):
        acts[name](*values)
    for step in range(1, seq_size):
        proj(step).wait_send()
    for index in range(3):
        for side in (0, 1):
            for hop in range(1, seq_size):

                @pl.when(has_next(side) & has_block(side, hop - 1))
                def _(index=index, side=side, hop=hop):
                    line(index, side, hop).wait_send()


def start_gathers(proj, ffn_in, ffn_out, tokens_in):
    seq_size, fsdp_size = lax.axis_size("seq"), lax.axis_size("fsdp")
    bits = fsdp_bits(False)
    count = len(bits)

    def whole(shard):
        return jax.ShapeDtypeStruct((seq_size, *[2] * count, *shard), BF)

    turns = 2 * seq_size - 1
    dma = pltpu.SemaphoreType.DMA
    anywhere = pl.BlockSpec(memory_space=pl.ANY)
    outs = pl.pallas_call(
        functools.partial(gather_kernel, seq_size, bits),
        in_specs=[pl.BlockSpec(memory_space=pltpu.VMEM)] * 4,
        out_specs=[anywhere] * 4,
        out_shape=[
            whole(proj.shape[1:]),
            whole(ffn_in.shape),
            whole(ffn_out.shape),
            jax.ShapeDtypeStruct((seq_size, *tokens_in.shape), BF),
        ],
        scratch_shapes=[
            dma((4,)),
            dma((seq_size - 1,)),
            dma((seq_size - 1,)),
            dma((3, 2, seq_size - 1)),
            dma((3, 2, seq_size - 1)),
            dma((3, turns, count)),
            dma((3, turns, count)),
        ],
        compiler_params=pltpu.CompilerParams(collective_id=0, has_side_effects=True),
        cost_estimate=pl.CostEstimate(flops=0, bytes_accessed=100 * 2**20, transcendentals=0),
    )(proj, ffn_in, ffn_out, tokens_in)
    proj_all, in_all, out_all, inputs_all = outs
    flat = (seq_size, fsdp_size)
    return (
        proj_all.reshape(*flat, *proj.shape[1:]),
        in_all.reshape(*flat, *ffn_in.shape),
        out_all.reshape(*flat, *ffn_out.shape),
        inputs_all,
    )


def copy_into(target, index, term, rows=64, add=False):
    depth = target.shape[-2]
    rows = next(n for n in (rows, 48, 32, 16, depth) if depth % n == 0)
    lead = target.shape[len(index) : -2]
    count = 1
    for size in lead:
        count *= size

    def step(i, carry):
        block, place = i // (depth // rows), pl.multiple_of((i % (depth // rows)) * rows, rows)
        where = []
        for size in reversed(lead):
            where.insert(0, block % size)
            block = block // size
        at = (*where, pl.ds(place, rows), slice(None))
        value = term(at).astype(target.dtype)
        target[(*index, *at)] = target[(*index, *at)] + value if add else value
        return carry

    lax.fori_loop(0, count * (depth // rows), step, 0)


def add_into(target, index, term):
    copy_into(target, index, term, add=True)


def finish_plan(seq_size, count):
    last = count - 1
    steps = [[("add", 2 * row + i, step) for i in (0, 1)] for row in range(seq_size) for step in range(1, count)]
    steps.sort(key=lambda pair: (pair[0][1] // 2 + 1.2 * pair[0][2], pair[0][2]))
    ffn = [item for pair in steps for item in pair]
    halves = [2 * seq_size, 2 * seq_size + 1]
    proj = [("add", k, step) for step in range(count) for k in halves]
    plan = [("send", 0), ("open",)]
    share = -(-len(ffn) // (seq_size - 1))
    for hop in range(1, seq_size):
        chunk, ffn = ffn[:share], ffn[share:]
        if hop == seq_size - 1:
            plan += proj[:2]
            proj = proj[2:]
        plan += chunk[: share // 3] + [("arrive", 0, hop)] + chunk[share // 3 :]
    plan += [("send", 1), ("send", 2)]
    proj += [("proj",)]
    share = -(-len(proj) // (seq_size - 1))
    for hop in range(1, seq_size):
        plan += [*proj[:share], ("arrive", 1, hop), ("arrive", 2, hop)]
        proj = proj[share:]
    return plan + [("total", 0), ("total", 1), ("total", 2)]


def finish_kernel(seq_size, bits, da_ref, in_ref, in_added, out_ref, out_added, proj_ref, *refs):
    count = len(bits)
    da_out, in_out, out_out, proj_out = refs[:4]
    da_line, in_line, out_line = refs[4:7]
    in_parts, out_parts, proj_parts = (refs[7 + i * count : 7 + (i + 1) * count] for i in range(3))
    own_sem, keep_sem, line_send, line_recv, cube_send, cube_recv, proj_send, proj_recv = refs[7 + 3 * count :]
    z = lax.axis_index("seq")
    f = lax.axis_index("fsdp")
    bit_of = {bit: (f // bit) % 2 for bit in bits}
    mesh_id = pl.DeviceIdType.MESH
    last = seq_size - 1

    def flipped(bit):
        return {"fsdp": f + bit * (1 - 2 * bit_of[bit])}

    barrier = pltpu.get_barrier_semaphore()
    for step in range(1, seq_size):
        pl.semaphore_signal(barrier, inc=1, device_id={"seq": lax.rem(z + step, seq_size)}, device_id_type=mesh_id)
    for bit in bits:
        pl.semaphore_signal(barrier, inc=1, device_id=flipped(bit), device_id_type=mesh_id)
    pl.semaphore_wait(barrier, seq_size - 1 + count)

    lines = ((da_ref, da_line, da_out), (in_parts[-1], in_line, in_out), (out_parts[-1], out_line, out_out))

    def line(index, side, hop, own):
        terms, sums, _ = lines[index]
        if own:
            source = terms.at[seq_size - hop if side == 0 else hop - 1]
        else:
            source = sums.at[side, hop - 2]
        return pltpu.make_async_remote_copy(
            src_ref=source,
            dst_ref=sums.at[side, hop - 1],
            send_sem=line_send.at[index, side, hop - 1],
            recv_sem=line_recv.at[index, side, hop - 1],
            device_id={"seq": z + 1 - 2 * side},
            device_id_type=mesh_id,
        )

    def at_end(side):
        return z == 0 if side == 0 else z == last

    def from_end(side):
        return z if side == 0 else last - z

    def send_own(index):
        for side in (0, 1):

            @pl.when(at_end(side))
            def _(side=side):
                for hop in range(1, seq_size):
                    line(index, side, hop, True).start()

    def arrive(index, hop):
        terms, sums, _ = lines[index]
        for side in (0, 1):

            @pl.when((from_end(side) >= 1) & (from_end(side) <= hop))
            def _(side=side):
                pltpu.make_async_remote_copy(
                    src_ref=sums.at[side, hop - 1],
                    dst_ref=sums.at[side, hop - 1],
                    send_sem=line_send.at[index, side, hop - 1],
                    recv_sem=line_recv.at[index, side, hop - 1],
                    device_id={"seq": z - 1 + 2 * side},
                    device_id_type=mesh_id,
                ).wait_recv()
                if hop < last:
                    target = z - 1 + seq_size - hop if side == 0 else hop - last + z
                    add_into(sums, (side, hop - 1), lambda at: terms[(target, *at)])
                    line(index, side, hop + 1, False).start()

    def total(index):
        terms, sums, result = lines[index]
        add_first(result, lambda at: terms[(z, *at)])
        for side in (0, 1):

            @pl.when(from_end(side) >= 1)
            def _(side=side):
                add_into(result, (), lambda at: sums[(side, last - 1, *at)])

    def add_first(result, term):
        depth = result.shape[0]
        rows = next(n for n in (64, 32, 16, depth) if depth % n == 0)

        def step(i, carry):
            at = (pl.ds(pl.multiple_of(i * rows, rows), rows), slice(None))
            result[at] = term(at).astype(F32)
            return carry

        lax.fori_loop(0, depth // rows, step, 0)

    plain = bits[::-1]
    turned = plain[:1] + plain[:0:-1]
    some = seq_size // 2
    cubes = []
    for row in range(seq_size):
        cubes += [([in_ref, *in_parts], plain, row, 1), ([out_ref, *out_parts], turned, row, 1)]
    cubes += [([proj_ref, *proj_parts], plain, 0, some), ([proj_ref, *proj_parts], turned, some, seq_size - some)]

    def half_of(index, step, kept):
        states, order = cubes[index][:2]
        where = 1 + sorted(order[step:], reverse=True).index(order[step])
        return states[step], where, bit_of[order[step]] if kept else 1 - bit_of[order[step]]

    def rows_of(index):
        return pl.ds(cubes[index][2], cubes[index][3])

    def cube(index, step):
        source, where, bit = half_of(index, step, False)
        states, order = cubes[index][:2]
        return pltpu.make_async_remote_copy(
            src_ref=source.at[(rows_of(index),) + (slice(None),) * (where - 1) + (bit,)],
            dst_ref=states[step + 1].at[rows_of(index)],
            send_sem=cube_send.at[index, step],
            recv_sem=cube_recv.at[index, step],
            device_id=flipped(order[step]),
            device_id_type=mesh_id,
        )

    def cube_add(index, step):
        source, where, bit = half_of(index, step, True)
        states, _, offset, length = cubes[index]
        cube(index, step).wait()
        for row in range(offset, offset + length):
            add_into(states[step + 1], (row,), lambda at, row=row: source[(row, *at[: where - 1], bit, *at[where - 1 :])])
        if step + 1 < count:
            cube(index, step + 1).start()

    def keep(index):
        source, where, bit = half_of(index, 0, True)
        view = source.at[(rows_of(index),) + (slice(None),) * (where - 1) + (bit,)]
        return pltpu.make_async_copy(view, cubes[index][0][1].at[rows_of(index)], keep_sem.at[index])

    def open_cubes():
        for index in range(2 * seq_size):
            keep(index).start()
        for index in (2 * seq_size, 2 * seq_size + 1):
            cube(index, 0).start()
        for index in range(2 * seq_size):
            row, added = index // 2, (in_added, out_added)[index % 2]
            keep(index).wait()
            add_into(cubes[index][0][1], (row,), lambda at, row=row, added=added: added[(row, *at)])
            cube(index, 1).start()

    def proj(step):
        to = lax.rem(z + step, seq_size)
        return pltpu.make_async_remote_copy(
            src_ref=proj_parts[-1].at[to],
            dst_ref=proj_out.at[z],
            send_sem=proj_send.at[step - 1],
            recv_sem=proj_recv.at[step - 1],
            device_id={"seq": to},
            device_id_type=mesh_id,
        )

    def proj_wait(step):
        view = proj_out.at[lax.rem(z + seq_size - step, seq_size)]
        copy = pltpu.make_async_remote_copy(
            src_ref=view,
            dst_ref=view,
            send_sem=proj_send.at[step - 1],
            recv_sem=proj_recv.at[step - 1],
            device_id={"seq": lax.rem(z + step, seq_size)},
            device_id_type=mesh_id,
        )
        copy.wait_recv()

    def proj_start():
        pltpu.make_async_copy(proj_parts[-1].at[z], proj_out.at[z], own_sem).start()
        for step in range(1, seq_size):
            proj(step).start()

    acts = {"send": send_own, "open": open_cubes, "add": cube_add, "arrive": arrive, "proj": proj_start, "total": total}
    for name, *values in finish_plan(seq_size, count):
        acts[name](*values)
    pltpu.make_async_copy(proj_parts[-1].at[z], proj_out.at[z], own_sem).wait()
    for step in range(1, seq_size):
        proj_wait(step)
        proj(step).wait_send()
    for index in range(3):
        for side in (0, 1):
            for hop in range(1, seq_size):

                @pl.when(at_end(side) | ((from_end(side) >= 1) & (from_end(side) <= hop - 1)))
                def _(index=index, side=side, hop=hop):
                    line(index, side, hop, True).wait_send()


def finish_sums(da, ffin, ffout, proj):
    seq_size = lax.axis_size("seq")
    bits = fsdp_bits(False)
    count = len(bits)
    dma = pltpu.SemaphoreType.DMA
    inside, anywhere = pl.BlockSpec(memory_space=pltpu.VMEM), pl.BlockSpec(memory_space=pl.ANY)
    shapes = [v.shape[-2:] for v in (da, ffin[0], ffout[0])]

    def parts_of(shape, first):
        return [pltpu.VMEM((seq_size, *[2] * (count - step), *shape), BF) for step in range(first, count + 1)]

    return pl.pallas_call(
        functools.partial(finish_kernel, seq_size, bits),
        in_specs=[inside, anywhere, inside, anywhere, inside, inside],
        out_specs=[inside] * 4,
        out_shape=[jax.ShapeDtypeStruct(shape, F32) for shape in shapes]
        + [jax.ShapeDtypeStruct((seq_size, *proj.shape[-2:]), BF)],
        scratch_shapes=[
            *[pltpu.VMEM((2, seq_size - 1, *shape), BF) for shape in shapes],
            *parts_of(shapes[1], 1),
            *parts_of(shapes[2], 1),
            *parts_of(proj.shape[-2:], 1),
            dma,
            dma((2 * seq_size,)),
            dma((3, 2, seq_size - 1)),
            dma((3, 2, seq_size - 1)),
            dma((2 * seq_size + 2, count)),
            dma((2 * seq_size + 2, count)),
            dma((seq_size - 1,)),
            dma((seq_size - 1,)),
        ],
        compiler_params=pltpu.CompilerParams(
            collective_id=1, has_side_effects=True, vmem_limit_bytes=56 * 2**20
        ),
        cost_estimate=pl.CostEstimate(flops=0, bytes_accessed=100 * 2**20, transcendentals=0),
    )(da, *ffin, *ffout, proj)


def whole_tiles(shard, rows=16):
    return shard if shard.shape[0] % rows == 0 else shard.reshape(rows, -1)


def on_device(
    inputs,
    qkv_proj,
    out_proj,
    ffn_in,
    ffn_out,
    norm_gains,
    norm_biases,
    centroids,
    expert_in,
    expert_out,
    doc_lengths,
    routes,
    out_grad,
):
    rows, span, width = inputs.shape
    tokens = rows * span
    seq_size, fsdp_size = lax.axis_size("seq"), lax.axis_size("fsdp")
    here = lax.axis_index("seq")
    length = span * seq_size
    cols = width // seq_size
    capacity = max(2, 3 * tokens // (2 * fsdp_size))
    groups = seq_size // 2

    docs = doc_lengths.shape[1]
    key_pos = jnp.arange(length, dtype=jnp.int32)
    doc_ids = jnp.zeros((rows, length), jnp.int32)
    doc_end = jnp.zeros((rows, 1), jnp.int32)
    for j in range(docs - 1):
        doc_end = doc_end + doc_lengths[:, j : j + 1]
        doc_ids = doc_ids + (key_pos[None, :] >= doc_end).astype(jnp.int32)
    id_rows, id_cols = doc_ids[:, None, :], doc_ids[:, :, None]

    depth = out_proj.shape[0]
    wide = 3 * cols + width + LANES
    small = jnp.concatenate(
        [norm_gains.reshape(-1), norm_biases.reshape(-1), centroids[0], routes.reshape(tokens).astype(BF)]
    )
    small = jnp.pad(small, (0, depth * LANES - small.shape[0])).reshape(depth, LANES)
    slices = jnp.stack(
        [
            jnp.concatenate([*[qkv_proj[j, :, i * cols : (i + 1) * cols] for j in range(3)], out_proj, small], axis=1)
            for i in range(seq_size)
        ]
    )
    spare = -depth % 16
    bits = fsdp_bits(False)
    crossed = fsdp_bits(True)
    tokens_in = inputs.reshape(tokens, width)
    proj_all, ffin_all, ffout_all, inputs_all = start_gathers(
        jnp.pad(slices, ((0, 0), (0, spare), (0, 0))), whole_tiles(ffn_in), whole_tiles(ffn_out), tokens_in
    )
    inputs_all = inputs_all.reshape(seq_size * tokens, width)
    ffin_all, ffout_all = ffin_all.reshape(width, -1), ffout_all.reshape(-1, width)
    qkv_mine = proj_all[:, :, :depth, : 3 * cols].reshape(width, 3 * cols)
    out_all = proj_all[:, :, :depth, 3 * cols : 3 * cols + width].reshape(width, width)
    small = proj_all[:, :, :depth, 3 * cols + width :].reshape(seq_size, fsdp_size, -1)
    rows_of = small[:, :, : 6 * depth].astype(F32).reshape(-1, 6, depth).transpose(1, 0, 2).reshape(6, width)
    gain_rows, bias_rows = rows_of[:3], rows_of[3:]
    mine = small[:, :, 6 * depth : 6 * depth + cols]
    centroid = lax.dynamic_index_in_dim(mine, lax.axis_index("fsdp"), 1, keepdims=False).reshape(width)
    inputs_all, win_mine, wout_mine, dr_mine = tie(
        inputs_all, expert_in[0], expert_out[0], out_grad.reshape(tokens, width)
    )
    gains_pad, biases_pad = jnp.pad(gain_rows, ((0, 5), (0, 0))), jnp.pad(bias_rows, ((0, 5), (0, 0)))
    proj_used = proj_all if spare == 0 else proj_all[:, :, :depth, : 3 * cols]
    normed_flat, projected = project(inputs_all, gains_pad, biases_pad, proj_used, 3 * cols, tokens)
    projected = projected.reshape(seq_size, rows, span, 3 * cols)

    attended_mine, lse_rows = attend(projected, id_rows, id_cols)
    fsdp_here = lax.axis_index("fsdp")
    routes_all = small[:, :, 6 * depth + cols : 6 * depth + cols + tokens]
    routes_all = lax.dynamic_index_in_dim(routes_all, fsdp_here, 1, keepdims=False)
    later = (jnp.arange(tokens)[:, None] > jnp.arange(tokens)[None, :]).astype(BF)
    placings = []
    for group in range(groups):
        route = pick(routes_all, (here + seq_size - 2 * group) % seq_size).astype(jnp.int32)
        choose = route[:, None] == jnp.arange(fsdp_size, dtype=jnp.int32)[None, :]
        before = mm(later, choose.astype(BF))
        slot_rank = jnp.sum(jnp.where(choose, before, 0.0), axis=1).astype(jnp.int32)
        target = route * capacity + slot_rank
        slots = jnp.arange(fsdp_size * capacity, dtype=jnp.int32)
        placings.append((target[:, None] == slots[None, :]).astype(BF))
    grad_tokens = out_grad.reshape(tokens, width)

    def slots_of(placing, values):
        return mm_tn(placing, values).astype(BF).reshape(fsdp_size, capacity, width)

    def swap_slots(values):
        return lax.all_to_all(values, "fsdp", split_axis=0, concat_axis=0, tiled=True)

    def tokens_of(placing, values):
        return mm(placing, values.reshape(fsdp_size * capacity, width))

    win_half, wout_half = win_mine.shape[1] // 2, wout_mine.shape[0] // 2
    pair_in_low = seq_pair(win_mine[:, :win_half])
    grad_moved = [seq_shift(dr_mine, 2 * group) for group in range(1, groups)]
    grad_slots = [slots_of(placings[group], ([grad_tokens] + grad_moved)[group]) for group in range(groups)]
    grad_slots = jnp.concatenate(grad_slots, axis=1)
    attended_mine, pair_in_low, grad_slots, win_high = tie(attended_mine, pair_in_low, grad_slots, win_mine[:, win_half:])
    grad_slots = swap_slots(grad_slots)
    attended = seq_exchange(attended_mine)
    attended = attended.transpose(1, 2, 0, 3).reshape(tokens, width)
    pair_in_high = seq_pair(win_high)
    attended, pair_out_low, wout_high = tie(attended, wout_mine[:wout_half], wout_mine[wout_half:])
    pair_out_low = seq_pair(pair_out_low)

    resid_in = tokens_in.astype(F32)
    middle = resid_in + mm(attended, out_all)
    hidden_low, active_low, active_slope, block_out, routed = ffn_forward(
        middle, gains_pad, biases_pad, ffin_all, ffout_all
    )
    routed, wout_high, pair_in_high, pair_out_low, grad_slots = tie(
        routed, wout_high, pair_in_high, pair_out_low, grad_slots
    )
    grad_slots = grad_slots.reshape(fsdp_size, groups, capacity, width)
    grad_slots = [grad_slots[:, group].reshape(-1, width) for group in range(groups)]
    slots_own = slots_of(placings[0], routed)
    pair_out_high = seq_pair(wout_high)

    own_mean, own_scale = norm_parts(resid_in)

    arrived = [swap_slots(slots_own).reshape(-1, width)]
    for group in range(1, groups):
        routed_here = seq_shift(routed, 2 * group)
        routed_here, pair_out_high, qkv_mine, own_mean, own_scale, *grad_slots = tie(
            routed_here, pair_out_high, qkv_mine, own_mean, own_scale, *grad_slots
        )
        slots_here = slots_of(placings[group], routed_here)
        slots_here, pair_out_high, *arrived = tie(slots_here, pair_out_high, *arrived)
        arrived.append(swap_slots(slots_here).reshape(-1, width))
    weights = (win_mine, wout_mine, pair_in_low, pair_in_high, pair_out_low, pair_out_high)
    shared, rows_grads, terms = (), [], []
    for group in range(groups):
        *shared, rows_grad, term = expert_block(
            group, groups, fsdp_size, arrived[group], grad_slots[group], centroid, weights, shared
        )
        rows_grads.append(rows_grad)
        terms.append(term)
    act, du, dz, arrived, gated_all = shared

    half = expert_in.shape[2]
    in_sent = mm_tn(arrived, du[:, half:]).astype(BF)
    back_low = [None] * groups
    for group in reversed(range(groups)):
        rows_grad = rows_grads[group].reshape(fsdp_size, capacity, width)
        if group + 1 < groups:
            rows_grad, back_low[group + 1] = tie(rows_grad, back_low[group + 1])
        back_slots = swap_slots(rows_grad)
        if group + 1 == groups:
            back_slots, in_sent = tie(back_slots, in_sent)
        back_low[group] = tokens_of(placings[group], back_slots)
        if group:
            back_low[group] = back_low[group].astype(BF)
    in_pair = seq_pair(in_sent)
    if groups > 1:
        gated_all, arrived, act, du, back_low[-1] = tie(gated_all, arrived, act, du, back_low[-1])
    back_sum = back_low[0]
    for group in range(1, groups):
        back_sum = back_sum + seq_shift(back_low[group], -2 * group).astype(F32)
    centroid_term = sum(term[0] for term in terms)
    out_sent = mm_tn(act[:, half:], dz).astype(BF)
    in_kept = mm_tn(arrived, du[:, :half])
    out_kept = mm_tn(act[:, :half], dz)

    gated_back = swap_slots(gated_all).reshape(fsdp_size, groups, capacity, width)
    out_terms = [tokens_of(placings[group], gated_back[:, group]) for group in range(groups)]
    out_terms = out_terms[:1] + [v.astype(BF) for v in out_terms[1:]]
    back_sum, out_sent, in_kept, out_kept = tie(back_sum, out_sent, in_kept, out_kept)

    block_low, hidden_grad, middle_grad, branch, dense_rows = ffn_backward(
        back_sum, block_out, grad_tokens, middle, gains_pad, active_slope, ffin_all, ffout_all
    )
    gain_three, bias_three, gain_two, bias_two = (dense_rows[i] for i in range(4))
    attended_grad = mm_nt(branch, out_all).astype(BF)
    attended_grad = attended_grad.reshape(rows, span, seq_size, cols).transpose(2, 0, 1, 3)
    attended_grad, in_pair, active_low, hidden_low, attended = tie(
        attended_grad, in_pair, active_low, hidden_low, attended
    )
    attended_grad = seq_exchange(attended_grad, True)

    def halved(term):
        terms = hyper_split(by_device(term))
        sent = lax.dynamic_index_in_dim(terms, 1 - fsdp_here % 2, terms.ndim - 3, keepdims=False)
        return terms, fsdp_flip(sent, 1)

    ffout_terms = halved(mm_tn(active_low, block_low))
    ffin_terms = mm_tn(hidden_low, hidden_grad).astype(BF)
    proj_terms = mm_tn(attended, branch).astype(BF).reshape(seq_size, fsdp_size, depth, width)
    def split(values):
        size = values.shape[0] // 8
        return values[: 4 * size], values[4 * size : 7 * size], values[7 * size :]

    def send_pieces(pieces):
        return [seq_pair(pieces[0])] + [seq_shift(pieces[group], -2 * group) for group in range(1, groups)]

    out_pieces = [split(values) for values in [out_sent, *out_terms[1:]]]
    sizes = len(out_pieces)
    attended_grad, *out_first = tie(attended_grad, *[pieces[0] for pieces in out_pieces])
    out_first = send_pieces(out_first)

    dq, dk, dv = attend_back(projected, attended_grad, lse_rows, id_rows, id_cols)
    projected_grad = jnp.concatenate([dq, dk, dv], axis=-1).reshape(seq_size * tokens, 3 * cols)
    projected_grad, inputs_all, in_kept, out_kept, proj_terms, ffin_terms, *moved = tie(
        projected_grad,
        inputs_all,
        in_kept,
        out_kept,
        proj_terms,
        ffin_terms,
        *out_first,
        *[pieces[1] for pieces in out_pieces],
    )
    ffin_terms = halved(ffin_terms)
    proj_terms = jnp.pad(proj_terms, ((0, 0), (0, 0), (0, spare), (3 * cols, LANES)))
    out_first, out_second = moved[:sizes], send_pieces(moved[sizes:])
    normed_low_terms = mm_nt(projected_grad, qkv_mine).astype(BF)
    normed_low_terms, *moved = tie(normed_low_terms, *out_second, *[pieces[2] for pieces in out_pieces])
    out_second, out_third = moved[:sizes], send_pieces(moved[sizes:])
    parts_all = norm_parts(inputs_all.astype(F32))
    unit_all = (inputs_all.astype(F32) - parts_all[0]) * parts_all[1]
    terms_wide = normed_low_terms.astype(F32)
    gain_one, bias_one = jnp.sum(terms_wide * unit_all, axis=0), jnp.sum(terms_wide, axis=0)
    small_terms = jnp.stack([gain_one, gain_two, gain_three, bias_one, bias_two, bias_three])

    qkv_term = mm_tn(normed_flat, projected_grad).astype(BF).reshape(seq_size, fsdp_size, depth, 3 * cols)
    small_rows = small_terms.astype(BF).reshape(6, seq_size, fsdp_size, depth).transpose(1, 2, 0, 3)
    centroid_rows = jnp.where(
        (jnp.arange(fsdp_size) == fsdp_here)[None, :, None], centroid_term.reshape(seq_size, 1, cols), 0.0
    )
    small_rows = jnp.concatenate([small_rows.reshape(seq_size, fsdp_size, 6 * depth), centroid_rows.astype(BF)], axis=2)
    small_rows = jnp.pad(small_rows, ((0, 0), (0, 0), (0, depth * LANES - small_rows.shape[2])))
    small_rows = small_rows.reshape(seq_size, fsdp_size, depth, LANES)
    proj_terms = lax.dynamic_update_slice(proj_terms, qkv_term, (0, 0, 0, 0))
    proj_terms = hyper_split(lax.dynamic_update_slice(proj_terms, small_rows, (0, 0, 0, 3 * cols + width)))
    proj_terms, *out_third = tie(proj_terms, *out_third)
    out_pair, *out_moved = [jnp.concatenate(v, axis=0) for v in zip(out_first, out_second, out_third, strict=True)]
    outputs = block_out + out_terms[0] + sum(v.astype(F32) for v in out_moved)
    outputs = outputs.astype(BF).reshape(rows, span, width)
    normed_one_grad, ffn_in_grad, ffn_out_grad, proj_sums = finish_sums(
        normed_low_terms.reshape(seq_size, tokens, width), ffin_terms, ffout_terms, proj_terms
    )
    ffn_in_grad, ffn_out_grad = ffn_in_grad.reshape(ffn_in.shape), ffn_out_grad.reshape(ffn_out.shape)
    proj_sums = proj_sums.astype(F32)
    qkv_grad = jnp.stack(
        [
            jnp.concatenate([proj_sums[i, :depth, j * cols : (j + 1) * cols] for i in range(seq_size)], axis=1)
            for j in range(3)
        ]
    )
    out_proj_grad = jnp.sum(proj_sums[:, :depth, 3 * cols : 3 * cols + width], axis=0)
    small = jnp.sum(proj_sums[:, :depth, 3 * cols + width :], axis=0).reshape(-1)
    small_grad = small[: 6 * depth].reshape(6, depth)
    centroids_grad = small[6 * depth : 6 * depth + cols][None]

    expert_in_grad = (in_kept + in_pair.astype(F32))[None]
    expert_out_grad = (out_kept + out_pair.astype(F32))[None]

    input_norm_grad, _, _ = norm_back(resid_in, (own_mean, own_scale), gain_rows[0], normed_one_grad)
    input_grad = (middle_grad + input_norm_grad).reshape(rows, span, width)
    return (
        outputs,
        input_grad,
        qkv_grad,
        out_proj_grad,
        ffn_in_grad,
        ffn_out_grad,
        small_grad[:3],
        small_grad[3:],
        centroids_grad,
        expert_in_grad,
        expert_out_grad,
    )


def solution(mesh):
    dense = P(("seq", "fsdp"), None)
    placed = (
        P("fsdp", "seq", None),
        P(None, ("seq", "fsdp"), None),
        dense,
        dense,
        dense,
        P(None, ("seq", "fsdp")),
        P(None, ("seq", "fsdp")),
        P("fsdp", "seq"),
        P("fsdp", None, "seq"),
        P("fsdp", "seq", None),
        P("fsdp", None),
        P("seq", "fsdp", None, None),
        P("fsdp", "seq", None),
    )
    returned = (
        P("fsdp", "seq", None),
        P("fsdp", "seq", None),
        P(None, ("seq", "fsdp"), None),
        dense,
        dense,
        dense,
        P(None, ("seq", "fsdp")),
        P(None, ("seq", "fsdp")),
        P("fsdp", "seq"),
        P("fsdp", None, "seq"),
        P("fsdp", "seq", None),
    )
    return jax.shard_map(on_device, mesh=mesh, in_specs=placed, out_specs=returned, check_vma=False)
```
